32 devices in a mesh: gx: 8 (over z, x), gy: 4 (over y, core).
Axes of the slice: x: 2, y: 2, z: 4, core: 2. Of those that a mesh axis runs over, the one named last changes fastest.
Arguments:
- velocity: float32 [3, 2048, 4, 2048], P(None, 'gx', None, 'gy'), may hold values from -6 to 6
- cut_flags: int32 [2048, 4, 2048], P('gx', None, 'gy'), may hold values 0 or 1
- redirect: int32 [2048, 4, 2048], P('gx', None, 'gy'), may hold values from 0 to 3
- share_weight: float32 [2048, 4, 2048], P('gx', None, 'gy'), may hold values from 0.2 to 0.8
- inverse_dx: float32 [2048], replicated, may hold values from 0.5 to 4.8
- inverse_dy: float32 [2048], replicated, may hold values from 0.5 to 4.8
- basis_x: bfloat16 [2048, 2048], replicated, may hold values from -0.125 to 0.125
- basis_y: bfloat16 [2048, 2048], replicated, may hold values from -0.125 to 0.125
- basis_z: float32 [4, 4], replicated, may hold values from -3 to 3
- eigen_x: float32 [2048], replicated, may hold values from 0.05 to 4
- eigen_y: float32 [2048], replicated, may hold values from 0.05 to 4
- eigen_z: float32 [4], replicated, may hold values from 0.05 to 4
Outputs:
- corrected: float32 [3, 2048, 4, 2048], P(None, 'gx', None, 'gy')
- pressure: float32 [2048, 4, 2048], P('gx', None, 'gy')
The draws below stay inside these ranges and needn't reach their ends.
Inputs may be any that keep to these rules, and one draw needn't show every extreme that they name: `redirect`: 0 sends to the next cell along the first dimension, 1 to the previous one, 2 to the next along the second dimension, 3 to the previous one; read only where cut_flags is 1.
All inputs are finite; a program needn't handle non-finite values. No bound on the sum of `cut_flags` on one device may be relied on, other than what follows from the above.
Results may differ from the reference program's by a relative error of at most 0.0003.
Values sent between devices are 32-bit elements; how exact they have to be, the bound alone decides.
No kernel may reach another device: no remote copies, remote signals or barrier semaphores. Data moves between devices by JAX's collectives and lax.ppermute only.
A program may use at most 192 MiB of HBM per device.

```python
import math
import jax
import jax.numpy as jnp
from jax import lax

NX = 2048
NY = 2048
NZ = 4
ITERS = 4


def stretched(key, count):
    rising = 3.0 ** (jnp.arange(count, dtype=jnp.float32) / (count - 1))
    rough = jax.random.uniform(key, (count,), jnp.float32, 0.7, 1.4)
    return rising * rough


def draw_inverse_dx(key, part):
    return stretched(jax.random.fold_in(key, 11), NX)


def draw_inverse_dy(key, part):
    return stretched(jax.random.fold_in(key, 23), NY)


def touch_ends(entries, own_key, least, high):
    spot = [jax.random.randint(jax.random.fold_in(own_key, axis), (), 0, length) for axis, length in enumerate(entries.shape)]
    main_axis = entries.shape.index(max(entries.shape))
    neighbour = spot[:main_axis] + [(spot[main_axis] + 1) % entries.shape[main_axis]] + spot[main_axis + 1:]
    return entries.at[tuple(spot)].set(least).at[tuple(neighbour)].set(high)


def block_levels(key, extent, pieces, smallest, largest):
    loudness = 1.0
    for dim, blocks in pieces:
        draws = jax.random.uniform(jax.random.fold_in(jax.random.fold_in(key, 6), dim), (blocks,), jnp.float32, smallest / len(pieces), largest / len(pieces))
        loudness = loudness * jnp.repeat(jnp.exp(draws), extent[dim] // blocks).reshape((-1,) + (1,) * (len(extent) - 1 - dim))
    return loudness


def normal_values(rng, dims, deviation, most, shards=(), kind=jnp.bfloat16):
    result = jax.random.normal(rng, dims, jnp.float32) * deviation
    if len(shards) > 0:
        result = block_levels(rng, dims, shards, -0.22, 0.18) * result
    return jnp.clip(result, min=-most, max=most).astype(kind)


def setup_inputs(seed: int = 0) -> dict:
    key_list = jax.random.split(jax.random.key(seed), 13)
    velocity = normal_values(key_list[0], (3, NX, NZ, NY), 1.0, 6.0, ((1, 8), (3, 4)), jnp.float32)
    cut_flags = touch_ends((jax.random.randint(key_list[1], (NX, NZ, NY), 0, 4) < 1).astype(jnp.int32), jax.random.fold_in(key_list[1], 1), 0, 1)
    redirect = touch_ends(jax.random.randint(key_list[2], (NX, NZ, NY), 0, 4), jax.random.fold_in(key_list[2], 1), 0, 3).astype(jnp.int32)
    share_weight = jnp.clip(0.2 + 0.6 * jax.random.uniform(key_list[3], (NX, NZ, NY), jnp.float32) ** block_levels(key_list[3], (NX, NZ, NY), ((0, 8), (2, 4)), -0.2, 0.2), 0.2, 0.8)
    inverse_dx = draw_inverse_dx(jax.random.fold_in(key_list[12], 71), 0)
    inverse_dy = draw_inverse_dy(jax.random.fold_in(key_list[12], 71), 0)
    basis_x = normal_values(key_list[6], (NX, NX), NX ** -0.5, 0.125)
    basis_y = normal_values(key_list[7], (NY, NY), NY ** -0.5, 0.125)
    basis_z = normal_values(key_list[8], (NZ, NZ), NZ ** -0.5, 3.0, (), jnp.float32)
    eigen_x = jnp.clip(jnp.exp(jax.random.uniform(key_list[9], (NX,), jnp.float32, math.log(0.05), math.log(4.0))), 0.05, 4.0)
    eigen_y = jnp.clip(jnp.exp(jax.random.uniform(key_list[10], (NY,), jnp.float32, math.log(0.05), math.log(4.0))), 0.05, 4.0)
    eigen_z = jnp.clip(jnp.exp(jax.random.uniform(key_list[11], (NZ,), jnp.float32, math.log(0.05), math.log(4.0))), 0.05, 4.0)
    return dict(velocity=velocity, cut_flags=cut_flags, redirect=redirect, share_weight=share_weight, inverse_dx=inverse_dx, inverse_dy=inverse_dy, basis_x=basis_x, basis_y=basis_y, basis_z=basis_z, eigen_x=eigen_x, eigen_y=eigen_y, eigen_z=eigen_z)


time_step = 0.25
cell_shift = 0.05
cut_shift = 0.45


def x_slope(values, inverse):
    padded = jnp.pad(values, [(0, 0)] * (values.ndim - 3) + [(1, 1), (0, 0), (0, 0)])
    return 0.5 * inverse[:, None, None] * (padded[..., 2:, :, :] - padded[..., :-2, :, :])


def y_slope(values, inverse):
    padded = jnp.pad(values, [(0, 0)] * (values.ndim - 1) + [(1, 1)])
    return 0.5 * inverse * (padded[..., 2:] - padded[..., :-2])


def z_slope(values):
    return 0.5 * (jnp.roll(values, -1, axis=-2) - jnp.roll(values, 1, axis=-2))


def operate(values, diagonal_term, face_x, face_y):
    padded = jnp.pad(values, ((1, 1), (0, 0), (1, 1)))
    flux_x = face_x[:, None, None] * (padded[1:, :, 1:-1] - padded[:-1, :, 1:-1])
    flux_y = face_y * (padded[1:-1, :, 1:] - padded[1:-1, :, :-1])
    plane_term = 2.0 * values - jnp.roll(values, 1, axis=1) - jnp.roll(values, -1, axis=1)
    return diagonal_term * values + (flux_x[:-1] - flux_x[1:]) + (flux_y[..., :-1] - flux_y[..., 1:]) + plane_term


def precondition(residual, basis_x, basis_y, basis_z, eigen_x, eigen_y, eigen_z):
    full_x, planes, full_y = residual.shape
    highest = lax.Precision.HIGHEST
    flat = residual.reshape(full_x, planes * full_y)
    spread = lax.dot_general(basis_x, flat, (((0,), (0,)), ((), ())), precision=highest, preferred_element_type=jnp.float32)
    spread = spread.reshape(full_x * planes, full_y)
    along_y = jnp.dot(spread, basis_y, precision=highest, preferred_element_type=jnp.float32).reshape(full_x, planes, full_y)
    spectral = jnp.einsum("xzy,zw->xwy", along_y, basis_z, precision=highest)
    spectral = spectral / (eigen_x[:, None, None] + eigen_z[None, :, None] + eigen_y[None, None, :])
    back_z = jnp.einsum("xwy,zw->xzy", spectral, basis_z, precision=highest)
    back_z = back_z.reshape(full_x * planes, full_y)
    back_y = lax.dot_general(back_z, basis_y, (((1,), (1,)), ((), ())), precision=highest, preferred_element_type=jnp.float32)
    back_y = back_y.reshape(full_x, planes * full_y)
    return jnp.dot(basis_x, back_y, precision=highest, preferred_element_type=jnp.float32).reshape(full_x, planes, full_y)


def reference(velocity, cut_flags, redirect, share_weight, inverse_dx, inverse_dy, basis_x, basis_y, basis_z, eigen_x, eigen_y, eigen_z):
    wide_x = basis_x.astype(jnp.float32)
    wide_y = basis_y.astype(jnp.float32)
    advect = x_slope(velocity[0][None] * velocity, inverse_dx) + y_slope(velocity[1][None] * velocity, inverse_dy) + z_slope(velocity[2][None] * velocity)
    flags_float = cut_flags.astype(jnp.float32)
    code = (cut_flags * (redirect + 1)).astype(jnp.float32)
    moved_part = share_weight * flags_float * advect
    shares = jnp.pad(moved_part, ((0, 0), (1, 1), (0, 0), (1, 1)))
    code_moved = jnp.pad(code, ((1, 1), (0, 0), (1, 1)))
    received = jnp.where(code_moved[:-2, :, 1:-1] == 1.0, shares[:, :-2, :, 1:-1], 0.0)
    received = received + jnp.where(code_moved[2:, :, 1:-1] == 2.0, shares[:, 2:, :, 1:-1], 0.0)
    received = received + jnp.where(code_moved[1:-1, :, :-2] == 3.0, shares[:, 1:-1, :, :-2], 0.0)
    received = received + jnp.where(code_moved[1:-1, :, 2:] == 4.0, shares[:, 1:-1, :, 2:], 0.0)
    settled = advect - moved_part + received
    predicted = velocity - time_step * settled
    source = -(x_slope(predicted[0], inverse_dx) + y_slope(predicted[1], inverse_dy) + z_slope(predicted[2]))
    diagonal_term = cell_shift + cut_shift * flags_float
    padded_x = jnp.pad(inverse_dx, 1)
    face_x = padded_x[:-1] * padded_x[1:]
    padded_y = jnp.pad(inverse_dy, 1)
    face_y = padded_y[:-1] * padded_y[1:]
    pressure = jnp.zeros_like(source)
    residual = source
    lifted = precondition(residual, wide_x, wide_y, basis_z, eigen_x, eigen_y, eigen_z)
    direction = lifted
    product = jnp.sum(residual * lifted)
    for iteration in range(ITERS):
        mapped = operate(direction, diagonal_term, face_x, face_y)
        step_length = product / jnp.sum(direction * mapped)
        pressure = pressure + step_length * direction
        residual = residual - step_length * mapped
        if iteration + 1 < ITERS:
            lifted = precondition(residual, wide_x, wide_y, basis_z, eigen_x, eigen_y, eigen_z)
            renewed = jnp.sum(residual * lifted)
            direction = lifted + (renewed / product) * direction
            product = renewed
    gradient = jnp.stack([x_slope(pressure, inverse_dx), y_slope(pressure, inverse_dy), z_slope(pressure)])
    return predicted - gradient, pressure
```

```python
import functools

import jax
import jax.numpy as jnp
from jax import lax
from jax.experimental import pallas as pl
from jax.experimental.pallas import tpu as pltpu
from jax.sharding import PartitionSpec as P

ITERS = 4


time_step = 0.25
cell_shift = 0.05
cut_shift = 0.45
both = ("gx", "gy")
spare = 8
vmem_bytes = 56 * 1024 * 1024


def extended_2(value, sides, width, wrap):
    for axis, dim in sides:
        size, length = (lax.axis_size(axis), value.shape[dim])
        up = [(i, (i + 1) % size) for i in range(size if wrap else size - 1)]
        down = [(j, i) for i, j in up]
        last = lax.slice_in_dim(value, length - width, length, axis=dim)
        leading = lax.slice_in_dim(value, 0, width, axis=dim)
        before = lax.ppermute(last, axis, up)
        after = lax.ppermute(leading, axis, down)
        value = jnp.concatenate([before, value, after], axis=dim)
    return value


def x_slope(extended, inverse):
    return 0.5 * inverse[:, None, None] * (extended[..., 2:, :, 1:-1] - extended[..., :-2, :, 1:-1])


def y_slope(extended, inverse):
    return 0.5 * inverse * (extended[..., 1:-1, :, 2:] - extended[..., 1:-1, :, :-2])


def z_slope(values):
    return 0.5 * (jnp.roll(values, -1, axis=-2) - jnp.roll(values, 1, axis=-2))


def halves(value):
    high = value.astype(jnp.bfloat16)
    low = (value - high.astype(jnp.float32)).astype(jnp.bfloat16)
    return high, low


def params(steps=True):
    return pltpu.CompilerParams(
        dimension_semantics=("arbitrary",) if steps else None, vmem_limit_bytes=vmem_bytes
    )


def whole(shape):
    return pl.BlockSpec(shape, lambda n: (0,) * len(shape))


def mix_planes(read, mix_ref, lines, rows):
    planes = mix_ref.shape[0]
    width = lines.shape[1]
    lane = 512 if width % 512 == 0 else width
    half = planes * rows

    def strip(index, carry):
        start = pl.multiple_of(index * 16, 16)
        for left in range(0, width, lane):
            fields = [read(k, pl.ds(start, 16), pl.ds(left, lane)) for k in range(planes)]
            for m in range(planes):
                total = fields[0] * mix_ref[0, m]
                for k in range(1, planes):
                    total = total + fields[k] * mix_ref[k, m]
                high, low = halves(total)
                lines[pl.ds(m * rows + start, 16), pl.ds(left, lane)] = high
                lines[pl.ds(half + m * rows + start, 16), pl.ds(left, lane)] = low
        return carry

    lax.fori_loop(0, rows // 16, strip, 0)


def send_lines(lines, basis_ref, out_ref, rows):
    planes, parts, _, columns = out_ref.shape
    half = planes * rows
    result = jnp.dot(lines[...], basis_ref[...], preferred_element_type=jnp.float32)
    result = result[:half] + result[half:]
    for m in range(planes):
        for part in range(parts):
            out_ref[m, part] = result[m * rows : (m + 1) * rows, part * columns : (part + 1) * columns]


def start_kernel(rows, mix_ref, field_ref, basis_ref, kept_ref, out_ref, lines):
    @pl.when(pl.program_id(0) == 0)
    def _():
        pieces, planes, _, span = field_ref.shape
        for piece in range(pieces):
            kept_ref[:, :, piece * span : (piece + 1) * span] = field_ref[piece]
        mix_planes(lambda k, i, j: kept_ref[k, i, j], mix_ref, lines, rows)

    send_lines(lines, basis_ref, out_ref, rows)


def start_lines(field, basis_z, basis_y, columns):
    pieces, planes, rows, span = field.shape
    full = pieces * span
    width = min(256, full)
    parts = width // columns
    return pl.pallas_call(
        functools.partial(start_kernel, rows),
        grid=(full // width,),
        in_specs=[
            pl.BlockSpec(memory_space=pltpu.SMEM),
            whole(field.shape),
            pl.BlockSpec((full, width), lambda n: (0, n)),
        ],
        out_specs=[
            whole((planes, rows, full)),
            pl.BlockSpec((planes, parts, rows, columns), lambda n: (0, n, 0, 0)),
        ],
        out_shape=[
            jax.ShapeDtypeStruct((planes, rows, full), jnp.float32),
            jax.ShapeDtypeStruct((planes, full // columns, rows, columns), jnp.float32),
        ],
        scratch_shapes=[pltpu.VMEM((2 * planes * rows, full), jnp.bfloat16)],
        compiler_params=params(),
    )(basis_z, field, basis_y)


def column_kernel(rows, blocks, field_ref, aux_ref, ahead_ref, back_ref, along_ref, other_ref, out_ref, lines, spectral):
    step = pl.program_id(0)
    full, columns = field_ref.shape
    block = full // blocks

    @pl.when(step == 0)
    def _():
        def strip(index, carry):
            start = pl.multiple_of(index * 64, 64)
            high, low = halves(field_ref[pl.ds(start, 64), :])
            lines[pl.ds(start, 64), :columns] = high
            lines[pl.ds(start, 64), columns:] = low
            return carry

        lax.fori_loop(0, full // 64, strip, 0)

    @pl.when(step < blocks)
    def _():
        result = jnp.dot(ahead_ref[...], lines[...], preferred_element_type=jnp.float32)
        result = result[:, :columns] + result[:, columns:]
        result = result / (along_ref[...] + other_ref[...])
        high, low = halves(result)
        start = pl.multiple_of(step * block, block)
        spectral[pl.ds(start, block), :columns] = high
        spectral[pl.ds(start, block), columns:] = low

    @pl.when(step >= blocks)
    def _():
        result = jnp.dot(back_ref[...], spectral[...], preferred_element_type=jnp.float32)
        result = result[:, :columns] + result[:, columns:]
        group = block // rows
        first = (step - blocks) * group
        for part in range(group):
            out_ref[first + part, :rows, :] = result[part * rows : (part + 1) * rows]

    @pl.when(step == 2 * blocks - 1)
    def _():
        devices = full // rows
        edge = jnp.zeros((1, columns), jnp.float32)
        rest = aux_ref[2:, :]
        for part in range(devices):
            above = out_ref[part - 1, rows - 1 : rows, :] if part > 0 else edge
            below = out_ref[part + 1, 0:1, :] if part + 1 < devices else edge
            out_ref[part, rows:, :] = jnp.concatenate([above, below, rest], axis=0)


def column_lines(field, aux, basis_xt, basis_x, along, other, rows):
    full, columns = field.shape
    block = min(512, full)
    blocks = full // block
    devices = full // rows
    return pl.pallas_call(
        functools.partial(column_kernel, rows, blocks),
        grid=(2 * blocks,),
        in_specs=[
            whole(field.shape),
            whole(aux.shape),
            pl.BlockSpec((block, full), lambda n: (jnp.minimum(n, blocks - 1), 0)),
            pl.BlockSpec((block, full), lambda n: (jnp.maximum(n - blocks, 0), 0)),
            pl.BlockSpec((block, 1), lambda n: (jnp.minimum(n, blocks - 1), 0)),
            whole(other.shape),
        ],
        out_specs=whole((devices, rows + spare, columns)),
        out_shape=jax.ShapeDtypeStruct((devices, rows + spare, columns), jnp.float32),
        scratch_shapes=[
            pltpu.VMEM((full, 2 * columns), jnp.bfloat16),
            pltpu.VMEM((full, 2 * columns), jnp.bfloat16),
        ],
        compiler_params=params(),
    )(field, aux, basis_xt, basis_x, along, other)


def turn_kernel(stage, last, blocks, rows, *refs):
    refs = list(refs)
    take = lambda: refs.pop(0)
    mix_ref, got_ref, rows_ref = take(), take(), take()
    ahead_ref = None if last else take()
    diagonal_ref, low_x, high_x, low_y, high_y = take(), take(), take(), take(), take()
    if stage >= 1:
        old_z, old_edge_z = take(), take()
    if stage >= 2:
        old_v, old_edge_v, old_scalars = take(), take(), take()
    z_ref, edge_z_ref, y_ref = take(), take(), take()
    if stage >= 1:
        v_ref, edge_v_ref, scalars_ref = take(), take(), take()
    out_ref = None if last else take()
    lines, around = take(), take()
    ahead_lines = None if last else take()
    step = pl.program_id(0)
    planes, _, full = y_ref.shape
    devices, _, columns = got_ref.shape
    parts = devices // planes
    half = planes * (rows + spare)
    main = planes * rows
    width = rows_ref.shape[0]

    @pl.when(step == 0)
    def _():
        edge_rows = lax.broadcasted_iota(jnp.int32, (spare, columns), 0) < 2
        for part in range(parts):
            lanes = slice(part * columns, (part + 1) * columns)
            edges = []
            for m in range(planes):
                high, low = halves(got_ref[m * parts + part, :rows, :])
                lines[m * rows : (m + 1) * rows, lanes] = high
                lines[half + m * rows : half + (m + 1) * rows, lanes] = low
                edges.append(jnp.where(edge_rows, got_ref[m * parts + part, rows:, :], 0.0))
            high, low = halves(jnp.concatenate(edges, axis=0))
            lines[main:half, lanes] = high
            lines[half + main :, lanes] = low
        if stage >= 1:
            product = jnp.sum(jnp.sum(got_ref[:, rows + 2, :], axis=0, keepdims=True), axis=1, keepdims=True)
            image = jnp.sum(jnp.sum(got_ref[:, rows + 3, :], axis=0, keepdims=True), axis=1, keepdims=True)
            if stage >= 2:
                turn = product / old_scalars[0:1, 0:1]
                image = image - turn * turn * old_scalars[1:2, 0:1]
            else:
                turn = jnp.zeros_like(product)
            length = product / image
            kept = [product, image, length, turn]
            kept = [jnp.broadcast_to(value, (1, 128)) for value in kept]
            scalars_ref[...] = jnp.concatenate(kept + [jnp.zeros((4, 128), jnp.float32)], axis=0)

    @pl.when(step < blocks)
    def _():
        result = lax.dot_general(
            lines[...], rows_ref[...], (((1,), (1,)), ((), ())), preferred_element_type=jnp.float32
        )
        result = result[:half] + result[half:]
        lanes = pl.ds(pl.multiple_of(step * width, width), width)
        if stage >= 1:
            length = scalars_ref[2:3, 0:1]
            turn = scalars_ref[3:4, 0:1]
        for k in range(planes):
            value = result[:rows] * mix_ref[k, 0]
            edge = result[main : main + spare] * mix_ref[k, 0]
            for m in range(1, planes):
                value = value + result[m * rows : (m + 1) * rows] * mix_ref[k, m]
                edge = edge + result[main + m * spare : main + (m + 1) * spare] * mix_ref[k, m]
            if stage >= 1:
                if stage >= 2:
                    value = value + turn * old_v[k]
                    edge = edge + turn * old_edge_v[k]
                v_ref[k] = value
                edge_v_ref[k] = edge
                value = old_z[k] - length * value
                edge = old_edge_z[k] - length * edge
            z_ref[k] = value
            edge_z_ref[k] = edge
            around[k, spare : spare + rows, lanes] = value
            around[k, spare - 1 : spare, lanes] = edge[0:1]
            around[k, spare + rows : spare + rows + 1, lanes] = edge[1:2]

    @pl.when(step == blocks - 1 if last else step == blocks)
    def _():
        for k in range(planes):
            for start in range(0, rows, 8):
                value = around[k, spare + start : spare + start + 8, :]
                above = around[k, spare + start - 1 : spare + start + 7, :]
                below = around[k, spare + start + 1 : spare + start + 9, :]
                before = around[(k - 1) % planes, spare + start : spare + start + 8, :]
                after = around[(k + 1) % planes, spare + start : spare + start + 8, :]
                total = diagonal_ref[k, start : start + 8, :] * value
                total = total + (
                    low_x[start : start + 8, :] * (value - above)
                    - high_x[start : start + 8, :] * (below - value)
                )
                left = pltpu.roll(value, 1, 1)
                right = pltpu.roll(value, full - 1, 1)
                total = total + (low_y[...] * (value - left) - high_y[...] * (right - value))
                y_ref[k, start : start + 8, :] = total + (2.0 * value - before - after)
        if not last:
            mix_planes(lambda k, i, j: y_ref[k, i, j], mix_ref, ahead_lines, rows)

    if not last:

        @pl.when(step >= blocks)
        def _():
            send_lines(ahead_lines, ahead_ref, out_ref, rows)


def turn_lines(stage, last, got, operator, basis_z, basis_y, state):
    diagonal, low_x, high_x, low_y, high_y = operator
    planes, rows, full = diagonal.shape
    devices, _, columns = got.shape
    width = min(256, full)
    blocks = full // width
    parts = width // columns
    down = lambda n: jnp.minimum(n, blocks - 1)
    field = pl.BlockSpec((planes, rows, width), lambda n: (0, 0, down(n)))
    edge = pl.BlockSpec((planes, spare, width), lambda n: (0, 0, down(n)))
    scalars = whole((8, 128))
    field_shape = jax.ShapeDtypeStruct((planes, rows, full), jnp.float32)
    edge_shape = jax.ShapeDtypeStruct((planes, spare, full), jnp.float32)
    scalars_shape = jax.ShapeDtypeStruct((8, 128), jnp.float32)
    specs = [
        pl.BlockSpec(memory_space=pltpu.SMEM),
        whole(got.shape),
        pl.BlockSpec((width, full), lambda n: (down(n), 0)),
    ]
    given = [basis_z, got, basis_y]
    if not last:
        specs.append(pl.BlockSpec((full, width), lambda n: (0, jnp.maximum(n - blocks, 0))))
        given.append(basis_y)
    specs += [whole(part.shape) for part in operator]
    given += list(operator)
    if stage >= 1:
        specs += [field, edge]
        given += [state["z"], state["edge_z"]]
    if stage >= 2:
        specs += [field, edge, scalars]
        given += [state["v"], state["edge_v"], state["scalars"]]
    names = ["z", "edge_z", "y"]
    outs = [field, edge, whole((planes, rows, full))]
    shapes = [field_shape, edge_shape, field_shape]
    if stage >= 1:
        names += ["v", "edge_v", "scalars"]
        outs += [field, edge, scalars]
        shapes += [field_shape, edge_shape, scalars_shape]
    half = planes * (rows + spare)
    scratch = [
        pltpu.VMEM((2 * half, full), jnp.bfloat16),
        pltpu.VMEM((planes, rows + 2 * spare, full), jnp.float32),
    ]
    if not last:
        names.append("sent")
        outs.append(
            pl.BlockSpec((planes, parts, rows, columns), lambda n: (0, jnp.maximum(n - blocks, 0), 0, 0))
        )
        shapes.append(jax.ShapeDtypeStruct((planes, full // columns, rows, columns), jnp.float32))
        scratch.append(pltpu.VMEM((2 * planes * rows, full), jnp.bfloat16))
    results = pl.pallas_call(
        functools.partial(turn_kernel, stage, last, blocks, rows),
        grid=(blocks if last else 2 * blocks,),
        in_specs=specs,
        out_specs=outs,
        out_shape=shapes,
        scratch_shapes=scratch,
        compiler_params=params(),
    )(*given)
    return dict(zip(names, results))


def lanes_sum(value, columns):
    return jnp.sum(value.reshape(-1, value.shape[-1] // columns, columns), axis=(0, 1))


def per_device(
    velocity,
    cut_flags,
    redirect,
    share_weight,
    inverse_dx,
    inverse_dy,
    basis_x,
    basis_y,
    basis_z,
    eigen_x,
    eigen_y,
    eigen_z,
):
    x_parts = lax.axis_size("gx")
    y_parts = lax.axis_size("gy")
    devices = x_parts * y_parts
    x_index = lax.axis_index("gx")
    y_index = lax.axis_index("gy")
    own = x_index * y_parts + y_index
    x_count, planes, y_count = velocity.shape[1:]
    full_x = x_count * x_parts
    full_y = y_count * y_parts
    rows = full_x // devices
    columns = planes * full_y // devices
    column_blocks = devices // planes
    inverse_x = lax.dynamic_slice_in_dim(inverse_dx, x_index * x_count, x_count)
    inverse_y = lax.dynamic_slice_in_dim(inverse_dy, y_index * y_count, y_count)
    extended = extended_2(velocity, (("gx", 1), ("gy", 3)), 1, False)
    advect = (
        x_slope(extended[0][None] * extended, inverse_x)
        + y_slope(extended[1][None] * extended, inverse_y)
        + z_slope(velocity[2][None] * velocity)
    )
    flags_float = cut_flags.astype(jnp.float32)
    code = (cut_flags * (redirect + 1)).astype(jnp.float32)
    moved_part = share_weight * flags_float * advect
    stacked = jnp.concatenate([moved_part, code[None]], axis=0)
    beside_all = extended_2(stacked, (("gx", 1), ("gy", 3)), 1, False)
    shares = beside_all[:3]
    code_moved = beside_all[3]
    received = jnp.where(code_moved[:-2, :, 1:-1] == 1.0, shares[:, :-2, :, 1:-1], 0.0)
    received = received + jnp.where(code_moved[2:, :, 1:-1] == 2.0, shares[:, 2:, :, 1:-1], 0.0)
    received = received + jnp.where(code_moved[1:-1, :, :-2] == 3.0, shares[:, 1:-1, :, :-2], 0.0)
    received = received + jnp.where(code_moved[1:-1, :, 2:] == 4.0, shares[:, 1:-1, :, 2:], 0.0)
    settled = advect - moved_part + received
    predicted = velocity - time_step * settled
    predicted_ext = extended_2(predicted, (("gx", 1), ("gy", 3)), 1, False)
    source = -(
        x_slope(predicted_ext[0], inverse_x)
        + y_slope(predicted_ext[1], inverse_y)
        + z_slope(predicted[2])
    )
    diagonal_term = cell_shift + cut_shift * flags_float

    def to_lines(block_form):
        block_form = block_form.reshape(y_parts, rows, planes, y_count)
        block_form = block_form.transpose(0, 2, 1, 3)
        return lax.all_to_all(block_form, "gy", 0, 0, tiled=True)

    diagonal = to_lines(diagonal_term).transpose(1, 2, 0, 3).reshape(planes, rows, full_y)
    source = to_lines(source)
    whole_x = jnp.pad(inverse_dx, 1)
    face_x = lax.dynamic_slice_in_dim(whole_x[:-1] * whole_x[1:], own * rows, rows + 1)
    whole_y = jnp.pad(inverse_dy, 1)
    face_y = whole_y[:-1] * whole_y[1:]
    operator = (diagonal, face_x[:-1, None], face_x[1:, None], face_y[None, :-1], face_y[None, 1:])
    basis_xt = basis_x.T
    along = eigen_x[:, None]
    other = (
        lax.dynamic_slice_in_dim(eigen_y, (own % column_blocks) * columns, columns)
        + lax.dynamic_slice_in_dim(eigen_z, own // column_blocks, 1)
    )[None]

    def through_columns(sent, aux):
        sent = sent.reshape(devices, rows, columns)
        got = lax.all_to_all(sent, both, 0, 0, tiled=True).reshape(full_x, columns)
        got = column_lines(got, aux, basis_xt, basis_x, along, other, rows)
        return lax.all_to_all(got, both, 0, 0, tiled=True)

    residual, sent = start_lines(source, basis_z, basis_y, columns)
    got = through_columns(sent, jnp.zeros((spare, columns), jnp.float32))
    state = turn_lines(0, False, got, operator, basis_z, basis_y, {})
    direction, image, pressure = state["z"], state["y"], None
    for iteration in range(ITERS):
        final = iteration + 1 == ITERS
        if iteration > 0:
            length = state["scalars"][2, 0]
            turn = state["scalars"][3, 0]
            if iteration > 1:
                direction = old_z + turn * direction
                image = old_y + turn * image
            pressure = length * direction + (pressure if iteration > 1 else 0.0)
            residual = residual - length * image
        partial = jnp.stack(
            [lanes_sum(residual * state["z"], columns), lanes_sum(state["z"] * state["y"], columns)]
        )
        if not final:
            aux = jnp.pad(partial, ((2, spare - 4), (0, 0)))
            got = through_columns(state["sent"], aux)
            old_z, old_y = state["z"], state["y"]
            state = {**state, **turn_lines(iteration + 1, iteration + 2 == ITERS, got, operator, basis_z, basis_y, state)}
    sums = jnp.broadcast_to(jnp.pad(partial, ((0, spare - 2), (0, 0)))[None], (devices, spare, columns))
    sums = lax.all_to_all(sums, both, 0, 0, tiled=True)
    product = jnp.sum(sums[:, 0])
    turn = product / state["scalars"][0, 0]
    length = product / (jnp.sum(sums[:, 1]) - turn * turn * state["scalars"][1, 0])
    pressure = pressure + length * (state["z"] + turn * direction)
    pressure = pressure.reshape(planes, rows, y_parts, y_count).transpose(2, 0, 1, 3)
    pressure = lax.all_to_all(pressure, "gy", 0, 0, tiled=True)
    pressure = pressure.transpose(0, 2, 1, 3).reshape(x_count, planes, y_count)
    pressure_ext = extended_2(pressure, (("gx", 0), ("gy", 2)), 1, False)
    gradient = jnp.stack(
        [x_slope(pressure_ext, inverse_x), y_slope(pressure_ext, inverse_y), z_slope(pressure)]
    )
    return (predicted - gradient, pressure)


def solution(mesh):
    in_specs = (
        P(None, "gx", None, "gy"),
        P("gx", None, "gy"),
        P("gx", None, "gy"),
        P("gx", None, "gy"),
        P(),
        P(),
        P(),
        P(),
        P(),
        P(),
        P(),
        P(),
    )
    out_specs = (P(None, "gx", None, "gy"), P("gx", None, "gy"))
    return jax.shard_map(
        per_device, mesh=mesh, in_specs=in_specs, out_specs=out_specs, check_vma=False
    )
```

```python
import functools

import jax
import jax.numpy as jnp
from jax import lax
from jax.experimental import pallas as pl
from jax.experimental.pallas import tpu as pltpu
from jax.sharding import PartitionSpec as P

ITERS = 4


time_step = 0.25
cell_shift = 0.05
cut_shift = 0.45
both = ("gx", "gy")
spare = 8
vmem_bytes = 56 * 1024 * 1024


def halves(value):
    high = value.astype(jnp.bfloat16)
    low = (value - high.astype(jnp.float32)).astype(jnp.bfloat16)
    return high, low


def params(steps=True):
    return pltpu.CompilerParams(
        dimension_semantics=("arbitrary",) if steps else None, vmem_limit_bytes=vmem_bytes
    )


def whole(shape):
    return pl.BlockSpec(shape, lambda n: (0,) * len(shape))


def mix_planes(read, mix_ref, lines, rows):
    planes = mix_ref.shape[0]
    width = lines.shape[1]
    lane = 512 if width % 512 == 0 else width
    half = planes * rows

    def strip(index, carry):
        start = pl.multiple_of(index * 16, 16)
        for left in range(0, width, lane):
            fields = [read(k, pl.ds(start, 16), pl.ds(left, lane)) for k in range(planes)]
            for m in range(planes):
                total = fields[0] * mix_ref[0, m]
                for k in range(1, planes):
                    total = total + fields[k] * mix_ref[k, m]
                high, low = halves(total)
                lines[pl.ds(m * rows + start, 16), pl.ds(left, lane)] = high
                lines[pl.ds(half + m * rows + start, 16), pl.ds(left, lane)] = low
        return carry

    lax.fori_loop(0, rows // 16, strip, 0)


def send_lines(lines, basis_ref, out_ref, rows):
    planes, parts, _, columns = out_ref.shape
    half = planes * rows
    result = jnp.dot(lines[...], basis_ref[...], preferred_element_type=jnp.float32)
    result = result[:half] + result[half:]
    for m in range(planes):
        for part in range(parts):
            out_ref[m, part] = result[m * rows : (m + 1) * rows, part * columns : (part + 1) * columns]


def start_kernel(rows, mix_ref, field_ref, basis_ref, kept_ref, out_ref, lines):
    @pl.when(pl.program_id(0) == 0)
    def _():
        pieces, planes, _, span = field_ref.shape
        for piece in range(pieces):
            kept_ref[:, :, piece * span : (piece + 1) * span] = field_ref[piece]
        mix_planes(lambda k, i, j: kept_ref[k, i, j], mix_ref, lines, rows)

    send_lines(lines, basis_ref, out_ref, rows)


def start_lines(field, basis_z, basis_y, columns):
    pieces, planes, rows, span = field.shape
    full = pieces * span
    width = min(256, full)
    parts = width // columns
    return pl.pallas_call(
        functools.partial(start_kernel, rows),
        grid=(full // width,),
        in_specs=[
            pl.BlockSpec(memory_space=pltpu.SMEM),
            whole(field.shape),
            pl.BlockSpec((full, width), lambda n: (0, n)),
        ],
        out_specs=[
            whole((planes, rows, full)),
            pl.BlockSpec((planes, parts, rows, columns), lambda n: (0, n, 0, 0)),
        ],
        out_shape=[
            jax.ShapeDtypeStruct((planes, rows, full), jnp.float32),
            jax.ShapeDtypeStruct((planes, full // columns, rows, columns), jnp.float32),
        ],
        scratch_shapes=[pltpu.VMEM((2 * planes * rows, full), jnp.bfloat16)],
        compiler_params=params(),
    )(basis_z, field, basis_y)


def column_kernel(rows, blocks, field_ref, aux_ref, ahead_ref, back_ref, along_ref, other_ref, out_ref, lines, spectral):
    step = pl.program_id(0)
    full, columns = field_ref.shape
    block = full // blocks

    @pl.when(step == 0)
    def _():
        def strip(index, carry):
            start = pl.multiple_of(index * 64, 64)
            high, low = halves(field_ref[pl.ds(start, 64), :])
            lines[pl.ds(start, 64), :columns] = high
            lines[pl.ds(start, 64), columns:] = low
            return carry

        lax.fori_loop(0, full // 64, strip, 0)

    @pl.when(step < blocks)
    def _():
        result = jnp.dot(ahead_ref[...], lines[...], preferred_element_type=jnp.float32)
        result = result[:, :columns] + result[:, columns:]
        result = result / (along_ref[...] + other_ref[...])
        high, low = halves(result)
        start = pl.multiple_of(step * block, block)
        spectral[pl.ds(start, block), :columns] = high
        spectral[pl.ds(start, block), columns:] = low

    @pl.when(step >= blocks)
    def _():
        result = jnp.dot(back_ref[...], spectral[...], preferred_element_type=jnp.float32)
        result = result[:, :columns] + result[:, columns:]
        group = block // rows
        first = (step - blocks) * group
        for part in range(group):
            out_ref[first + part, :rows, :] = result[part * rows : (part + 1) * rows]

    @pl.when(step == 2 * blocks - 1)
    def _():
        devices = full // rows
        edge = jnp.zeros((1, columns), jnp.float32)
        rest = aux_ref[2:, :]
        for part in range(devices):
            above = out_ref[part - 1, rows - 1 : rows, :] if part > 0 else edge
            below = out_ref[part + 1, 0:1, :] if part + 1 < devices else edge
            out_ref[part, rows:, :] = jnp.concatenate([above, below, rest], axis=0)


def column_lines(field, aux, basis_xt, basis_x, along, other, rows):
    full, columns = field.shape
    block = min(512, full)
    blocks = full // block
    devices = full // rows
    return pl.pallas_call(
        functools.partial(column_kernel, rows, blocks),
        grid=(2 * blocks,),
        in_specs=[
            whole(field.shape),
            whole(aux.shape),
            pl.BlockSpec((block, full), lambda n: (jnp.minimum(n, blocks - 1), 0)),
            pl.BlockSpec((block, full), lambda n: (jnp.maximum(n - blocks, 0), 0)),
            pl.BlockSpec((block, 1), lambda n: (jnp.minimum(n, blocks - 1), 0)),
            whole(other.shape),
        ],
        out_specs=whole((devices, rows + spare, columns)),
        out_shape=jax.ShapeDtypeStruct((devices, rows + spare, columns), jnp.float32),
        scratch_shapes=[
            pltpu.VMEM((full, 2 * columns), jnp.bfloat16),
            pltpu.VMEM((full, 2 * columns), jnp.bfloat16),
        ],
        compiler_params=params(),
    )(field, aux, basis_xt, basis_x, along, other)


def turn_kernel(stage, last, blocks, rows, *refs):
    refs = list(refs)
    take = lambda: refs.pop(0)
    mix_ref, got_ref, rows_ref = take(), take(), take()
    ahead_ref = None if last else take()
    diagonal_ref, low_x, high_x, low_y, high_y = take(), take(), take(), take(), take()
    if stage >= 1:
        old_z, old_edge_z = take(), take()
    if stage >= 2:
        old_v, old_edge_v, old_scalars = take(), take(), take()
    z_ref, edge_z_ref, y_ref = take(), take(), take()
    if stage >= 1:
        v_ref, edge_v_ref, scalars_ref = take(), take(), take()
    out_ref = None if last else take()
    lines, around = take(), take()
    ahead_lines = None if last else take()
    step = pl.program_id(0)
    planes, _, full = y_ref.shape
    devices, _, columns = got_ref.shape
    parts = devices // planes
    half = planes * (rows + spare)
    main = planes * rows
    width = rows_ref.shape[0]

    @pl.when(step == 0)
    def _():
        edge_rows = lax.broadcasted_iota(jnp.int32, (spare, columns), 0) < 2
        for part in range(parts):
            lanes = slice(part * columns, (part + 1) * columns)
            edges = []
            for m in range(planes):
                high, low = halves(got_ref[m * parts + part, :rows, :])
                lines[m * rows : (m + 1) * rows, lanes] = high
                lines[half + m * rows : half + (m + 1) * rows, lanes] = low
                edges.append(jnp.where(edge_rows, got_ref[m * parts + part, rows:, :], 0.0))
            high, low = halves(jnp.concatenate(edges, axis=0))
            lines[main:half, lanes] = high
            lines[half + main :, lanes] = low
        if stage >= 1:
            product = jnp.sum(jnp.sum(got_ref[:, rows + 2, :], axis=0, keepdims=True), axis=1, keepdims=True)
            image = jnp.sum(jnp.sum(got_ref[:, rows + 3, :], axis=0, keepdims=True), axis=1, keepdims=True)
            if stage >= 2:
                turn = product / old_scalars[0:1, 0:1]
                image = image - turn * turn * old_scalars[1:2, 0:1]
            else:
                turn = jnp.zeros_like(product)
            length = product / image
            kept = [product, image, length, turn]
            kept = [jnp.broadcast_to(value, (1, 128)) for value in kept]
            scalars_ref[...] = jnp.concatenate(kept + [jnp.zeros((4, 128), jnp.float32)], axis=0)

    @pl.when(step < blocks)
    def _():
        result = lax.dot_general(
            lines[...], rows_ref[...], (((1,), (1,)), ((), ())), preferred_element_type=jnp.float32
        )
        result = result[:half] + result[half:]
        lanes = pl.ds(pl.multiple_of(step * width, width), width)
        if stage >= 1:
            length = scalars_ref[2:3, 0:1]
            turn = scalars_ref[3:4, 0:1]
        for k in range(planes):
            value = result[:rows] * mix_ref[k, 0]
            edge = result[main : main + spare] * mix_ref[k, 0]
            for m in range(1, planes):
                value = value + result[m * rows : (m + 1) * rows] * mix_ref[k, m]
                edge = edge + result[main + m * spare : main + (m + 1) * spare] * mix_ref[k, m]
            if stage >= 1:
                if stage >= 2:
                    value = value + turn * old_v[k]
                    edge = edge + turn * old_edge_v[k]
                v_ref[k] = value
                edge_v_ref[k] = edge
                value = old_z[k] - length * value
                edge = old_edge_z[k] - length * edge
            z_ref[k] = value
            edge_z_ref[k] = edge
            around[k, spare : spare + rows, lanes] = value
            around[k, spare - 1 : spare, lanes] = edge[0:1]
            around[k, spare + rows : spare + rows + 1, lanes] = edge[1:2]

    @pl.when(step == blocks - 1 if last else step == blocks)
    def _():
        for k in range(planes):
            for start in range(0, rows, 8):
                value = around[k, spare + start : spare + start + 8, :]
                above = around[k, spare + start - 1 : spare + start + 7, :]
                below = around[k, spare + start + 1 : spare + start + 9, :]
                before = around[(k - 1) % planes, spare + start : spare + start + 8, :]
                after = around[(k + 1) % planes, spare + start : spare + start + 8, :]
                total = diagonal_ref[k, start : start + 8, :] * value
                total = total + (
                    low_x[start : start + 8, :] * (value - above)
                    - high_x[start : start + 8, :] * (below - value)
                )
                left = pltpu.roll(value, 1, 1)
                right = pltpu.roll(value, full - 1, 1)
                total = total + (low_y[...] * (value - left) - high_y[...] * (right - value))
                y_ref[k, start : start + 8, :] = total + (2.0 * value - before - after)
        if not last:
            mix_planes(lambda k, i, j: y_ref[k, i, j], mix_ref, ahead_lines, rows)

    if not last:

        @pl.when(step >= blocks)
        def _():
            send_lines(ahead_lines, ahead_ref, out_ref, rows)


def turn_lines(stage, last, got, operator, basis_z, basis_y, state):
    diagonal, low_x, high_x, low_y, high_y = operator
    planes, rows, full = diagonal.shape
    devices, _, columns = got.shape
    width = min(256, full)
    blocks = full // width
    parts = width // columns
    down = lambda n: jnp.minimum(n, blocks - 1)
    field = pl.BlockSpec((planes, rows, width), lambda n: (0, 0, down(n)))
    edge = pl.BlockSpec((planes, spare, width), lambda n: (0, 0, down(n)))
    scalars = whole((8, 128))
    field_shape = jax.ShapeDtypeStruct((planes, rows, full), jnp.float32)
    edge_shape = jax.ShapeDtypeStruct((planes, spare, full), jnp.float32)
    scalars_shape = jax.ShapeDtypeStruct((8, 128), jnp.float32)
    specs = [
        pl.BlockSpec(memory_space=pltpu.SMEM),
        whole(got.shape),
        pl.BlockSpec((width, full), lambda n: (down(n), 0)),
    ]
    given = [basis_z, got, basis_y]
    if not last:
        specs.append(pl.BlockSpec((full, width), lambda n: (0, jnp.maximum(n - blocks, 0))))
        given.append(basis_y)
    specs += [whole(part.shape) for part in operator]
    given += list(operator)
    if stage >= 1:
        specs += [field, edge]
        given += [state["z"], state["edge_z"]]
    if stage >= 2:
        specs += [field, edge, scalars]
        given += [state["v"], state["edge_v"], state["scalars"]]
    names = ["z", "edge_z", "y"]
    outs = [field, edge, whole((planes, rows, full))]
    shapes = [field_shape, edge_shape, field_shape]
    if stage >= 1:
        names += ["v", "edge_v", "scalars"]
        outs += [field, edge, scalars]
        shapes += [field_shape, edge_shape, scalars_shape]
    half = planes * (rows + spare)
    scratch = [
        pltpu.VMEM((2 * half, full), jnp.bfloat16),
        pltpu.VMEM((planes, rows + 2 * spare, full), jnp.float32),
    ]
    if not last:
        names.append("sent")
        outs.append(
            pl.BlockSpec((planes, parts, rows, columns), lambda n: (0, jnp.maximum(n - blocks, 0), 0, 0))
        )
        shapes.append(jax.ShapeDtypeStruct((planes, full // columns, rows, columns), jnp.float32))
        scratch.append(pltpu.VMEM((2 * planes * rows, full), jnp.bfloat16))
    results = pl.pallas_call(
        functools.partial(turn_kernel, stage, last, blocks, rows),
        grid=(blocks if last else 2 * blocks,),
        in_specs=specs,
        out_specs=outs,
        out_shape=shapes,
        scratch_shapes=scratch,
        compiler_params=params(),
    )(*given)
    return dict(zip(names, results))


def first_kernel(
    rows, velocity_ref, weight_ref, code_ref, above_ref, below_ref, side_ref, half_x_ref, half_y_ref,
    source_ref, predicted_ref, fields, moved, kept, semaphores,
):
    planes, count, span = weight_ref.shape
    wide = half_y_ref.shape[1]
    pad = 16
    copies = []
    for channel in range(5):
        if channel < 3:
            main = velocity_ref.at[channel]
        else:
            main = weight_ref if channel == 3 else code_ref
        target = fields.at[channel]
        copies.append((main, target.at[:, pad : pad + count, :span]))
        copies.append((above_ref.at[channel], target.at[:, pad - 8 : pad, :span]))
        copies.append((below_ref.at[channel], target.at[:, pad + count : pad + count + 8, :span]))
        copies.append((side_ref.at[channel], target.at[:, :, span:]))
    copies = [
        pltpu.make_async_copy(given, target, semaphores.at[index])
        for index, (given, target) in enumerate(copies)
    ]
    for copy in copies:
        copy.start()
    for copy in copies:
        copy.wait()
    tiles = count // 8 + 2
    half_y = half_y_ref[...]

    def lane_slope(value):
        return pltpu.roll(value, wide - 1, 1) - pltpu.roll(value, 1, 1)

    def advance(index, carry):
        k = index // tiles
        start = pl.multiple_of(8 + (index - k * tiles) * 8, 8)
        window = pl.ds(pl.multiple_of(start - 8, 8), 24)
        own = pl.ds(start, 8)
        before = jnp.where(k == 0, planes - 1, k - 1)
        after = jnp.where(k == planes - 1, 0, k + 1)
        half_x = half_x_ref[own, :]
        first = fields[0, k, window, :]
        second = fields[1, k, own, :]
        third_before = fields[2, before, own, :]
        third_after = fields[2, after, own, :]
        weight = fields[3, k, own, :]
        for c in range(3):
            value = first if c == 0 else fields[c, k, window, :]
            along = first * value
            center = value[8:16]
            total = half_x * (pltpu.roll(along, 23, 0)[8:16] - pltpu.roll(along, 1, 0)[8:16])
            total = total + half_y * lane_slope(second * center)
            total = total + 0.5 * (third_after * fields[c, after, own, :] - third_before * fields[c, before, own, :])
            share = weight * total
            moved[c, k, own, :] = share
            kept[c, k, own, :] = total - share
        return carry

    lax.fori_loop(0, planes * tiles, advance, 0, unroll=4)

    def settle(index, carry):
        k = index // tiles
        start = pl.multiple_of(8 + (index - k * tiles) * 8, 8)
        window = pl.ds(pl.multiple_of(start - 8, 8), 24)
        own = pl.ds(start, 8)
        code = fields[4, k, window, :]
        inside_x = half_x_ref[own, :] > 0.0
        inside_y = half_y > 0.0
        for c in range(3):
            share = moved[c, k, window, :]
            received = pltpu.roll(jnp.where(code == 1.0, share, 0.0), 1, 0)[8:16] + pltpu.roll(jnp.where(code == 2.0, share, 0.0), 23, 0)[8:16]
            center = share[8:16]
            middle = code[8:16]
            received = received + pltpu.roll(jnp.where(middle == 3.0, center, 0.0), 1, 1)
            received = received + pltpu.roll(jnp.where(middle == 4.0, center, 0.0), wide - 1, 1)
            result = fields[c, k, own, :] - time_step * (kept[c, k, own, :] + received)
            if c == 0:
                result = jnp.where(inside_x, result, 0.0)
            if c == 1:
                result = jnp.where(inside_y, result, 0.0)
            kept[c, k, own, :] = result
        return carry

    lax.fori_loop(0, planes * tiles, settle, 0, unroll=4)
    inner = count // 8
    group = rows // 8

    def collect(index, carry):
        k = index // inner
        tile = index - k * inner
        start = pl.multiple_of(pad + tile * 8, 8)
        window = pl.ds(pl.multiple_of(start - 8, 8), 24)
        own = pl.ds(start, 8)
        before = jnp.where(k == 0, planes - 1, k - 1)
        after = jnp.where(k == planes - 1, 0, k + 1)
        first = kept[0, k, window, :]
        second = kept[1, k, own, :]
        total = half_x_ref[own, :] * (pltpu.roll(first, 23, 0)[8:16] - pltpu.roll(first, 1, 0)[8:16])
        total = total + half_y * lane_slope(second)
        total = total + 0.5 * (kept[2, after, own, :] - kept[2, before, own, :])
        target = tile // group
        spot = pl.multiple_of((tile - target * group) * 8, 8)
        source_ref[target, k, pl.ds(spot, 8), :] = -total[:, :span]
        out = pl.ds(pl.multiple_of(tile * 8, 8), 8)
        predicted_ref[0, k, out, :] = first[8:16, :span]
        predicted_ref[1, k, out, :] = second[:, :span]
        predicted_ref[2, k, out, :] = kept[2, k, own, :span]
        return carry

    lax.fori_loop(0, planes * inner, collect, 0, unroll=8)


def first_step(velocity, weight, code, above, below, side, half_x, half_y, rows):
    planes, count, span = weight.shape
    tall, wide = half_x.shape[0], half_y.shape[1]
    anywhere = pl.BlockSpec(memory_space=pl.ANY)
    vector = pl.BlockSpec(memory_space=pltpu.VMEM)
    return pl.pallas_call(
        functools.partial(first_kernel, rows),
        in_specs=[anywhere] * 6 + [vector] * 2,
        out_specs=[vector] * 2,
        out_shape=[
            jax.ShapeDtypeStruct((count // rows, planes, rows, span), jnp.float32),
            jax.ShapeDtypeStruct((3, planes, count, span), jnp.float32),
        ],
        scratch_shapes=[
            pltpu.VMEM((5, planes, tall, wide), jnp.float32),
            pltpu.VMEM((3, planes, tall, wide), jnp.float32),
            pltpu.VMEM((3, planes, tall, wide), jnp.float32),
            pltpu.SemaphoreType.DMA((20,)),
        ],
        compiler_params=params(False),
    )(velocity, weight, code, above, below, side, half_x, half_y)


def neighbours(axis, last, leading):
    size = lax.axis_size(axis)
    up = [(i, i + 1) for i in range(size - 1)]
    down = [(i + 1, i) for i in range(size - 1)]
    return lax.ppermute(last, axis, up), lax.ppermute(leading, axis, down)


def extended_1(value, start, count, before, after):
    padded = jnp.pad(value, (before, after))
    return lax.dynamic_slice_in_dim(padded, start, count + before + after)


def lanes_sum(value, columns):
    return jnp.sum(value.reshape(-1, value.shape[-1] // columns, columns), axis=(0, 1))


def per_device(
    velocity,
    cut_flags,
    redirect,
    share_weight,
    inverse_dx,
    inverse_dy,
    basis_x,
    basis_y,
    basis_z,
    eigen_x,
    eigen_y,
    eigen_z,
):
    x_parts = lax.axis_size("gx")
    y_parts = lax.axis_size("gy")
    devices = x_parts * y_parts
    x_index = lax.axis_index("gx")
    y_index = lax.axis_index("gy")
    own = x_index * y_parts + y_index
    x_count, planes, y_count = velocity.shape[1:]
    full_x = x_count * x_parts
    full_y = y_count * y_parts
    rows = full_x // devices
    columns = planes * full_y // devices
    column_blocks = devices // planes
    inverse_x = lax.dynamic_slice_in_dim(inverse_dx, x_index * x_count, x_count)
    inverse_y = lax.dynamic_slice_in_dim(inverse_dy, y_index * y_count, y_count)
    flags = cut_flags.astype(jnp.float32)
    code = (cut_flags * (redirect + 1)).astype(jnp.float32)
    weight = share_weight * flags
    reach = 3

    def edge_rows(part):
        return jnp.concatenate([velocity[:, part], weight[None, part], code[None, part]])

    above, below = neighbours("gx", edge_rows(slice(x_count - reach, None)), edge_rows(slice(0, reach)))
    velocity = velocity.transpose(0, 2, 1, 3)
    weight = weight.transpose(1, 0, 2)
    code = code.transpose(1, 0, 2)
    above = above.transpose(0, 2, 1, 3)
    below = below.transpose(0, 2, 1, 3)

    def edge_columns(part):
        middle = jnp.concatenate([velocity[..., part], weight[None, ..., part], code[None, ..., part]])
        return jnp.concatenate([above[..., part], middle, below[..., part]], axis=2).swapaxes(2, 3)

    left, right = neighbours("gy", edge_columns(slice(y_count - reach, None)), edge_columns(slice(0, reach)))
    side = jnp.concatenate([right, jnp.zeros((5, planes, 128 - 2 * reach, x_count + 2 * reach), jnp.float32), left], axis=2)
    side = jnp.pad(side.swapaxes(2, 3), ((0, 0), (0, 0), (16 - reach, 16 - reach), (0, 0)))
    above = jnp.pad(above, ((0, 0), (0, 0), (8 - reach, 0), (0, 0)))
    below = jnp.pad(below, ((0, 0), (0, 0), (0, 8 - reach), (0, 0)))
    half_x = 0.5 * extended_1(inverse_dx, x_index * x_count, x_count, 16, 16)[:, None]
    half_y = 0.5 * extended_1(inverse_dy, y_index * y_count, y_count, reach, reach)
    half_y = jnp.concatenate([half_y[reach:], jnp.zeros((128 - 2 * reach,), jnp.float32), half_y[:reach]])[None]
    source, predicted = first_step(velocity, weight, code, above, below, side, half_x, half_y, rows)
    diagonal = (cell_shift + cut_shift * flags).reshape(y_parts, rows, planes, y_count).transpose(0, 2, 1, 3)
    diagonal = lax.all_to_all(diagonal, "gy", 0, 0, tiled=True)
    source, diagonal = lax.optimization_barrier((source, diagonal))
    source = lax.all_to_all(source, "gy", 0, 0, tiled=True)
    source, basis_xt = lax.optimization_barrier((source, basis_x.T))
    diagonal = diagonal.transpose(1, 2, 0, 3).reshape(planes, rows, full_y)
    whole_x = jnp.pad(inverse_dx, 1)
    face_x = lax.dynamic_slice_in_dim(whole_x[:-1] * whole_x[1:], own * rows, rows + 1)
    whole_y = jnp.pad(inverse_dy, 1)
    face_y = whole_y[:-1] * whole_y[1:]
    operator = (diagonal, face_x[:-1, None], face_x[1:, None], face_y[None, :-1], face_y[None, 1:])
    along = eigen_x[:, None]
    other = (
        lax.dynamic_slice_in_dim(eigen_y, (own % column_blocks) * columns, columns)
        + lax.dynamic_slice_in_dim(eigen_z, own // column_blocks, 1)
    )[None]

    def through_columns(sent, aux):
        sent = sent.reshape(devices, rows, columns)
        got = lax.all_to_all(sent, both, 0, 0, tiled=True).reshape(full_x, columns)
        got = column_lines(got, aux, basis_xt, basis_x, along, other, rows)
        return lax.all_to_all(got, both, 0, 0, tiled=True)

    residual, sent = start_lines(source, basis_z, basis_y, columns)
    got = through_columns(sent, jnp.zeros((spare, columns), jnp.float32))
    state = turn_lines(0, False, got, operator, basis_z, basis_y, {})
    direction, image, pressure = state["z"], state["y"], None
    for iteration in range(ITERS):
        final = iteration + 1 == ITERS
        if iteration > 0:
            length = state["scalars"][2, 0]
            turn = state["scalars"][3, 0]
            if iteration > 1:
                direction = old_z + turn * direction
                image = old_y + turn * image
            pressure = length * direction + (pressure if iteration > 1 else 0.0)
            residual = residual - length * image
        partial = jnp.stack(
            [lanes_sum(residual * state["z"], columns), lanes_sum(state["z"] * state["y"], columns)]
        )
        if not final:
            aux = jnp.pad(partial, ((2, spare - 4), (0, 0)))
            got = through_columns(state["sent"], aux)
            old_z, old_y = state["z"], state["y"]
            state = {**state, **turn_lines(iteration + 1, iteration + 2 == ITERS, got, operator, basis_z, basis_y, state)}
    sums = jnp.broadcast_to(jnp.pad(partial, ((0, spare - 2), (0, 0)))[None], (devices, spare, columns))
    sums = lax.all_to_all(sums, both, 0, 0, tiled=True)
    product = jnp.sum(sums[:, 0])
    turn = product / state["scalars"][0, 0]
    length = product / (jnp.sum(sums[:, 1]) - turn * turn * state["scalars"][1, 0])
    pressure = pressure + length * (state["z"] + turn * direction)
    pressure = pressure.reshape(planes, rows, y_parts, y_count).transpose(2, 0, 1, 3)
    pressure = lax.all_to_all(pressure, "gy", 0, 0, tiled=True)
    pressure = pressure.transpose(1, 0, 2, 3).reshape(planes, x_count, y_count)
    above, below = neighbours("gx", pressure[:, -1:], pressure[:, :1])
    left, right = neighbours("gy", pressure[:, :, -1], pressure[:, :, 0])
    slope_x = jnp.concatenate([pressure[:, 1:], below], axis=1) - jnp.concatenate([above, pressure[:, :-1]], axis=1)
    slope_y = jnp.concatenate([pressure[:, :, 1:], right[:, :, None]], axis=2) - jnp.concatenate(
        [left[:, :, None], pressure[:, :, :-1]], axis=2
    )
    slope_z = jnp.roll(pressure, -1, axis=0) - jnp.roll(pressure, 1, axis=0)
    corrected = jnp.stack(
        [
            predicted[0] - 0.5 * inverse_x[:, None] * slope_x,
            predicted[1] - 0.5 * inverse_y * slope_y,
            predicted[2] - 0.5 * slope_z,
        ]
    )
    return corrected.transpose(0, 2, 1, 3), pressure.transpose(1, 0, 2)


def solution(mesh):
    in_specs = (
        P(None, "gx", None, "gy"),
        P("gx", None, "gy"),
        P("gx", None, "gy"),
        P("gx", None, "gy"),
        P(),
        P(),
        P(),
        P(),
        P(),
        P(),
        P(),
        P(),
    )
    out_specs = (P(None, "gx", None, "gy"), P("gx", None, "gy"))
    return jax.shard_map(
        per_device, mesh=mesh, in_specs=in_specs, out_specs=out_specs, check_vma=False
    )
```

```python
import functools

import jax
import jax.numpy as jnp
from jax import lax
from jax.experimental import pallas as pl
from jax.experimental.pallas import tpu as pltpu
from jax.sharding import PartitionSpec as P

ITERS = 4


time_step = 0.25
cell_shift = 0.05
cut_shift = 0.45
both = ("gx", "gy")
spare = 8
vmem_bytes = 56 * 1024 * 1024


def halves(value):
    high = value.astype(jnp.bfloat16)
    low = (value - high.astype(jnp.float32)).astype(jnp.bfloat16)
    return high, low


def params():
    return pltpu.CompilerParams(vmem_limit_bytes=vmem_bytes)


def mix_planes(read, mix_ref, lines, rows):
    planes = mix_ref.shape[0]
    width = lines.shape[1]
    lane = 512 if width % 512 == 0 else width
    half = planes * rows

    def strip(index, carry):
        start = pl.multiple_of(index * 16, 16)
        for left in range(0, width, lane):
            fields = [read(k, pl.ds(start, 16), pl.ds(left, lane)) for k in range(planes)]
            for m in range(planes):
                total = fields[0] * mix_ref[0, m]
                for k in range(1, planes):
                    total = total + fields[k] * mix_ref[k, m]
                high, low = halves(total)
                lines[pl.ds(m * rows + start, 16), pl.ds(left, lane)] = high
                lines[pl.ds(half + m * rows + start, 16), pl.ds(left, lane)] = low
        return carry

    lax.fori_loop(0, rows // 16, strip, 0)


anywhere = pl.BlockSpec(memory_space=pl.ANY)
vector = pl.BlockSpec(memory_space=pltpu.VMEM)
scalar = pl.BlockSpec(memory_space=pltpu.SMEM)


class Stream:
    def __init__(self, pairs, count, semaphores):
        self.pairs = pairs
        self.count = count
        self.semaphores = semaphores

    def copies(self, n):
        pairs = self.pairs(n)
        return [
            pltpu.make_async_copy(given, target, self.semaphores.at[n, index])
            for index, (given, target) in enumerate(pairs)
        ]

    def start(self, n):
        for copy in self.copies(n):
            copy.start()

    def begin(self):
        for n in range(min(2, self.count)):
            self.start(n)

    def take(self, n):
        for copy in self.copies(n):
            copy.wait()

        @pl.when(n + 2 < self.count)
        def _():
            self.start(n + 2)

    def end(self):
        def step(n, carry):
            for copy in self.copies(n):
                copy.wait()
            return carry

        lax.fori_loop(0, self.count, step, 0)


def start_all(pairs, semaphores):
    copies = [
        pltpu.make_async_copy(given, target, semaphores.at[index])
        for index, (given, target) in enumerate(pairs)
    ]
    for copy in copies:
        copy.start()
    return copies


def wait_all(copies):
    for copy in copies:
        copy.wait()


def piece(index, size):
    return pl.ds(pl.multiple_of(index * size, size), size)


def send_lines(lines, basis, sent, out_ref, block, chunk, semaphores, stream=None):
    planes, all_parts, rows, columns = sent.shape
    half = planes * rows
    parts = block // columns
    blocks = all_parts // parts
    out = Stream(
        lambda n: [(sent.at[:, pl.ds(n * parts, parts)], out_ref.at[:, pl.ds(n * parts, parts)])],
        blocks,
        semaphores,
    )

    def step(n, carry):
        if stream is not None:
            stream.take(n)
        result = jnp.dot(lines[...], basis[:, piece(chunk * blocks + n, block)], preferred_element_type=jnp.float32)
        result = result[:half] + result[half:]
        for m in range(planes):
            for part in range(parts):
                sent[m, n * parts + part] = result[
                    m * rows : (m + 1) * rows, part * columns : (part + 1) * columns
                ]
        out.start(n)
        return carry

    lax.fori_loop(0, blocks, step, 0)
    out.end()


def column_stream(basis_ref, basis, block, chunk, blocks, semaphores):
    def pairs(n):
        own = piece(chunk * blocks + n, block)
        return [(basis_ref.at[:, own], basis.at[:, own])]

    return Stream(pairs, blocks, semaphores)


def start_kernel(
    block, mix_ref, field_ref, basis_ref, kept_ref, out_ref, lines_ref,
    field, basis, lines, sent, semaphores, basis_semaphores, out_semaphores,
):
    pieces, planes, rows, span = field_ref.shape
    given = [(field_ref.at[n], field.at[:, :, n * span : (n + 1) * span]) for n in range(pieces)]
    given = start_all(given, semaphores)
    stream = column_stream(basis_ref, basis, block, 0, basis_semaphores.shape[0], basis_semaphores)
    stream.begin()
    wait_all(given)
    kept = pltpu.make_async_copy(field, kept_ref, semaphores.at[pieces])
    kept.start()
    mix_planes(lambda k, i, j: field[k, i, j], mix_ref, lines, rows)
    mixed = pltpu.make_async_copy(lines, lines_ref, semaphores.at[pieces + 1])
    mixed.start()
    send_lines(lines, basis, sent, out_ref, block, 0, out_semaphores, stream)
    kept.wait()
    mixed.wait()


def start_lines(field, basis_z, basis_y, columns, chunks):
    pieces, planes, rows, span = field.shape
    full = pieces * span
    block = min(256, full // chunks)
    blocks = full // chunks // block
    sent = (planes, full // chunks // columns, rows, columns)
    return pl.pallas_call(
        functools.partial(start_kernel, block),
        in_specs=[scalar, anywhere, anywhere],
        out_specs=[anywhere] * 3,
        out_shape=[
            jax.ShapeDtypeStruct((planes, rows, full), jnp.float32),
            jax.ShapeDtypeStruct(sent, jnp.float32),
            jax.ShapeDtypeStruct((2 * planes * rows, full), jnp.bfloat16),
        ],
        scratch_shapes=[
            pltpu.VMEM((planes, rows, full), jnp.float32),
            pltpu.VMEM(basis_y.shape, jnp.bfloat16),
            pltpu.VMEM((2 * planes * rows, full), jnp.bfloat16),
            pltpu.VMEM(sent, jnp.float32),
            pltpu.SemaphoreType.DMA((pieces + 2,)),
            pltpu.SemaphoreType.DMA((blocks, 1)),
            pltpu.SemaphoreType.DMA((blocks, 1)),
        ],
        compiler_params=params(),
    )(basis_z, field, basis_y)


def more_kernel(block, chunk, lines_ref, basis_ref, out_ref, basis, lines, sent, semaphore, basis_semaphores, out_semaphores):
    given = pltpu.make_async_copy(lines_ref, lines, semaphore)
    given.start()
    stream = column_stream(basis_ref, basis, block, chunk, basis_semaphores.shape[0], basis_semaphores)
    stream.begin()
    given.wait()
    send_lines(lines, basis, sent, out_ref, block, chunk, out_semaphores, stream)


def more_lines(lines, basis_y, planes, rows, columns, chunks, chunk):
    full = lines.shape[1]
    block = min(256, full // chunks)
    blocks = full // chunks // block
    sent = (planes, full // chunks // columns, rows, columns)
    return pl.pallas_call(
        functools.partial(more_kernel, block, chunk),
        in_specs=[anywhere, anywhere],
        out_specs=anywhere,
        out_shape=jax.ShapeDtypeStruct(sent, jnp.float32),
        scratch_shapes=[
            pltpu.VMEM(basis_y.shape, jnp.bfloat16),
            pltpu.VMEM(lines.shape, jnp.bfloat16),
            pltpu.VMEM(sent, jnp.float32),
            pltpu.SemaphoreType.DMA,
            pltpu.SemaphoreType.DMA((blocks, 1)),
            pltpu.SemaphoreType.DMA((blocks, 1)),
        ],
        compiler_params=params(),
    )(lines, basis_y)


def take_lines(got, lines, planes, rows):
    devices, _, columns = got.shape
    parts = devices // planes
    half = planes * (rows + spare)
    main = planes * rows
    edge_rows = lax.broadcasted_iota(jnp.int32, (spare, columns), 0) < 2
    for part in range(parts):
        lanes = slice(part * columns, (part + 1) * columns)
        edges = []
        for m in range(planes):
            high, low = halves(got[m * parts + part, :rows, :])
            lines[m * rows : (m + 1) * rows, lanes] = high
            lines[half + m * rows : half + (m + 1) * rows, lanes] = low
            edges.append(jnp.where(edge_rows, got[m * parts + part, rows:, :], 0.0))
        high, low = halves(jnp.concatenate(edges, axis=0))
        lines[main:half, lanes] = high
        lines[half + main :, lanes] = low


def part_kernel(planes, rows, block, got_ref, basis_ref, out_ref, got, basis, lines, out, given_semaphores, semaphores, out_semaphores):
    parts = got.shape[0] // planes
    width = lines.shape[1]
    half = planes * (rows + spare)
    blocks = basis.shape[0] // block
    groups = [slice(m * parts, (m + 1) * parts) for m in range(planes)]
    given = start_all([(got_ref.at[group], got.at[group]) for group in groups], given_semaphores)
    stream = Stream(
        lambda n: [(basis_ref.at[piece(n, block), :width], basis.at[piece(n, block)])], blocks, semaphores
    )
    sink = Stream(
        lambda n: [(out.at[:, piece(n, block)], out_ref.at[:, piece(n, block)])], blocks, out_semaphores
    )
    stream.begin()
    wait_all(given)
    take_lines(got, lines, planes, rows)

    def step(n, carry):
        stream.take(n)
        result = lax.dot_general(
            lines[...], basis[piece(n, block), :], (((1,), (1,)), ((), ())), preferred_element_type=jnp.float32
        )
        out[:, piece(n, block)] = result[:half] + result[half:]
        sink.start(n)
        return carry

    lax.fori_loop(0, blocks, step, 0)
    sink.end()


def part_lines(got, basis_y, planes, rows, chunks):
    full = basis_y.shape[0]
    block = min(256, full)
    half = planes * (rows + spare)
    return pl.pallas_call(
        functools.partial(part_kernel, planes, rows, block),
        in_specs=[anywhere, anywhere],
        out_specs=anywhere,
        out_shape=jax.ShapeDtypeStruct((half, full), jnp.float32),
        scratch_shapes=[
            pltpu.VMEM(got.shape, jnp.float32),
            pltpu.VMEM((full, full // chunks), jnp.bfloat16),
            pltpu.VMEM((2 * half, full // chunks), jnp.bfloat16),
            pltpu.VMEM((half, full), jnp.float32),
            pltpu.SemaphoreType.DMA((planes,)),
            pltpu.SemaphoreType.DMA((full // block, 1)),
            pltpu.SemaphoreType.DMA((full // block, 1)),
        ],
        compiler_params=params(),
    )(got, basis_y)


def column_kernel(
    rows, block, field_ref, aux_ref, ahead_ref, back_ref, along_ref, other_ref, out_ref,
    field, ahead, back, lines, spectral, buffer, given_semaphores, semaphores, out_semaphores,
):
    full, columns = field_ref.shape
    blocks = full // block
    group = block // rows
    devices = full // rows
    given = Stream(
        lambda n: [(field_ref.at[piece(n, block)], field.at[piece(n, block)])], blocks, given_semaphores
    )
    aheads = Stream(
        lambda n: [(ahead_ref.at[piece(n, block)], ahead.at[piece(n, block)])], blocks, semaphores.at[0]
    )
    backs = Stream(
        lambda n: [(back_ref.at[piece(n, block)], back.at[piece(n, block)])], blocks, semaphores.at[1]
    )
    out = Stream(
        lambda n: [(buffer.at[pl.ds(n * group, group)], out_ref.at[pl.ds(n * group, group)])],
        blocks,
        out_semaphores,
    )
    for n in range(blocks):
        given.start(n)
    aheads.begin()
    given.end()

    def strip(index, carry):
        own = piece(index, 64)
        high, low = halves(field[own, :])
        lines[own, :columns] = high
        lines[own, columns:] = low
        return carry

    lax.fori_loop(0, full // 64, strip, 0, unroll=4)

    def forth(n, carry):
        aheads.take(n)

        @pl.when(n == blocks - 1)
        def _():
            backs.begin()

        own = piece(n, block)
        result = jnp.dot(ahead[own, :], lines[...], preferred_element_type=jnp.float32)
        result = result[:, :columns] + result[:, columns:]
        high, low = halves(result / (along_ref[own, :] + other_ref[...]))
        spectral[own, :columns] = high
        spectral[own, columns:] = low
        return carry

    lax.fori_loop(0, blocks, forth, 0)

    def reverse(n, carry):
        backs.take(n)
        result = jnp.dot(back[piece(n, block), :], spectral[...], preferred_element_type=jnp.float32)
        result = result[:, :columns] + result[:, columns:]
        for part in range(group):
            buffer[n * group + part, :rows, :] = result[part * rows : (part + 1) * rows]
        return carry

    lax.fori_loop(0, blocks, reverse, 0)
    rest = aux_ref[2:, :]

    def close(n, carry):
        for part in range(group):
            own = n * group + part
            above = buffer[jnp.maximum(own - 1, 0), rows - 1 : rows, :]
            above = jnp.where(own > 0, above, 0.0)
            below = buffer[jnp.minimum(own + 1, devices - 1), 0:1, :]
            below = jnp.where(own + 1 < devices, below, 0.0)
            buffer[own, rows:, :] = jnp.concatenate([above, below, rest], axis=0)
        out.start(n)
        return carry

    lax.fori_loop(0, blocks, close, 0)
    out.end()


def column_lines(field, aux, basis_xt, basis_x, along, other, rows):
    full, columns = field.shape
    block = min(512, full)
    devices = full // rows
    return pl.pallas_call(
        functools.partial(column_kernel, rows, block),
        in_specs=[anywhere, vector, anywhere, anywhere, vector, vector],
        out_specs=anywhere,
        out_shape=jax.ShapeDtypeStruct((devices, rows + spare, columns), jnp.float32),
        scratch_shapes=[
            pltpu.VMEM((full, columns), jnp.float32),
            pltpu.VMEM((full, full), jnp.bfloat16),
            pltpu.VMEM((full, full), jnp.bfloat16),
            pltpu.VMEM((full, 2 * columns), jnp.bfloat16),
            pltpu.VMEM((full, 2 * columns), jnp.bfloat16),
            pltpu.VMEM((devices, rows + spare, columns), jnp.float32),
            pltpu.SemaphoreType.DMA((full // block, 1)),
            pltpu.SemaphoreType.DMA((2, full // block, 1)),
            pltpu.SemaphoreType.DMA((full // block, 1)),
        ],
        compiler_params=params(),
    )(field, aux, basis_xt, basis_x, along, other)


def turn_kernel(stage, last, block, chunks, *refs):
    refs = list(refs)
    take = lambda: refs.pop(0)
    mix_ref, got_ref, basis_ref = take(), take(), take()
    part_ref = take() if chunks > 1 else None
    diagonal_ref, low_x, high_x, low_y, high_y = take(), take(), take(), take(), take()
    if stage >= 1:
        old_z, old_edge_z = take(), take()
    if stage >= 2:
        old_v, old_edge_v, old_scalars = take(), take(), take()
    z_ref, edge_z_ref, y_ref = take(), take(), take()
    if stage >= 1:
        v_ref, edge_v_ref, scalars_ref = take(), take(), take()
    if not last:
        out_ref, lines_ref = take(), take()
    got, basis, diagonal, lines, around, edge_z, image = [take() for _ in range(7)]
    if stage >= 1:
        z, v, edge_v = take(), take(), take()
    if not last:
        ahead_lines, sent = take(), take()
    part = take() if chunks > 1 else None
    given_semaphores, semaphores, late_semaphores = take(), take(), take()
    if not last:
        basis_semaphores, out_semaphores = take(), take()
    planes, rows, full = diagonal.shape
    devices, _, columns = got.shape
    parts = devices // planes
    half = planes * (rows + spare)
    main = planes * rows
    blocks = full // block
    groups = [slice(m * parts, (m + 1) * parts) for m in range(planes)]
    given = start_all([(got_ref.at[group], got.at[group]) for group in groups], given_semaphores)
    width = full // chunks
    turned = slice(full - width, full)
    fields = []
    if stage >= 1:
        fields += [(old_z, z), (old_edge_z, edge_z)]
    if stage >= 2:
        fields += [(old_v, v), (old_edge_v, edge_v)]

    def needed(n):
        own = piece(n, block)
        pairs = [(basis_ref.at[own, turned], basis.at[own, turned])]
        if chunks > 1:
            pairs.append((part_ref.at[:, own], part.at[:, own]))
        return pairs + [(old.at[:, :, own], target.at[:, :, own]) for old, target in fields]

    stream = Stream(needed, blocks, semaphores)
    stream.begin()
    wait_all(given)
    take_lines(got, lines, planes, rows)
    if stage >= 1:
        product = jnp.sum(jnp.sum(got[:, rows + 2, :], axis=0, keepdims=True), axis=1, keepdims=True)
        bend = jnp.sum(jnp.sum(got[:, rows + 3, :], axis=0, keepdims=True), axis=1, keepdims=True)
        if stage >= 2:
            turn = product / old_scalars[0:1, 0:1]
            bend = bend - turn * turn * old_scalars[1:2, 0:1]
        else:
            turn = jnp.zeros_like(product)
        length = product / bend
        numbers = [jnp.broadcast_to(value, (1, 128)) for value in (product, bend, length, turn)]
        scalars_ref[...] = jnp.concatenate(numbers + [jnp.zeros((4, 128), jnp.float32)], axis=0)

    def finish_block(n, carry):
        stream.take(n)
        lanes = piece(n, block)
        result = lax.dot_general(
            lines[...], basis[lanes, turned], (((1,), (1,)), ((), ())), preferred_element_type=jnp.float32
        )
        result = result[:half] + result[half:]
        if chunks > 1:
            result = result + part[:, lanes]
        if stage >= 1:
            length = scalars_ref[2:3, 0:1]
            turn = scalars_ref[3:4, 0:1]
        for k in range(planes):
            value = result[:rows] * mix_ref[k, 0]
            edge = result[main : main + spare] * mix_ref[k, 0]
            for m in range(1, planes):
                value = value + result[m * rows : (m + 1) * rows] * mix_ref[k, m]
                edge = edge + result[main + m * spare : main + (m + 1) * spare] * mix_ref[k, m]
            if stage >= 1:
                if stage >= 2:
                    value = value + turn * v[k, :, lanes]
                    edge = edge + turn * edge_v[k, :, lanes]
                v[k, :, lanes] = value
                edge_v[k, :, lanes] = edge
                value = z[k, :, lanes] - length * value
                edge = edge_z[k, :, lanes] - length * edge
            edge_z[k, :, lanes] = edge
            around[k, spare : spare + rows, lanes] = value
            around[k, spare - 1 : spare, lanes] = edge[0:1]
            around[k, spare + rows : spare + rows + 1, lanes] = edge[1:2]
        return carry

    diagonal_copy = pltpu.make_async_copy(diagonal_ref, diagonal, late_semaphores.at[0])
    diagonal_copy.start()
    lax.fori_loop(0, blocks, finish_block, 0)
    done = [(around.at[:, spare : spare + rows], z_ref), (edge_z, edge_z_ref)]
    if stage >= 1:
        done += [(v, v_ref), (edge_v, edge_v_ref)]
    done = start_all(done, late_semaphores.at[2:6])
    ahead = None
    if not last and chunks > 1:
        ahead = column_stream(basis_ref, basis, block, 0, width // block, basis_semaphores)
        ahead.begin()
    diagonal_copy.wait()

    def operate(index, carry):
        k = index // (rows // 8)
        tile = index - k * (rows // 8)
        own = piece(tile, 8)
        window = around[k, pl.ds(pl.multiple_of(tile * 8, 8), 24), :]
        value = window[8:16]
        above = pltpu.roll(window, 1, 0)[8:16]
        below = pltpu.roll(window, 23, 0)[8:16]
        middle = pl.ds(pl.multiple_of(tile * 8 + spare, 8), 8)
        before = around[jnp.where(k == 0, planes - 1, k - 1), middle, :]
        after = around[jnp.where(k == planes - 1, 0, k + 1), middle, :]
        total = diagonal[k, own, :] * value
        total = total + (low_x[own, :] * (value - above) - high_x[own, :] * (below - value))
        left = pltpu.roll(value, 1, 1)
        right = pltpu.roll(value, full - 1, 1)
        total = total + (low_y[...] * (value - left) - high_y[...] * (right - value))
        image[k, own, :] = total + (2.0 * value - before - after)
        return carry

    lax.fori_loop(0, planes * (rows // 8), operate, 0, unroll=2)
    image_copy = pltpu.make_async_copy(image, y_ref, late_semaphores.at[1])
    image_copy.start()
    if not last:
        mix_planes(lambda k, i, j: image[k, i, j], mix_ref, ahead_lines, rows)
        mixed = pltpu.make_async_copy(ahead_lines, lines_ref, late_semaphores.at[6])
        mixed.start()
        send_lines(ahead_lines, basis, sent, out_ref, block, 0, out_semaphores, ahead)
        mixed.wait()
    image_copy.wait()
    wait_all(done)


def turn_lines(stage, last, got, part, operator, basis_z, basis_y, state, chunks):
    planes, rows, full = operator[0].shape
    _, _, columns = got.shape
    block = min(256, full // chunks)
    blocks = full // block
    field_shape = jax.ShapeDtypeStruct((planes, rows, full), jnp.float32)
    edge_shape = jax.ShapeDtypeStruct((planes, spare, full), jnp.float32)
    specs = [scalar] + [anywhere] * (4 if chunks > 1 else 3) + [vector] * 4
    given = [basis_z, got, basis_y] + ([part] if chunks > 1 else []) + list(operator)
    if stage >= 1:
        specs += [anywhere] * 2
        given += [state["z"], state["edge_z"]]
    if stage >= 2:
        specs += [anywhere] * 2 + [vector]
        given += [state["v"], state["edge_v"], state["scalars"]]
    names = ["z", "edge_z", "y"]
    outs = [anywhere] * 3
    shapes = [field_shape, edge_shape, field_shape]
    if stage >= 1:
        names += ["v", "edge_v", "scalars"]
        outs += [anywhere, anywhere, vector]
        shapes += [field_shape, edge_shape, jax.ShapeDtypeStruct((8, 128), jnp.float32)]
    field = pltpu.VMEM((planes, rows, full), jnp.float32)
    edge = pltpu.VMEM((planes, spare, full), jnp.float32)
    scratch = [
        pltpu.VMEM(got.shape, jnp.float32),
        pltpu.VMEM(basis_y.shape, jnp.bfloat16),
        field,
        pltpu.VMEM((2 * planes * (rows + spare), full // chunks), jnp.bfloat16),
        pltpu.VMEM((planes, rows + 2 * spare, full), jnp.float32),
        edge,
        field,
    ]
    if stage >= 1:
        scratch += [field, field, edge]
    if not last:
        sent = (planes, full // chunks // columns, rows, columns)
        mixed = (2 * planes * rows, full)
        names += ["sent", "lines"]
        outs += [anywhere] * 2
        shapes += [jax.ShapeDtypeStruct(sent, jnp.float32), jax.ShapeDtypeStruct(mixed, jnp.bfloat16)]
        scratch += [pltpu.VMEM(mixed, jnp.bfloat16), pltpu.VMEM(sent, jnp.float32)]
    if chunks > 1:
        scratch.append(pltpu.VMEM(part.shape, jnp.float32))
    scratch += [
        pltpu.SemaphoreType.DMA((planes,)),
        pltpu.SemaphoreType.DMA((blocks, 6)),
        pltpu.SemaphoreType.DMA((7,)),
    ]
    if not last:
        scratch += [pltpu.SemaphoreType.DMA((blocks // chunks, 1))] * 2
    results = pl.pallas_call(
        functools.partial(turn_kernel, stage, last, block, chunks),
        in_specs=specs,
        out_specs=outs,
        out_shape=shapes,
        scratch_shapes=scratch,
        compiler_params=params(),
    )(*given)
    return dict(zip(names, results))


def first_kernel(
    rows, velocity_ref, weight_ref, code_ref, above_ref, below_ref, side_ref, half_x_ref, half_y_ref,
    source_ref, predicted_ref, fields, moved, kept, semaphores,
):
    planes, count, span = weight_ref.shape
    wide = half_y_ref.shape[1]
    pad = 16
    copies = []
    for channel in range(5):
        if channel < 3:
            main = velocity_ref.at[channel]
        else:
            main = weight_ref if channel == 3 else code_ref
        target = fields.at[channel]
        copies.append((main, target.at[:, pad : pad + count, :span]))
        copies.append((above_ref.at[channel], target.at[:, pad - 8 : pad, :span]))
        copies.append((below_ref.at[channel], target.at[:, pad + count : pad + count + 8, :span]))
        copies.append((side_ref.at[channel], target.at[:, :, span:]))
    copies = [
        pltpu.make_async_copy(given, target, semaphores.at[index])
        for index, (given, target) in enumerate(copies)
    ]
    for copy in copies:
        copy.start()
    for copy in copies:
        copy.wait()
    tiles = count // 8 + 2
    half_y = half_y_ref[...]

    def lane_slope(value):
        return pltpu.roll(value, wide - 1, 1) - pltpu.roll(value, 1, 1)

    def advance(index, carry):
        k = index // tiles
        start = pl.multiple_of(8 + (index - k * tiles) * 8, 8)
        window = pl.ds(pl.multiple_of(start - 8, 8), 24)
        own = pl.ds(start, 8)
        before = jnp.where(k == 0, planes - 1, k - 1)
        after = jnp.where(k == planes - 1, 0, k + 1)
        half_x = half_x_ref[own, :]
        first = fields[0, k, window, :]
        second = fields[1, k, own, :]
        third_before = fields[2, before, own, :]
        third_after = fields[2, after, own, :]
        weight = fields[3, k, own, :]
        for c in range(3):
            value = first if c == 0 else fields[c, k, window, :]
            along = first * value
            center = value[8:16]
            total = half_x * (pltpu.roll(along, 23, 0)[8:16] - pltpu.roll(along, 1, 0)[8:16])
            total = total + half_y * lane_slope(second * center)
            total = total + 0.5 * (third_after * fields[c, after, own, :] - third_before * fields[c, before, own, :])
            share = weight * total
            moved[c, k, own, :] = share
            kept[c, k, own, :] = total - share
        return carry

    lax.fori_loop(0, planes * tiles, advance, 0, unroll=4)

    def settle(index, carry):
        k = index // tiles
        start = pl.multiple_of(8 + (index - k * tiles) * 8, 8)
        window = pl.ds(pl.multiple_of(start - 8, 8), 24)
        own = pl.ds(start, 8)
        code = fields[4, k, window, :]
        inside_x = half_x_ref[own, :] > 0.0
        inside_y = half_y > 0.0
        for c in range(3):
            share = moved[c, k, window, :]
            received = pltpu.roll(jnp.where(code == 1.0, share, 0.0), 1, 0)[8:16] + pltpu.roll(jnp.where(code == 2.0, share, 0.0), 23, 0)[8:16]
            center = share[8:16]
            middle = code[8:16]
            received = received + pltpu.roll(jnp.where(middle == 3.0, center, 0.0), 1, 1)
            received = received + pltpu.roll(jnp.where(middle == 4.0, center, 0.0), wide - 1, 1)
            result = fields[c, k, own, :] - time_step * (kept[c, k, own, :] + received)
            if c == 0:
                result = jnp.where(inside_x, result, 0.0)
            if c == 1:
                result = jnp.where(inside_y, result, 0.0)
            kept[c, k, own, :] = result
        return carry

    lax.fori_loop(0, planes * tiles, settle, 0, unroll=4)
    inner = count // 8
    group = rows // 8

    def collect(index, carry):
        k = index // inner
        tile = index - k * inner
        start = pl.multiple_of(pad + tile * 8, 8)
        window = pl.ds(pl.multiple_of(start - 8, 8), 24)
        own = pl.ds(start, 8)
        before = jnp.where(k == 0, planes - 1, k - 1)
        after = jnp.where(k == planes - 1, 0, k + 1)
        first = kept[0, k, window, :]
        second = kept[1, k, own, :]
        total = half_x_ref[own, :] * (pltpu.roll(first, 23, 0)[8:16] - pltpu.roll(first, 1, 0)[8:16])
        total = total + half_y * lane_slope(second)
        total = total + 0.5 * (kept[2, after, own, :] - kept[2, before, own, :])
        target = tile // group
        spot = pl.multiple_of((tile - target * group) * 8, 8)
        source_ref[target, k, pl.ds(spot, 8), :] = -total[:, :span]
        out = pl.ds(pl.multiple_of(tile * 8, 8), 8)
        predicted_ref[0, k, out, :] = first[8:16, :span]
        predicted_ref[1, k, out, :] = second[:, :span]
        predicted_ref[2, k, out, :] = kept[2, k, own, :span]
        return carry

    lax.fori_loop(0, planes * inner, collect, 0, unroll=8)


def first_step(velocity, weight, code, above, below, side, half_x, half_y, rows):
    planes, count, span = weight.shape
    tall, wide = half_x.shape[0], half_y.shape[1]
    return pl.pallas_call(
        functools.partial(first_kernel, rows),
        in_specs=[anywhere] * 6 + [vector] * 2,
        out_specs=[vector] * 2,
        out_shape=[
            jax.ShapeDtypeStruct((count // rows, planes, rows, span), jnp.float32),
            jax.ShapeDtypeStruct((3, planes, count, span), jnp.float32),
        ],
        scratch_shapes=[
            pltpu.VMEM((5, planes, tall, wide), jnp.float32),
            pltpu.VMEM((3, planes, tall, wide), jnp.float32),
            pltpu.VMEM((3, planes, tall, wide), jnp.float32),
            pltpu.SemaphoreType.DMA((20,)),
        ],
        compiler_params=params(),
    )(velocity, weight, code, above, below, side, half_x, half_y)


def neighbours(axis, last, leading):
    size = lax.axis_size(axis)
    up = [(i, i + 1) for i in range(size - 1)]
    down = [(i + 1, i) for i in range(size - 1)]
    return lax.ppermute(last, axis, up), lax.ppermute(leading, axis, down)


def extended_1(value, start, count, before, after):
    padded = jnp.pad(value, (before, after))
    return lax.dynamic_slice_in_dim(padded, start, count + before + after)


def lanes_sum(value, columns):
    return jnp.sum(value.reshape(-1, value.shape[-1] // columns, columns), axis=(0, 1))


def per_device(
    velocity,
    cut_flags,
    redirect,
    share_weight,
    inverse_dx,
    inverse_dy,
    basis_x,
    basis_y,
    basis_z,
    eigen_x,
    eigen_y,
    eigen_z,
):
    x_parts = lax.axis_size("gx")
    y_parts = lax.axis_size("gy")
    devices = x_parts * y_parts
    x_index = lax.axis_index("gx")
    y_index = lax.axis_index("gy")
    own = x_index * y_parts + y_index
    x_count, planes, y_count = velocity.shape[1:]
    full_x = x_count * x_parts
    full_y = y_count * y_parts
    rows = full_x // devices
    columns = planes * full_y // devices
    chunks = 2 if columns % 256 == 0 else 1
    columns = columns // chunks
    column_blocks = devices // planes
    inverse_x = lax.dynamic_slice_in_dim(inverse_dx, x_index * x_count, x_count)
    inverse_y = lax.dynamic_slice_in_dim(inverse_dy, y_index * y_count, y_count)
    flags = cut_flags.astype(jnp.float32)
    code = (cut_flags * (redirect + 1)).astype(jnp.float32)
    weight = share_weight * flags
    reach = 3

    def edge_rows(part):
        return jnp.concatenate([velocity[:, part], weight[None, part], code[None, part]])

    above, below = neighbours("gx", edge_rows(slice(x_count - reach, None)), edge_rows(slice(0, reach)))
    velocity = velocity.transpose(0, 2, 1, 3)
    weight = weight.transpose(1, 0, 2)
    code = code.transpose(1, 0, 2)
    above = above.transpose(0, 2, 1, 3)
    below = below.transpose(0, 2, 1, 3)

    def edge_columns(part):
        middle = jnp.concatenate([velocity[..., part], weight[None, ..., part], code[None, ..., part]])
        return jnp.concatenate([above[..., part], middle, below[..., part]], axis=2).swapaxes(2, 3)

    left, right = neighbours("gy", edge_columns(slice(y_count - reach, None)), edge_columns(slice(0, reach)))
    side = jnp.concatenate([right, jnp.zeros((5, planes, 128 - 2 * reach, x_count + 2 * reach), jnp.float32), left], axis=2)
    side = jnp.pad(side.swapaxes(2, 3), ((0, 0), (0, 0), (16 - reach, 16 - reach), (0, 0)))
    above = jnp.pad(above, ((0, 0), (0, 0), (8 - reach, 0), (0, 0)))
    below = jnp.pad(below, ((0, 0), (0, 0), (0, 8 - reach), (0, 0)))
    half_x = 0.5 * extended_1(inverse_dx, x_index * x_count, x_count, 16, 16)[:, None]
    half_y = 0.5 * extended_1(inverse_dy, y_index * y_count, y_count, reach, reach)
    half_y = jnp.concatenate([half_y[reach:], jnp.zeros((128 - 2 * reach,), jnp.float32), half_y[:reach]])[None]
    source, predicted = first_step(velocity, weight, code, above, below, side, half_x, half_y, rows)
    diagonal = (cell_shift + cut_shift * flags).reshape(y_parts, rows, planes, y_count).transpose(0, 2, 1, 3)
    diagonal = lax.all_to_all(diagonal, "gy", 0, 0, tiled=True)
    source, diagonal = lax.optimization_barrier((source, diagonal))
    source = lax.all_to_all(source, "gy", 0, 0, tiled=True)
    source, basis_xt = lax.optimization_barrier((source, basis_x.T))
    diagonal = diagonal.transpose(1, 2, 0, 3).reshape(planes, rows, full_y)
    whole_x = jnp.pad(inverse_dx, 1)
    face_x = lax.dynamic_slice_in_dim(whole_x[:-1] * whole_x[1:], own * rows, rows + 1)
    whole_y = jnp.pad(inverse_dy, 1)
    face_y = whole_y[:-1] * whole_y[1:]
    operator = (diagonal, face_x[:-1, None], face_x[1:, None], face_y[None, :-1], face_y[None, 1:])
    along = eigen_x[:, None]
    other = [
        (
            lax.dynamic_slice_in_dim(
                eigen_y, full_y // chunks * chunk + (own % column_blocks) * columns, columns
            )
            + lax.dynamic_slice_in_dim(eigen_z, own // column_blocks, 1)
        )[None]
        for chunk in range(chunks)
    ]

    def apply(sent, lines, aux):
        part = None
        sents = [sent] + [
            more_lines(lines, basis_y, planes, rows, columns, chunks, chunk) for chunk in range(1, chunks)
        ]
        for chunk, sent in enumerate(sents):
            final = chunk + 1 == chunks
            sent = sent.reshape(devices, rows, columns)
            got = lax.all_to_all(sent, both, 0, 0, tiled=True).reshape(full_x, columns)
            given = aux if final else jnp.zeros((spare, columns), jnp.float32)
            got = column_lines(got, given, basis_xt, basis_x, along, other[chunk], rows)
            got = lax.all_to_all(got, both, 0, 0, tiled=True)
            if not final:
                part = part_lines(got, basis_y, planes, rows, chunks)
        return got, part

    residual, sent, lines = start_lines(source, basis_z, basis_y, columns, chunks)
    got, part = apply(sent, lines, jnp.zeros((spare, columns), jnp.float32))
    state = turn_lines(0, False, got, part, operator, basis_z, basis_y, {}, chunks)
    direction, image, pressure = state["z"], state["y"], None
    for iteration in range(ITERS):
        final = iteration + 1 == ITERS
        if iteration > 0:
            length = state["scalars"][2, 0]
            turn = state["scalars"][3, 0]
            if iteration > 1:
                direction = old_z + turn * direction
                image = old_y + turn * image
            pressure = length * direction + (pressure if iteration > 1 else 0.0)
            residual = residual - length * image
        partial = jnp.stack(
            [lanes_sum(residual * state["z"], columns), lanes_sum(state["z"] * state["y"], columns)]
        )
        if not final:
            aux = jnp.pad(partial, ((2, spare - 4), (0, 0)))
            got, part = apply(state["sent"], state["lines"], aux)
            old_z, old_y = state["z"], state["y"]
            last = iteration + 2 == ITERS
            state |= turn_lines(iteration + 1, last, got, part, operator, basis_z, basis_y, state, chunks)
    sums = jnp.broadcast_to(jnp.pad(partial, ((0, spare - 2), (0, 0)))[None], (devices, spare, columns))
    sums = lax.all_to_all(sums, both, 0, 0, tiled=True)
    product = jnp.sum(sums[:, 0])
    turn = product / state["scalars"][0, 0]
    length = product / (jnp.sum(sums[:, 1]) - turn * turn * state["scalars"][1, 0])
    pressure = pressure + length * (state["z"] + turn * direction)
    pressure = pressure.reshape(planes, rows, y_parts, y_count).transpose(2, 0, 1, 3)
    pressure = lax.all_to_all(pressure, "gy", 0, 0, tiled=True)
    pressure = pressure.transpose(1, 0, 2, 3).reshape(planes, x_count, y_count)
    above, below = neighbours("gx", pressure[:, -1:], pressure[:, :1])
    left, right = neighbours("gy", pressure[:, :, -1], pressure[:, :, 0])
    slope_x = jnp.concatenate([pressure[:, 1:], below], axis=1) - jnp.concatenate([above, pressure[:, :-1]], axis=1)
    slope_y = jnp.concatenate([pressure[:, :, 1:], right[:, :, None]], axis=2) - jnp.concatenate(
        [left[:, :, None], pressure[:, :, :-1]], axis=2
    )
    slope_z = jnp.roll(pressure, -1, axis=0) - jnp.roll(pressure, 1, axis=0)
    corrected = jnp.stack(
        [
            predicted[0] - 0.5 * inverse_x[:, None] * slope_x,
            predicted[1] - 0.5 * inverse_y * slope_y,
            predicted[2] - 0.5 * slope_z,
        ]
    )
    return corrected.transpose(0, 2, 1, 3), pressure.transpose(1, 0, 2)


def solution(mesh):
    in_specs = (
        P(None, "gx", None, "gy"),
        P("gx", None, "gy"),
        P("gx", None, "gy"),
        P("gx", None, "gy"),
        P(),
        P(),
        P(),
        P(),
        P(),
        P(),
        P(),
        P(),
    )
    out_specs = (P(None, "gx", None, "gy"), P("gx", None, "gy"))
    return jax.shard_map(
        per_device, mesh=mesh, in_specs=in_specs, out_specs=out_specs, check_vma=False
    )
```

```python
import functools

import jax
import jax.numpy as jnp
from jax import lax
from jax.experimental import pallas as pl
from jax.experimental.pallas import tpu as pltpu
from jax.sharding import PartitionSpec as P

ITERS = 4


time_step = 0.25
cell_shift = 0.05
cut_shift = 0.45
both = ("gx", "gy")
spare = 8
vmem_bytes = 56 * 1024 * 1024


def halves(value):
    high = value.astype(jnp.bfloat16)
    low = (value - high.astype(jnp.float32)).astype(jnp.bfloat16)
    return high, low


def params():
    return pltpu.CompilerParams(vmem_limit_bytes=vmem_bytes)


def mix_planes(read, mix_ref, lines, rows):
    planes = mix_ref.shape[0]
    width = lines.shape[1]
    lane = 512 if width % 512 == 0 else width
    half = planes * rows

    def strip(index, carry):
        start = pl.multiple_of(index * 16, 16)
        for left in range(0, width, lane):
            fields = [read(k, pl.ds(start, 16), pl.ds(left, lane)) for k in range(planes)]
            for m in range(planes):
                total = fields[0] * mix_ref[0, m]
                for k in range(1, planes):
                    total = total + fields[k] * mix_ref[k, m]
                high, low = halves(total)
                lines[pl.ds(m * rows + start, 16), pl.ds(left, lane)] = high
                lines[pl.ds(half + m * rows + start, 16), pl.ds(left, lane)] = low
        return carry

    lax.fori_loop(0, rows // 16, strip, 0)


anywhere = pl.BlockSpec(memory_space=pl.ANY)
vector = pl.BlockSpec(memory_space=pltpu.VMEM)
scalar = pl.BlockSpec(memory_space=pltpu.SMEM)


class Stream:
    def __init__(self, pairs, count, semaphores):
        self.pairs = pairs
        self.count = count
        self.semaphores = semaphores

    def copies(self, n):
        pairs = self.pairs(n)
        return [
            pltpu.make_async_copy(given, target, self.semaphores.at[n, index])
            for index, (given, target) in enumerate(pairs)
        ]

    def start(self, n):
        for copy in self.copies(n):
            copy.start()

    def begin(self):
        for n in range(min(2, self.count)):
            self.start(n)

    def take(self, n):
        for copy in self.copies(n):
            copy.wait()

        @pl.when(n + 2 < self.count)
        def _():
            self.start(n + 2)

    def end(self):
        def step(n, carry):
            for copy in self.copies(n):
                copy.wait()
            return carry

        lax.fori_loop(0, self.count, step, 0)


def start_all(pairs, semaphores):
    copies = [
        pltpu.make_async_copy(given, target, semaphores.at[index])
        for index, (given, target) in enumerate(pairs)
    ]
    for copy in copies:
        copy.start()
    return copies


def wait_all(copies):
    for copy in copies:
        copy.wait()


def piece(index, size):
    return pl.ds(pl.multiple_of(index * size, size), size)


def send_lines(lines, basis, sent, out_ref, block, chunk, semaphores, stream=None):
    planes, all_parts, rows, columns = sent.shape
    half = planes * rows
    parts = block // columns
    blocks = all_parts // parts
    out = Stream(
        lambda n: [(sent.at[:, pl.ds(n * parts, parts)], out_ref.at[:, pl.ds(n * parts, parts)])],
        blocks,
        semaphores,
    )

    def step(n, carry):
        if stream is not None:
            stream.take(n)
        result = jnp.dot(lines[...], basis[:, piece(chunk * blocks + n, block)], preferred_element_type=jnp.float32)
        result = result[:half] + result[half:]
        for m in range(planes):
            for part in range(parts):
                sent[m, n * parts + part] = result[
                    m * rows : (m + 1) * rows, part * columns : (part + 1) * columns
                ]
        out.start(n)
        return carry

    lax.fori_loop(0, blocks, step, 0)
    out.end()


def column_stream(basis_ref, basis, block, chunk, blocks, semaphores):
    def pairs(n):
        own = piece(chunk * blocks + n, block)
        return [(basis_ref.at[:, own], basis.at[:, own])]

    return Stream(pairs, blocks, semaphores)


def start_kernel(
    block, mix_ref, field_ref, basis_ref, kept_ref, out_ref, lines_ref,
    field, basis, lines, sent, semaphores, basis_semaphores, out_semaphores,
):
    pieces, planes, rows, span = field_ref.shape
    given = [(field_ref.at[n], field.at[:, :, n * span : (n + 1) * span]) for n in range(pieces)]
    given = start_all(given, semaphores)
    stream = column_stream(basis_ref, basis, block, 0, basis_semaphores.shape[0], basis_semaphores)
    stream.begin()
    wait_all(given)
    kept = pltpu.make_async_copy(field, kept_ref, semaphores.at[pieces])
    kept.start()
    mix_planes(lambda k, i, j: field[k, i, j], mix_ref, lines, rows)
    mixed = pltpu.make_async_copy(lines, lines_ref, semaphores.at[pieces + 1])
    mixed.start()
    send_lines(lines, basis, sent, out_ref, block, 0, out_semaphores, stream)
    kept.wait()
    mixed.wait()


def start_lines(field, basis_z, basis_y, columns, chunks):
    pieces, planes, rows, span = field.shape
    full = pieces * span
    block = min(256, full // chunks)
    blocks = full // chunks // block
    sent = (planes, full // chunks // columns, rows, columns)
    return pl.pallas_call(
        functools.partial(start_kernel, block),
        in_specs=[scalar, anywhere, anywhere],
        out_specs=[anywhere] * 3,
        out_shape=[
            jax.ShapeDtypeStruct((planes, rows, full), jnp.float32),
            jax.ShapeDtypeStruct(sent, jnp.float32),
            jax.ShapeDtypeStruct((2 * planes * rows, full), jnp.bfloat16),
        ],
        scratch_shapes=[
            pltpu.VMEM((planes, rows, full), jnp.float32),
            pltpu.VMEM(basis_y.shape, jnp.bfloat16),
            pltpu.VMEM((2 * planes * rows, full), jnp.bfloat16),
            pltpu.VMEM(sent, jnp.float32),
            pltpu.SemaphoreType.DMA((pieces + 2,)),
            pltpu.SemaphoreType.DMA((blocks, 1)),
            pltpu.SemaphoreType.DMA((blocks, 1)),
        ],
        compiler_params=params(),
    )(basis_z, field, basis_y)


def more_kernel(block, chunk, lines_ref, basis_ref, out_ref, basis, lines, sent, semaphore, basis_semaphores, out_semaphores):
    given = pltpu.make_async_copy(lines_ref, lines, semaphore)
    given.start()
    stream = column_stream(basis_ref, basis, block, chunk, basis_semaphores.shape[0], basis_semaphores)
    stream.begin()
    given.wait()
    send_lines(lines, basis, sent, out_ref, block, chunk, out_semaphores, stream)


def more_lines(lines, basis_y, planes, rows, columns, chunks, chunk):
    full = lines.shape[1]
    block = min(256, full // chunks)
    blocks = full // chunks // block
    sent = (planes, full // chunks // columns, rows, columns)
    return pl.pallas_call(
        functools.partial(more_kernel, block, chunk),
        in_specs=[anywhere, anywhere],
        out_specs=anywhere,
        out_shape=jax.ShapeDtypeStruct(sent, jnp.float32),
        scratch_shapes=[
            pltpu.VMEM(basis_y.shape, jnp.bfloat16),
            pltpu.VMEM(lines.shape, jnp.bfloat16),
            pltpu.VMEM(sent, jnp.float32),
            pltpu.SemaphoreType.DMA,
            pltpu.SemaphoreType.DMA((blocks, 1)),
            pltpu.SemaphoreType.DMA((blocks, 1)),
        ],
        compiler_params=params(),
    )(lines, basis_y)


def take_lines(got, lines, planes, rows):
    devices, _, columns = got.shape
    parts = devices // planes
    half = planes * (rows + spare)
    main = planes * rows
    edge_rows = lax.broadcasted_iota(jnp.int32, (spare, columns), 0) < 2
    for part in range(parts):
        lanes = slice(part * columns, (part + 1) * columns)
        edges = []
        for m in range(planes):
            high, low = halves(got[m * parts + part, :rows, :])
            lines[m * rows : (m + 1) * rows, lanes] = high
            lines[half + m * rows : half + (m + 1) * rows, lanes] = low
            edges.append(jnp.where(edge_rows, got[m * parts + part, rows:, :], 0.0))
        high, low = halves(jnp.concatenate(edges, axis=0))
        lines[main:half, lanes] = high
        lines[half + main :, lanes] = low


def part_kernel(planes, rows, block, got_ref, basis_ref, out_ref, got, basis, lines, out, given_semaphores, semaphores, out_semaphores):
    parts = got.shape[0] // planes
    width = lines.shape[1]
    half = planes * (rows + spare)
    blocks = basis.shape[0] // block
    groups = [slice(m * parts, (m + 1) * parts) for m in range(planes)]
    given = start_all([(got_ref.at[group], got.at[group]) for group in groups], given_semaphores)
    stream = Stream(
        lambda n: [(basis_ref.at[piece(n, block), :width], basis.at[piece(n, block)])], blocks, semaphores
    )
    sink = Stream(
        lambda n: [(out.at[:, piece(n, block)], out_ref.at[:, piece(n, block)])], blocks, out_semaphores
    )
    stream.begin()
    wait_all(given)
    take_lines(got, lines, planes, rows)

    def step(n, carry):
        stream.take(n)
        result = lax.dot_general(
            lines[...], basis[piece(n, block), :], (((1,), (1,)), ((), ())), preferred_element_type=jnp.float32
        )
        out[:, piece(n, block)] = result[:half] + result[half:]
        sink.start(n)
        return carry

    lax.fori_loop(0, blocks, step, 0)
    sink.end()


def part_lines(got, basis_y, planes, rows, chunks):
    full = basis_y.shape[0]
    block = min(256, full)
    half = planes * (rows + spare)
    return pl.pallas_call(
        functools.partial(part_kernel, planes, rows, block),
        in_specs=[anywhere, anywhere],
        out_specs=anywhere,
        out_shape=jax.ShapeDtypeStruct((half, full), jnp.float32),
        scratch_shapes=[
            pltpu.VMEM(got.shape, jnp.float32),
            pltpu.VMEM((full, full // chunks), jnp.bfloat16),
            pltpu.VMEM((2 * half, full // chunks), jnp.bfloat16),
            pltpu.VMEM((half, full), jnp.float32),
            pltpu.SemaphoreType.DMA((planes,)),
            pltpu.SemaphoreType.DMA((full // block, 1)),
            pltpu.SemaphoreType.DMA((full // block, 1)),
        ],
        compiler_params=params(),
    )(got, basis_y)


def column_kernel(
    rows, block, field_ref, aux_ref, ahead_ref, back_ref, along_ref, other_ref, out_ref,
    field, ahead, back, lines, spectral, buffer, given_semaphores, semaphores, out_semaphores,
):
    full, columns = field_ref.shape
    blocks = full // block
    group = block // rows
    devices = full // rows
    given = Stream(
        lambda n: [(field_ref.at[piece(n, block)], field.at[piece(n, block)])], blocks, given_semaphores
    )
    aheads = Stream(
        lambda n: [(ahead_ref.at[piece(n, block)], ahead.at[piece(n, block)])], blocks, semaphores.at[0]
    )
    backs = Stream(
        lambda n: [(back_ref.at[piece(n, block)], back.at[piece(n, block)])], blocks, semaphores.at[1]
    )
    out = Stream(
        lambda n: [(buffer.at[pl.ds(n * group, group)], out_ref.at[pl.ds(n * group, group)])],
        blocks,
        out_semaphores,
    )
    for n in range(blocks):
        given.start(n)
    aheads.begin()
    given.end()

    def strip(index, carry):
        own = piece(index, 64)
        high, low = halves(field[own, :])
        lines[own, :columns] = high
        lines[own, columns:] = low
        return carry

    lax.fori_loop(0, full // 64, strip, 0, unroll=4)

    def forth(n, carry):
        aheads.take(n)

        @pl.when(n == blocks - 1)
        def _():
            backs.begin()

        own = piece(n, block)
        result = jnp.dot(ahead[own, :], lines[...], preferred_element_type=jnp.float32)
        result = result[:, :columns] + result[:, columns:]
        high, low = halves(result / (along_ref[own, :] + other_ref[...]))
        spectral[own, :columns] = high
        spectral[own, columns:] = low
        return carry

    lax.fori_loop(0, blocks, forth, 0)

    def reverse(n, carry):
        backs.take(n)
        result = jnp.dot(back[piece(n, block), :], spectral[...], preferred_element_type=jnp.float32)
        result = result[:, :columns] + result[:, columns:]
        for part in range(group):
            buffer[n * group + part, :rows, :] = result[part * rows : (part + 1) * rows]
        return carry

    lax.fori_loop(0, blocks, reverse, 0)
    rest = aux_ref[2:, :]

    def close(n, carry):
        for part in range(group):
            own = n * group + part
            above = buffer[jnp.maximum(own - 1, 0), rows - 1 : rows, :]
            above = jnp.where(own > 0, above, 0.0)
            below = buffer[jnp.minimum(own + 1, devices - 1), 0:1, :]
            below = jnp.where(own + 1 < devices, below, 0.0)
            buffer[own, rows:, :] = jnp.concatenate([above, below, rest], axis=0)
        out.start(n)
        return carry

    lax.fori_loop(0, blocks, close, 0)
    out.end()


def column_lines(field, aux, basis_xt, basis_x, along, other, rows):
    full, columns = field.shape
    block = min(512, full)
    devices = full // rows
    return pl.pallas_call(
        functools.partial(column_kernel, rows, block),
        in_specs=[anywhere, vector, anywhere, anywhere, vector, vector],
        out_specs=anywhere,
        out_shape=jax.ShapeDtypeStruct((devices, rows + spare, columns), jnp.float32),
        scratch_shapes=[
            pltpu.VMEM((full, columns), jnp.float32),
            pltpu.VMEM((full, full), jnp.bfloat16),
            pltpu.VMEM((full, full), jnp.bfloat16),
            pltpu.VMEM((full, 2 * columns), jnp.bfloat16),
            pltpu.VMEM((full, 2 * columns), jnp.bfloat16),
            pltpu.VMEM((devices, rows + spare, columns), jnp.float32),
            pltpu.SemaphoreType.DMA((full // block, 1)),
            pltpu.SemaphoreType.DMA((2, full // block, 1)),
            pltpu.SemaphoreType.DMA((full // block, 1)),
        ],
        compiler_params=params(),
    )(field, aux, basis_xt, basis_x, along, other)


def turn_kernel(stage, last, block, chunks, *refs):
    refs = list(refs)
    take = lambda: refs.pop(0)
    mix_ref, got_ref, basis_ref = take(), take(), take()
    part_ref = take() if chunks > 1 else None
    diagonal_ref, low_x, high_x, low_y, high_y = take(), take(), take(), take(), take()
    residual_ref = take()
    if stage >= 1:
        old_z, old_edge_z, scalars_ref = take(), take(), take()
    if stage >= 2:
        old_v, old_edge_v = take(), take()
    z_ref, edge_z_ref, y_ref, aux_ref = take(), take(), take(), take()
    if stage >= 1:
        v_ref, edge_v_ref = take(), take()
    if not last:
        out_ref, lines_ref = take(), take()
    got, basis, diagonal, lines, around, edge_z, image, residual = [take() for _ in range(8)]
    if stage >= 1:
        z, v, edge_v = take(), take(), take()
    if not last:
        ahead_lines, sent = take(), take()
    part = take() if chunks > 1 else None
    given_semaphores, semaphores, late_semaphores = take(), take(), take()
    if not last:
        basis_semaphores, out_semaphores = take(), take()
    planes, rows, full = diagonal.shape
    devices, _, columns = got.shape
    parts = devices // planes
    half = planes * (rows + spare)
    main = planes * rows
    blocks = full // block
    groups = [slice(m * parts, (m + 1) * parts) for m in range(planes)]
    given = start_all([(got_ref.at[group], got.at[group]) for group in groups], given_semaphores)
    width = full // chunks
    turned = slice(full - width, full)
    fields = [(residual_ref, residual)]
    if stage >= 1:
        fields += [(old_z, z), (old_edge_z, edge_z)]
    if stage >= 2:
        fields += [(old_v, v), (old_edge_v, edge_v)]

    def needed(n):
        own = piece(n, block)
        pairs = [(basis_ref.at[own, turned], basis.at[own, turned])]
        if chunks > 1:
            pairs.append((part_ref.at[:, own], part.at[:, own]))
        return pairs + [(old.at[:, :, own], target.at[:, :, own]) for old, target in fields]

    stream = Stream(needed, blocks, semaphores)
    stream.begin()
    wait_all(given)
    take_lines(got, lines, planes, rows)
    def fold(value):
        total = value[:, :columns]
        for left in range(columns, value.shape[1], columns):
            total = total + value[:, left : left + columns]
        return total

    def finish_block(n, carry):
        stream.take(n)
        lanes = piece(n, block)
        result = lax.dot_general(
            lines[...], basis[lanes, turned], (((1,), (1,)), ((), ())), preferred_element_type=jnp.float32
        )
        result = result[:half] + result[half:]
        if chunks > 1:
            result = result + part[:, lanes]
        if stage >= 1:
            length = scalars_ref[2:3, 0:1]
            turn = scalars_ref[3:4, 0:1]
        for k in range(planes):
            value = result[:rows] * mix_ref[k, 0]
            edge = result[main : main + spare] * mix_ref[k, 0]
            for m in range(1, planes):
                value = value + result[m * rows : (m + 1) * rows] * mix_ref[k, m]
                edge = edge + result[main + m * spare : main + (m + 1) * spare] * mix_ref[k, m]
            if stage >= 1:
                if stage >= 2:
                    value = value + turn * v[k, :, lanes]
                    edge = edge + turn * edge_v[k, :, lanes]
                v[k, :, lanes] = value
                edge_v[k, :, lanes] = edge
                value = z[k, :, lanes] - length * value
                edge = edge_z[k, :, lanes] - length * edge
            edge_z[k, :, lanes] = edge
            shared = fold(residual[k, :, lanes] * value)
            for start in range(0, rows, 8):
                carry = carry + shared[start : start + 8]
            around[k, spare : spare + rows, lanes] = value
            around[k, spare - 1 : spare, lanes] = edge[0:1]
            around[k, spare + rows : spare + rows + 1, lanes] = edge[1:2]
        return carry

    diagonal_copy = pltpu.make_async_copy(diagonal_ref, diagonal, late_semaphores.at[0])
    diagonal_copy.start()
    nothing = jnp.zeros((8, columns), jnp.float32)
    product = lax.fori_loop(0, blocks, finish_block, nothing)
    done = [(around.at[:, spare : spare + rows], z_ref), (edge_z, edge_z_ref)]
    if stage >= 1:
        done += [(v, v_ref), (edge_v, edge_v_ref)]
    done = start_all(done, late_semaphores.at[2:6])
    ahead = None
    if not last and chunks > 1:
        ahead = column_stream(basis_ref, basis, block, 0, width // block, basis_semaphores)
        ahead.begin()
    diagonal_copy.wait()

    def operate(index, carry):
        k = index // (rows // 8)
        tile = index - k * (rows // 8)
        own = piece(tile, 8)
        window = around[k, pl.ds(pl.multiple_of(tile * 8, 8), 24), :]
        value = window[8:16]
        above = pltpu.roll(window, 1, 0)[8:16]
        below = pltpu.roll(window, 23, 0)[8:16]
        middle = pl.ds(pl.multiple_of(tile * 8 + spare, 8), 8)
        before = around[jnp.where(k == 0, planes - 1, k - 1), middle, :]
        after = around[jnp.where(k == planes - 1, 0, k + 1), middle, :]
        total = diagonal[k, own, :] * value
        total = total + (low_x[own, :] * (value - above) - high_x[own, :] * (below - value))
        left = pltpu.roll(value, 1, 1)
        right = pltpu.roll(value, full - 1, 1)
        total = total + (low_y[...] * (value - left) - high_y[...] * (right - value))
        total = total + (2.0 * value - before - after)
        image[k, own, :] = total
        return carry + fold(value * total)

    bend = lax.fori_loop(0, planes * (rows // 8), operate, nothing, unroll=2)
    aux_ref[...] = jnp.concatenate(
        [
            nothing[:2],
            jnp.sum(product, axis=0, keepdims=True),
            jnp.sum(bend, axis=0, keepdims=True),
            nothing[4:],
        ],
        axis=0,
    )
    image_copy = pltpu.make_async_copy(image, y_ref, late_semaphores.at[1])
    image_copy.start()
    if not last:
        mix_planes(lambda k, i, j: image[k, i, j], mix_ref, ahead_lines, rows)
        mixed = pltpu.make_async_copy(ahead_lines, lines_ref, late_semaphores.at[6])
        mixed.start()
        send_lines(ahead_lines, basis, sent, out_ref, block, 0, out_semaphores, ahead)
        mixed.wait()
    image_copy.wait()
    wait_all(done)


def turn_lines(stage, last, got, part, operator, basis_z, basis_y, state, chunks):
    planes, rows, full = operator[0].shape
    _, _, columns = got.shape
    block = min(256, full // chunks)
    blocks = full // block
    field_shape = jax.ShapeDtypeStruct((planes, rows, full), jnp.float32)
    edge_shape = jax.ShapeDtypeStruct((planes, spare, full), jnp.float32)
    specs = [scalar] + [anywhere] * (4 if chunks > 1 else 3) + [vector] * 4
    given = [basis_z, got, basis_y] + ([part] if chunks > 1 else []) + list(operator)
    specs.append(anywhere)
    given.append(state["residual"])
    if stage >= 1:
        specs += [anywhere] * 2 + [vector]
        given += [state["z"], state["edge_z"], state["scalars"]]
    if stage >= 2:
        specs += [anywhere] * 2
        given += [state["v"], state["edge_v"]]
    names = ["z", "edge_z", "y", "aux"]
    outs = [anywhere] * 3 + [vector]
    shapes = [field_shape, edge_shape, field_shape, jax.ShapeDtypeStruct((spare, columns), jnp.float32)]
    if stage >= 1:
        names += ["v", "edge_v"]
        outs += [anywhere, anywhere]
        shapes += [field_shape, edge_shape]
    field = pltpu.VMEM((planes, rows, full), jnp.float32)
    edge = pltpu.VMEM((planes, spare, full), jnp.float32)
    scratch = [
        pltpu.VMEM(got.shape, jnp.float32),
        pltpu.VMEM(basis_y.shape, jnp.bfloat16),
        field,
        pltpu.VMEM((2 * planes * (rows + spare), full // chunks), jnp.bfloat16),
        pltpu.VMEM((planes, rows + 2 * spare, full), jnp.float32),
        edge,
        field,
        field,
    ]
    if stage >= 1:
        scratch += [field, field, edge]
    if not last:
        sent = (planes, full // chunks // columns, rows, columns)
        mixed = (2 * planes * rows, full)
        names += ["sent", "lines"]
        outs += [anywhere] * 2
        shapes += [jax.ShapeDtypeStruct(sent, jnp.float32), jax.ShapeDtypeStruct(mixed, jnp.bfloat16)]
        scratch += [pltpu.VMEM(mixed, jnp.bfloat16), pltpu.VMEM(sent, jnp.float32)]
    if chunks > 1:
        scratch.append(pltpu.VMEM(part.shape, jnp.float32))
    scratch += [
        pltpu.SemaphoreType.DMA((planes,)),
        pltpu.SemaphoreType.DMA((blocks, 7)),
        pltpu.SemaphoreType.DMA((7,)),
    ]
    if not last:
        scratch += [pltpu.SemaphoreType.DMA((blocks // chunks, 1))] * 2
    results = pl.pallas_call(
        functools.partial(turn_kernel, stage, last, block, chunks),
        in_specs=specs,
        out_specs=outs,
        out_shape=shapes,
        scratch_shapes=scratch,
        compiler_params=params(),
    )(*given)
    return dict(zip(names, results))


def first_kernel(
    rows, velocity_ref, weight_ref, code_ref, above_ref, below_ref, side_ref, half_x_ref, half_y_ref,
    source_ref, predicted_ref, fields, moved, kept, semaphores,
):
    planes, count, span = weight_ref.shape
    wide = half_y_ref.shape[1]
    pad = 16
    copies = []
    for channel in range(5):
        if channel < 3:
            main = velocity_ref.at[channel]
        else:
            main = weight_ref if channel == 3 else code_ref
        target = fields.at[channel]
        copies.append((main, target.at[:, pad : pad + count, :span]))
        copies.append((above_ref.at[channel], target.at[:, pad - 8 : pad, :span]))
        copies.append((below_ref.at[channel], target.at[:, pad + count : pad + count + 8, :span]))
        copies.append((side_ref.at[channel], target.at[:, :, span:]))
    copies = [
        pltpu.make_async_copy(given, target, semaphores.at[index])
        for index, (given, target) in enumerate(copies)
    ]
    for copy in copies:
        copy.start()
    for copy in copies:
        copy.wait()
    tiles = count // 8 + 2
    half_y = half_y_ref[...]

    def lane_slope(value):
        return pltpu.roll(value, wide - 1, 1) - pltpu.roll(value, 1, 1)

    def advance(index, carry):
        k = index // tiles
        start = pl.multiple_of(8 + (index - k * tiles) * 8, 8)
        window = pl.ds(pl.multiple_of(start - 8, 8), 24)
        own = pl.ds(start, 8)
        before = jnp.where(k == 0, planes - 1, k - 1)
        after = jnp.where(k == planes - 1, 0, k + 1)
        half_x = half_x_ref[own, :]
        first = fields[0, k, window, :]
        second = fields[1, k, own, :]
        third_before = fields[2, before, own, :]
        third_after = fields[2, after, own, :]
        weight = fields[3, k, own, :]
        for c in range(3):
            value = first if c == 0 else fields[c, k, window, :]
            along = first * value
            center = value[8:16]
            total = half_x * (pltpu.roll(along, 23, 0)[8:16] - pltpu.roll(along, 1, 0)[8:16])
            total = total + half_y * lane_slope(second * center)
            total = total + 0.5 * (third_after * fields[c, after, own, :] - third_before * fields[c, before, own, :])
            share = weight * total
            moved[c, k, own, :] = share
            kept[c, k, own, :] = total - share
        return carry

    lax.fori_loop(0, planes * tiles, advance, 0, unroll=4)

    def settle(index, carry):
        k = index // tiles
        start = pl.multiple_of(8 + (index - k * tiles) * 8, 8)
        window = pl.ds(pl.multiple_of(start - 8, 8), 24)
        own = pl.ds(start, 8)
        code = fields[4, k, window, :]
        inside_x = half_x_ref[own, :] > 0.0
        inside_y = half_y > 0.0
        for c in range(3):
            share = moved[c, k, window, :]
            received = pltpu.roll(jnp.where(code == 1.0, share, 0.0), 1, 0)[8:16] + pltpu.roll(jnp.where(code == 2.0, share, 0.0), 23, 0)[8:16]
            center = share[8:16]
            middle = code[8:16]
            received = received + pltpu.roll(jnp.where(middle == 3.0, center, 0.0), 1, 1)
            received = received + pltpu.roll(jnp.where(middle == 4.0, center, 0.0), wide - 1, 1)
            result = fields[c, k, own, :] - time_step * (kept[c, k, own, :] + received)
            if c == 0:
                result = jnp.where(inside_x, result, 0.0)
            if c == 1:
                result = jnp.where(inside_y, result, 0.0)
            kept[c, k, own, :] = result
        return carry

    lax.fori_loop(0, planes * tiles, settle, 0, unroll=4)
    inner = count // 8
    group = rows // 8

    def collect(index, carry):
        k = index // inner
        tile = index - k * inner
        start = pl.multiple_of(pad + tile * 8, 8)
        window = pl.ds(pl.multiple_of(start - 8, 8), 24)
        own = pl.ds(start, 8)
        before = jnp.where(k == 0, planes - 1, k - 1)
        after = jnp.where(k == planes - 1, 0, k + 1)
        first = kept[0, k, window, :]
        second = kept[1, k, own, :]
        total = half_x_ref[own, :] * (pltpu.roll(first, 23, 0)[8:16] - pltpu.roll(first, 1, 0)[8:16])
        total = total + half_y * lane_slope(second)
        total = total + 0.5 * (kept[2, after, own, :] - kept[2, before, own, :])
        target = tile // group
        spot = pl.multiple_of((tile - target * group) * 8, 8)
        source_ref[target, k, pl.ds(spot, 8), :] = -total[:, :span]
        out = pl.ds(pl.multiple_of(tile * 8, 8), 8)
        predicted_ref[0, k, out, :] = first[8:16, :span]
        predicted_ref[1, k, out, :] = second[:, :span]
        predicted_ref[2, k, out, :] = kept[2, k, own, :span]
        return carry

    lax.fori_loop(0, planes * inner, collect, 0, unroll=8)


def first_step(velocity, weight, code, above, below, side, half_x, half_y, rows):
    planes, count, span = weight.shape
    tall, wide = half_x.shape[0], half_y.shape[1]
    return pl.pallas_call(
        functools.partial(first_kernel, rows),
        in_specs=[anywhere] * 6 + [vector] * 2,
        out_specs=[vector] * 2,
        out_shape=[
            jax.ShapeDtypeStruct((count // rows, planes, rows, span), jnp.float32),
            jax.ShapeDtypeStruct((3, planes, count, span), jnp.float32),
        ],
        scratch_shapes=[
            pltpu.VMEM((5, planes, tall, wide), jnp.float32),
            pltpu.VMEM((3, planes, tall, wide), jnp.float32),
            pltpu.VMEM((3, planes, tall, wide), jnp.float32),
            pltpu.SemaphoreType.DMA((20,)),
        ],
        compiler_params=params(),
    )(velocity, weight, code, above, below, side, half_x, half_y)


def neighbours(axis, last, leading):
    size = lax.axis_size(axis)
    up = [(i, i + 1) for i in range(size - 1)]
    down = [(i + 1, i) for i in range(size - 1)]
    return lax.ppermute(last, axis, up), lax.ppermute(leading, axis, down)


def extended_1(value, start, count, before, after):
    padded = jnp.pad(value, (before, after))
    return lax.dynamic_slice_in_dim(padded, start, count + before + after)


def add_kernel(numbers_ref, pressure_ref, direction_ref, lifted_ref, out_ref):
    length = numbers_ref[2:3, 0:1]
    turn = numbers_ref[3:4, 0:1]
    for k in range(pressure_ref.shape[0]):
        direction = lifted_ref[k] + turn * direction_ref[k]
        out_ref[0, k] = pressure_ref[k] + length * direction


def add_step(numbers, pressure, direction, lifted, pieces):
    planes, rows, full = pressure.shape
    span = full // pieces
    field = pl.BlockSpec((planes, rows, span), lambda n: (0, 0, n))
    return pl.pallas_call(
        add_kernel,
        grid=(pieces,),
        in_specs=[vector] + [field] * 3,
        out_specs=pl.BlockSpec((1, planes, rows, span), lambda n: (n, 0, 0, 0)),
        out_shape=jax.ShapeDtypeStruct((pieces, planes, rows, span), jnp.float32),
        compiler_params=params(),
    )(numbers, pressure, direction, lifted)


def correct_kernel(
    predicted_ref, own_ref, previous_ref, next_ref, above_ref, below_ref, left_ref, right_ref,
    half_x_ref, half_y_ref, corrected_ref, pressure_ref,
):
    n = pl.program_id(0)
    last = pl.num_programs(0) - 1
    _, planes, rows, _ = own_ref.shape
    for k in range(planes):
        value = own_ref[0, k]
        above = jnp.where(n == 0, above_ref[k], previous_ref[0, k, rows - 1 : rows, :])
        below = jnp.where(n == last, below_ref[k], next_ref[0, k, 0:1, :])
        rising = jnp.concatenate([value[1:], below], axis=0) - jnp.concatenate([above, value[:-1]], axis=0)
        ahead = jnp.concatenate([value[:, 1:], right_ref[0, k]], axis=1)
        behind = jnp.concatenate([left_ref[0, k], value[:, :-1]], axis=1)
        across = own_ref[0, (k + 1) % planes] - own_ref[0, (k - 1) % planes]
        pressure_ref[:, k, :] = value
        corrected_ref[0, :, k, :] = predicted_ref[0, k] - half_x_ref[...] * rising
        corrected_ref[1, :, k, :] = predicted_ref[1, k] - half_y_ref[...] * (ahead - behind)
        corrected_ref[2, :, k, :] = predicted_ref[2, k] - 0.5 * across


def correct_step(predicted, pressure, above, below, left, right, half_x, half_y):
    pieces, planes, rows, span = pressure.shape
    count = pieces * rows
    own = lambda shift: pl.BlockSpec(
        (1, planes, rows, span), lambda n: (jnp.clip(n + shift, 0, pieces - 1), 0, 0, 0)
    )
    column = pl.BlockSpec((1, planes, rows, 1), lambda n: (n, 0, 0, 0))
    return pl.pallas_call(
        correct_kernel,
        grid=(pieces,),
        in_specs=[
            pl.BlockSpec((3, planes, rows, span), lambda n: (0, 0, n, 0)),
            own(0),
            own(-1),
            own(1),
            vector,
            vector,
            column,
            column,
            pl.BlockSpec((rows, 1), lambda n: (n, 0)),
            vector,
        ],
        out_specs=[
            pl.BlockSpec((3, rows, planes, span), lambda n: (0, n, 0, 0)),
            pl.BlockSpec((rows, planes, span), lambda n: (n, 0, 0)),
        ],
        out_shape=[
            jax.ShapeDtypeStruct((3, count, planes, span), jnp.float32),
            jax.ShapeDtypeStruct((count, planes, span), jnp.float32),
        ],
        compiler_params=params(),
    )(predicted, pressure, pressure, pressure, above, below, left, right, half_x, half_y)


def per_device(
    velocity,
    cut_flags,
    redirect,
    share_weight,
    inverse_dx,
    inverse_dy,
    basis_x,
    basis_y,
    basis_z,
    eigen_x,
    eigen_y,
    eigen_z,
):
    x_parts = lax.axis_size("gx")
    y_parts = lax.axis_size("gy")
    devices = x_parts * y_parts
    x_index = lax.axis_index("gx")
    y_index = lax.axis_index("gy")
    own = x_index * y_parts + y_index
    x_count, planes, y_count = velocity.shape[1:]
    full_x = x_count * x_parts
    full_y = y_count * y_parts
    rows = full_x // devices
    columns = planes * full_y // devices
    chunks = 2 if columns % 256 == 0 else 1
    columns = columns // chunks
    column_blocks = devices // planes
    inverse_x = lax.dynamic_slice_in_dim(inverse_dx, x_index * x_count, x_count)
    inverse_y = lax.dynamic_slice_in_dim(inverse_dy, y_index * y_count, y_count)
    flags = cut_flags.astype(jnp.float32)
    code = (cut_flags * (redirect + 1)).astype(jnp.float32)
    weight = share_weight * flags
    reach = 3

    def edge_rows(part):
        return jnp.concatenate([velocity[:, part], weight[None, part], code[None, part]])

    above, below = neighbours("gx", edge_rows(slice(x_count - reach, None)), edge_rows(slice(0, reach)))
    velocity = velocity.transpose(0, 2, 1, 3)
    weight = weight.transpose(1, 0, 2)
    code = code.transpose(1, 0, 2)
    above = above.transpose(0, 2, 1, 3)
    below = below.transpose(0, 2, 1, 3)

    def edge_columns(part):
        middle = jnp.concatenate([velocity[..., part], weight[None, ..., part], code[None, ..., part]])
        return jnp.concatenate([above[..., part], middle, below[..., part]], axis=2).swapaxes(2, 3)

    left, right = neighbours("gy", edge_columns(slice(y_count - reach, None)), edge_columns(slice(0, reach)))
    side = jnp.concatenate([right, jnp.zeros((5, planes, 128 - 2 * reach, x_count + 2 * reach), jnp.float32), left], axis=2)
    side = jnp.pad(side.swapaxes(2, 3), ((0, 0), (0, 0), (16 - reach, 16 - reach), (0, 0)))
    above = jnp.pad(above, ((0, 0), (0, 0), (8 - reach, 0), (0, 0)))
    below = jnp.pad(below, ((0, 0), (0, 0), (0, 8 - reach), (0, 0)))
    half_x = 0.5 * extended_1(inverse_dx, x_index * x_count, x_count, 16, 16)[:, None]
    half_y = 0.5 * extended_1(inverse_dy, y_index * y_count, y_count, reach, reach)
    half_y = jnp.concatenate([half_y[reach:], jnp.zeros((128 - 2 * reach,), jnp.float32), half_y[:reach]])[None]
    source, predicted = first_step(velocity, weight, code, above, below, side, half_x, half_y, rows)
    diagonal = (cell_shift + cut_shift * flags).reshape(y_parts, rows, planes, y_count).transpose(0, 2, 1, 3)
    diagonal = lax.all_to_all(diagonal, "gy", 0, 0, tiled=True)
    source, diagonal = lax.optimization_barrier((source, diagonal))
    source = lax.all_to_all(source, "gy", 0, 0, tiled=True)
    source, basis_xt = lax.optimization_barrier((source, basis_x.T))
    diagonal = diagonal.transpose(1, 2, 0, 3).reshape(planes, rows, full_y)
    whole_x = jnp.pad(inverse_dx, 1)
    face_x = lax.dynamic_slice_in_dim(whole_x[:-1] * whole_x[1:], own * rows, rows + 1)
    whole_y = jnp.pad(inverse_dy, 1)
    face_y = whole_y[:-1] * whole_y[1:]
    operator = (diagonal, face_x[:-1, None], face_x[1:, None], face_y[None, :-1], face_y[None, 1:])
    along = eigen_x[:, None]
    other = [
        (
            lax.dynamic_slice_in_dim(
                eigen_y, full_y // chunks * chunk + (own % column_blocks) * columns, columns
            )
            + lax.dynamic_slice_in_dim(eigen_z, own // column_blocks, 1)
        )[None]
        for chunk in range(chunks)
    ]

    def apply(sent, lines, aux):
        part = sums = None
        sents = [sent] + [
            more_lines(lines, basis_y, planes, rows, columns, chunks, chunk) for chunk in range(1, chunks)
        ]
        for chunk, sent in enumerate(sents):
            sent = sent.reshape(devices, rows, columns)
            got = lax.all_to_all(sent, both, 0, 0, tiled=True).reshape(full_x, columns)
            given = aux if chunk == 0 else jnp.zeros((spare, columns), jnp.float32)
            got = column_lines(got, given, basis_xt, basis_x, along, other[chunk], rows)
            got = lax.all_to_all(got, both, 0, 0, tiled=True)
            if chunk == 0:
                sums = got[:, rows:]
            if chunk + 1 < chunks:
                part = part_lines(got, basis_y, planes, rows, chunks)
        return got, part, sums

    def numbers_of(sums, numbers):
        product = jnp.sum(sums[:, 2])
        bend = jnp.sum(sums[:, 3])
        turn = jnp.zeros_like(product)
        if numbers is not None:
            turn = product / numbers[0, 0]
            bend = bend - turn * turn * numbers[1, 0]
        numbers = jnp.stack([product, bend, product / bend, turn])
        return jnp.broadcast_to(jnp.pad(numbers, (0, 4))[:, None], (8, 128))

    residual, sent, lines = start_lines(source, basis_z, basis_y, columns, chunks)
    got, part, _ = apply(sent, lines, jnp.zeros((spare, columns), jnp.float32))
    state = {"residual": residual}
    state |= turn_lines(0, False, got, part, operator, basis_z, basis_y, state, chunks)
    numbers = None
    for stage in range(1, ITERS):
        got, part, sums = apply(state["sent"], state["lines"], state["aux"])
        numbers = numbers_of(sums, numbers)
        length, turn = numbers[2, 0], numbers[3, 0]
        if stage == 1:
            direction, image = state["z"], state["y"]
            pressure = length * direction
        else:
            direction = state["z"] + turn * direction
            image = state["y"] + turn * image
            pressure = pressure + length * direction
        state["residual"] = state["residual"] - length * image
        state["scalars"] = numbers
        last = stage + 1 == ITERS
        state |= turn_lines(stage, last, got, part, operator, basis_z, basis_y, state, chunks)
    sums = jnp.broadcast_to(state["aux"][None], (devices, spare, columns))
    sums = lax.all_to_all(sums, both, 0, 0, tiled=True)
    numbers = numbers_of(sums, numbers)
    pressure = add_step(numbers, pressure, direction, state["z"], y_parts)
    pressure = lax.all_to_all(pressure, "gy", 0, 0, tiled=True)
    above, below = neighbours("gx", pressure[-1, :, -1:], pressure[0, :, :1])
    left, right = neighbours("gy", pressure[..., -1], pressure[..., 0])
    half_x = 0.5 * inverse_x[:, None]
    half_y = 0.5 * inverse_y[None]
    corrected, pressure = correct_step(
        predicted, pressure, above, below, left[..., None], right[..., None], half_x, half_y
    )
    return corrected, pressure


def solution(mesh):
    in_specs = (
        P(None, "gx", None, "gy"),
        P("gx", None, "gy"),
        P("gx", None, "gy"),
        P("gx", None, "gy"),
        P(),
        P(),
        P(),
        P(),
        P(),
        P(),
        P(),
        P(),
    )
    out_specs = (P(None, "gx", None, "gy"), P("gx", None, "gy"))
    return jax.shard_map(
        per_device, mesh=mesh, in_specs=in_specs, out_specs=out_specs, check_vma=False
    )
```

```python
import functools

import jax
import jax.numpy as jnp
from jax import lax
from jax.experimental import pallas as pl
from jax.experimental.pallas import tpu as pltpu
from jax.sharding import PartitionSpec as P

ITERS = 4


time_step = 0.25
cell_shift = 0.05
cut_shift = 0.45
both = ("gx", "gy")
spare = 8
vmem_bytes = 56 * 1024 * 1024


def halves(value):
    high = value.astype(jnp.bfloat16)
    low = (value - high.astype(jnp.float32)).astype(jnp.bfloat16)
    return high, low


def params():
    return pltpu.CompilerParams(vmem_limit_bytes=vmem_bytes)


def mix_planes(read, mix_ref, lines, rows):
    planes = mix_ref.shape[0]
    width = lines.shape[1]
    lane = 512 if width % 512 == 0 else width
    half = planes * rows

    def strip(index, carry):
        start = pl.multiple_of(index * 16, 16)
        for left in range(0, width, lane):
            fields = [read(k, pl.ds(start, 16), pl.ds(left, lane)) for k in range(planes)]
            for m in range(planes):
                total = fields[0] * mix_ref[0, m]
                for k in range(1, planes):
                    total = total + fields[k] * mix_ref[k, m]
                high, low = halves(total)
                lines[pl.ds(m * rows + start, 16), pl.ds(left, lane)] = high
                lines[pl.ds(half + m * rows + start, 16), pl.ds(left, lane)] = low
        return carry

    lax.fori_loop(0, rows // 16, strip, 0)


anywhere = pl.BlockSpec(memory_space=pl.ANY)
vector = pl.BlockSpec(memory_space=pltpu.VMEM)
scalar = pl.BlockSpec(memory_space=pltpu.SMEM)


class Stream:
    def __init__(self, pairs, count, semaphores):
        self.pairs = pairs
        self.count = count
        self.semaphores = semaphores

    def copies(self, n):
        pairs = self.pairs(n)
        return [
            pltpu.make_async_copy(given, target, self.semaphores.at[n, index])
            for index, (given, target) in enumerate(pairs)
        ]

    def start(self, n):
        for copy in self.copies(n):
            copy.start()

    def begin(self):
        for n in range(min(2, self.count)):
            self.start(n)

    def take(self, n):
        for copy in self.copies(n):
            copy.wait()

        @pl.when(n + 2 < self.count)
        def _():
            self.start(n + 2)

    def end(self):
        def step(n, carry):
            for copy in self.copies(n):
                copy.wait()
            return carry

        lax.fori_loop(0, self.count, step, 0)


def start_all(pairs, semaphores):
    copies = [
        pltpu.make_async_copy(given, target, semaphores.at[index])
        for index, (given, target) in enumerate(pairs)
    ]
    for copy in copies:
        copy.start()
    return copies


def wait_all(copies):
    for copy in copies:
        copy.wait()


def piece(index, size):
    return pl.ds(pl.multiple_of(index * size, size), size)


def send_lines(lines, basis, sent, out_ref, block, chunk, semaphores, stream=None):
    planes, all_parts, rows, columns = sent.shape
    half = planes * rows
    parts = block // columns
    blocks = all_parts // parts
    out = Stream(
        lambda n: [(sent.at[:, pl.ds(n * parts, parts)], out_ref.at[:, pl.ds(n * parts, parts)])],
        blocks,
        semaphores,
    )

    def step(n, carry):
        if stream is not None:
            stream.take(n)
        result = jnp.dot(lines[...], basis[:, piece(chunk * blocks + n, block)], preferred_element_type=jnp.float32)
        result = result[:half] + result[half:]
        for m in range(planes):
            for part in range(parts):
                sent[m, n * parts + part] = result[
                    m * rows : (m + 1) * rows, part * columns : (part + 1) * columns
                ]
        out.start(n)
        return carry

    lax.fori_loop(0, blocks, step, 0)
    out.end()


def column_stream(basis_ref, basis, block, chunk, blocks, semaphores):
    def pairs(n):
        own = piece(chunk * blocks + n, block)
        return [(basis_ref.at[:, own], basis.at[:, own])]

    return Stream(pairs, blocks, semaphores)


def start_kernel(
    block, mix_ref, field_ref, basis_ref, kept_ref, out_ref,
    field, basis, lines, sent, semaphores, basis_semaphores, out_semaphores,
):
    pieces, planes, rows, span = field_ref.shape
    given = [(field_ref.at[n], field.at[:, :, n * span : (n + 1) * span]) for n in range(pieces)]
    given = start_all(given, semaphores)
    stream = column_stream(basis_ref, basis, block, 0, basis_semaphores.shape[0], basis_semaphores)
    stream.begin()
    wait_all(given)
    kept = pltpu.make_async_copy(field, kept_ref, semaphores.at[pieces])
    kept.start()
    mix_planes(lambda k, i, j: field[k, i, j], mix_ref, lines, rows)
    send_lines(lines, basis, sent, out_ref, block, 0, out_semaphores, stream)
    kept.wait()


def start_lines(field, basis_z, basis_y, columns, chunks):
    pieces, planes, rows, span = field.shape
    full = pieces * span
    block = min(256, full // chunks)
    blocks = full // chunks // block
    sent = (planes, full // chunks // columns, rows, columns)
    return pl.pallas_call(
        functools.partial(start_kernel, block),
        in_specs=[scalar, anywhere, anywhere],
        out_specs=[anywhere] * 2,
        out_shape=[
            jax.ShapeDtypeStruct((planes, rows, full), jnp.float32),
            jax.ShapeDtypeStruct(sent, jnp.float32),
        ],
        scratch_shapes=[
            pltpu.VMEM((planes, rows, full), jnp.float32),
            pltpu.VMEM(basis_y.shape, jnp.bfloat16),
            pltpu.VMEM((2 * planes * rows, full), jnp.bfloat16),
            pltpu.VMEM(sent, jnp.float32),
            pltpu.SemaphoreType.DMA((pieces + 1,)),
            pltpu.SemaphoreType.DMA((blocks, 1)),
            pltpu.SemaphoreType.DMA((blocks, 1)),
        ],
        compiler_params=params(),
    )(basis_z, field, basis_y)


def more_kernel(
    block, chunk, mix_ref, field_ref, basis_ref, out_ref, field, basis, lines, sent, semaphore, basis_semaphores, out_semaphores
):
    given = pltpu.make_async_copy(field_ref, field, semaphore)
    given.start()
    stream = column_stream(basis_ref, basis, block, chunk, basis_semaphores.shape[0], basis_semaphores)
    stream.begin()
    given.wait()
    mix_planes(lambda k, i, j: field[k, i, j], mix_ref, lines, field.shape[1])
    send_lines(lines, basis, sent, out_ref, block, chunk, out_semaphores, stream)


def more_lines(field, basis_z, basis_y, columns, chunks, chunk):
    planes, rows, full = field.shape
    block = min(256, full // chunks)
    blocks = full // chunks // block
    sent = (planes, full // chunks // columns, rows, columns)
    return pl.pallas_call(
        functools.partial(more_kernel, block, chunk),
        in_specs=[scalar, anywhere, anywhere],
        out_specs=anywhere,
        out_shape=jax.ShapeDtypeStruct(sent, jnp.float32),
        scratch_shapes=[
            pltpu.VMEM(field.shape, jnp.float32),
            pltpu.VMEM(basis_y.shape, jnp.bfloat16),
            pltpu.VMEM((2 * planes * rows, full), jnp.bfloat16),
            pltpu.VMEM(sent, jnp.float32),
            pltpu.SemaphoreType.DMA,
            pltpu.SemaphoreType.DMA((blocks, 1)),
            pltpu.SemaphoreType.DMA((blocks, 1)),
        ],
        compiler_params=params(),
    )(basis_z, field, basis_y)


def take_lines(got, lines, planes, rows):
    devices, _, columns = got.shape
    parts = devices // planes
    half = planes * (rows + spare)
    main = planes * rows
    edge_rows = lax.broadcasted_iota(jnp.int32, (spare, columns), 0) < 2
    for part in range(parts):
        lanes = slice(part * columns, (part + 1) * columns)
        edges = []
        for m in range(planes):
            high, low = halves(got[m * parts + part, :rows, :])
            lines[m * rows : (m + 1) * rows, lanes] = high
            lines[half + m * rows : half + (m + 1) * rows, lanes] = low
            edges.append(jnp.where(edge_rows, got[m * parts + part, rows:, :], 0.0))
        high, low = halves(jnp.concatenate(edges, axis=0))
        lines[main:half, lanes] = high
        lines[half + main :, lanes] = low


def mixed_back(result, mix_ref, k, rows):
    planes = mix_ref.shape[0]
    main = planes * rows
    value = result[:rows] * mix_ref[k, 0]
    edge = result[main : main + spare] * mix_ref[k, 0]
    for m in range(1, planes):
        value = value + result[m * rows : (m + 1) * rows] * mix_ref[k, m]
        edge = edge + result[main + m * spare : main + (m + 1) * spare] * mix_ref[k, m]
    return value, edge


def part_kernel(stage, rows, block, *refs):
    refs = list(refs)
    take = lambda: refs.pop(0)
    mix_ref, got_ref, basis_ref = take(), take(), take()
    if stage >= 1:
        scalars_ref, old_z, old_edge_z = take(), take(), take()
    if stage >= 2:
        old_v, old_edge_v = take(), take()
    out_refs = [take() for _ in range(4 if stage >= 1 else 2)]
    got, basis, lines = take(), take(), take()
    outs = [take() for _ in range(4 if stage >= 1 else 2)]
    given_semaphores, semaphores, out_semaphores = take(), take(), take()
    z, edge_z = outs[:2]
    planes = mix_ref.shape[0]
    parts = got.shape[0] // planes
    width = lines.shape[1]
    half = planes * (rows + spare)
    blocks = basis.shape[0] // block
    groups = [slice(m * parts, (m + 1) * parts) for m in range(planes)]
    given = start_all([(got_ref.at[group], got.at[group]) for group in groups], given_semaphores)
    fields = []
    if stage >= 1:
        v, edge_v = outs[2:]
        fields += [(old_z, z), (old_edge_z, edge_z)]
    if stage >= 2:
        fields += [(old_v, v), (old_edge_v, edge_v)]

    def needed(n):
        own = piece(n, block)
        pairs = [(basis_ref.at[own, :width], basis.at[own])]
        return pairs + [(old.at[:, :, own], target.at[:, :, own]) for old, target in fields]

    def made(n):
        own = piece(n, block)
        return [(out.at[:, :, own], out_ref.at[:, :, own]) for out, out_ref in zip(outs, out_refs)]

    stream = Stream(needed, blocks, semaphores)
    sink = Stream(made, blocks, out_semaphores)
    stream.begin()
    wait_all(given)
    take_lines(got, lines, planes, rows)

    def step(n, carry):
        stream.take(n)
        lanes = piece(n, block)
        result = lax.dot_general(
            lines[...], basis[lanes, :], (((1,), (1,)), ((), ())), preferred_element_type=jnp.float32
        )
        result = result[:half] + result[half:]
        if stage >= 1:
            length = scalars_ref[2:3, 0:1]
            turn = scalars_ref[3:4, 0:1]
        for k in range(planes):
            value, edge = mixed_back(result, mix_ref, k, rows)
            if stage >= 1:
                if stage >= 2:
                    value = value + turn * v[k, :, lanes]
                    edge = edge + turn * edge_v[k, :, lanes]
                v[k, :, lanes] = value
                edge_v[k, :, lanes] = edge
                value = z[k, :, lanes] - length * value
                edge = edge_z[k, :, lanes] - length * edge
            z[k, :, lanes] = value
            edge_z[k, :, lanes] = edge
        sink.start(n)
        return carry

    lax.fori_loop(0, blocks, step, 0)
    sink.end()


def part_lines(stage, got, basis_z, basis_y, rows, chunks, state):
    planes = basis_z.shape[0]
    full = basis_y.shape[0]
    block = min(256, full)
    half = planes * (rows + spare)
    field, edge = (planes, rows, full), (planes, spare, full)
    names = ["z", "edge_z"]
    given = [basis_z, got, basis_y]
    specs = [scalar, anywhere, anywhere]
    if stage >= 1:
        names += ["v", "edge_v"]
        given += [state["scalars"], state["z"], state["edge_z"]]
        specs += [vector, anywhere, anywhere]
    if stage >= 2:
        given += [state["v"], state["edge_v"]]
        specs += [anywhere, anywhere]
    shapes = [field, edge] * (len(names) // 2)
    results = pl.pallas_call(
        functools.partial(part_kernel, stage, rows, block),
        in_specs=specs,
        out_specs=[anywhere] * len(names),
        out_shape=[jax.ShapeDtypeStruct(shape, jnp.float32) for shape in shapes],
        scratch_shapes=[
            pltpu.VMEM(got.shape, jnp.float32),
            pltpu.VMEM((full, full // chunks), jnp.bfloat16),
            pltpu.VMEM((2 * half, full // chunks), jnp.bfloat16),
        ]
        + [pltpu.VMEM(shape, jnp.float32) for shape in shapes]
        + [
            pltpu.SemaphoreType.DMA((planes,)),
            pltpu.SemaphoreType.DMA((full // block, 5)),
            pltpu.SemaphoreType.DMA((full // block, 4)),
        ],
        compiler_params=params(),
    )(*given)
    return dict(zip(names, results))


def column_kernel(
    rows, block, field_ref, aux_ref, ahead_ref, back_ref, along_ref, other_ref, out_ref,
    field, ahead, back, lines, spectral, buffer, given_semaphores, semaphores, out_semaphores,
):
    full, columns = field_ref.shape
    blocks = full // block
    group = block // rows
    devices = full // rows
    given = Stream(
        lambda n: [(field_ref.at[piece(n, block)], field.at[piece(n, block)])], blocks, given_semaphores
    )
    aheads = Stream(
        lambda n: [(ahead_ref.at[piece(n, block)], ahead.at[piece(n, block)])], blocks, semaphores.at[0]
    )
    backs = Stream(
        lambda n: [(back_ref.at[piece(n, block)], back.at[piece(n, block)])], blocks, semaphores.at[1]
    )
    out = Stream(
        lambda n: [(buffer.at[pl.ds(n * group, group)], out_ref.at[pl.ds(n * group, group)])],
        blocks,
        out_semaphores,
    )
    for n in range(blocks):
        given.start(n)
    aheads.begin()
    given.end()

    def strip(index, carry):
        own = piece(index, 64)
        high, low = halves(field[own, :])
        lines[own, :columns] = high
        lines[own, columns:] = low
        return carry

    lax.fori_loop(0, full // 64, strip, 0, unroll=4)

    def forth(n, carry):
        aheads.take(n)

        @pl.when(n == blocks - 1)
        def _():
            backs.begin()

        own = piece(n, block)
        result = jnp.dot(ahead[own, :], lines[...], preferred_element_type=jnp.float32)
        result = result[:, :columns] + result[:, columns:]
        high, low = halves(result / (along_ref[own, :] + other_ref[...]))
        spectral[own, :columns] = high
        spectral[own, columns:] = low
        return carry

    lax.fori_loop(0, blocks, forth, 0)

    def reverse(n, carry):
        backs.take(n)
        result = jnp.dot(back[piece(n, block), :], spectral[...], preferred_element_type=jnp.float32)
        result = result[:, :columns] + result[:, columns:]
        for part in range(group):
            buffer[n * group + part, :rows, :] = result[part * rows : (part + 1) * rows]
        return carry

    lax.fori_loop(0, blocks, reverse, 0)
    rest = aux_ref[2:, :]

    def close(n, carry):
        for part in range(group):
            own = n * group + part
            above = buffer[jnp.maximum(own - 1, 0), rows - 1 : rows, :]
            above = jnp.where(own > 0, above, 0.0)
            below = buffer[jnp.minimum(own + 1, devices - 1), 0:1, :]
            below = jnp.where(own + 1 < devices, below, 0.0)
            buffer[own, rows:, :] = jnp.concatenate([above, below, rest], axis=0)
        out.start(n)
        return carry

    lax.fori_loop(0, blocks, close, 0)
    out.end()


def column_lines(field, aux, basis_xt, basis_x, along, other, rows):
    full, columns = field.shape
    block = min(512, full)
    devices = full // rows
    return pl.pallas_call(
        functools.partial(column_kernel, rows, block),
        in_specs=[anywhere, vector, anywhere, anywhere, vector, vector],
        out_specs=anywhere,
        out_shape=jax.ShapeDtypeStruct((devices, rows + spare, columns), jnp.float32),
        scratch_shapes=[
            pltpu.VMEM((full, columns), jnp.float32),
            pltpu.VMEM((full, full), jnp.bfloat16),
            pltpu.VMEM((full, full), jnp.bfloat16),
            pltpu.VMEM((full, 2 * columns), jnp.bfloat16),
            pltpu.VMEM((full, 2 * columns), jnp.bfloat16),
            pltpu.VMEM((devices, rows + spare, columns), jnp.float32),
            pltpu.SemaphoreType.DMA((full // block, 1)),
            pltpu.SemaphoreType.DMA((2, full // block, 1)),
            pltpu.SemaphoreType.DMA((full // block, 1)),
        ],
        compiler_params=params(),
    )(field, aux, basis_xt, basis_x, along, other)


def turn_kernel(stage, last, block, chunks, *refs):
    refs = list(refs)
    take = lambda: refs.pop(0)
    mix_ref, got_ref, basis_ref = take(), take(), take()
    has_z = stage >= 1 or chunks > 1
    has_v = stage >= 2 or (stage >= 1 and chunks > 1)
    diagonal_ref, low_x, high_x, low_y, high_y = take(), take(), take(), take(), take()
    residual_ref = take() if last else None
    scalars_ref = take() if stage >= 1 else None
    if has_z:
        old_z, old_edge_z = take(), take()
    if has_v:
        old_v, old_edge_v = take(), take()
    z_ref, edge_z_ref, y_ref = take(), take(), take()
    aux_ref = take() if last else None
    if stage >= 1:
        v_ref, edge_v_ref = take(), take()
    if not last:
        out_ref = take()
    got, basis, diagonal, lines, around, edge_z, image = [take() for _ in range(7)]
    residual = take() if last else None
    z = take() if has_z else None
    if stage >= 1:
        v, edge_v = take(), take()
    if not last:
        ahead_lines, sent = take(), take()
    given_semaphores, semaphores, late_semaphores = take(), take(), take()
    if not last:
        basis_semaphores, out_semaphores = take(), take()
    planes, rows, full = diagonal.shape
    devices, _, columns = got.shape
    parts = devices // planes
    half = planes * (rows + spare)
    main = planes * rows
    blocks = full // block
    groups = [slice(m * parts, (m + 1) * parts) for m in range(planes)]
    given = start_all([(got_ref.at[group], got.at[group]) for group in groups], given_semaphores)
    width = full // chunks
    turned = slice(full - width, full)
    fields = [(residual_ref, residual)] if last else []
    if has_z:
        fields += [(old_z, z), (old_edge_z, edge_z)]
    if has_v:
        fields += [(old_v, v), (old_edge_v, edge_v)]

    def needed(n):
        own = piece(n, block)
        pairs = [(basis_ref.at[own, turned], basis.at[own, turned])]
        return pairs + [(old.at[:, :, own], target.at[:, :, own]) for old, target in fields]

    stream = Stream(needed, blocks, semaphores)
    stream.begin()
    wait_all(given)
    take_lines(got, lines, planes, rows)
    def fold(value):
        total = value[:, :columns]
        for left in range(columns, value.shape[1], columns):
            total = total + value[:, left : left + columns]
        return total

    def finish_block(n, carry):
        stream.take(n)
        lanes = piece(n, block)
        result = lax.dot_general(
            lines[...], basis[lanes, turned], (((1,), (1,)), ((), ())), preferred_element_type=jnp.float32
        )
        result = result[:half] + result[half:]
        if stage >= 1:
            length = scalars_ref[2:3, 0:1]
            turn = scalars_ref[3:4, 0:1]
        for k in range(planes):
            value, edge = mixed_back(result, mix_ref, k, rows)
            if chunks > 1:
                scale = 1.0 if stage == 0 else -length
                if stage >= 1:
                    v[k, :, lanes] = v[k, :, lanes] + value
                    edge_v[k, :, lanes] = edge_v[k, :, lanes] + edge
                value = z[k, :, lanes] + scale * value
                edge = edge_z[k, :, lanes] + scale * edge
            elif stage >= 1:
                if stage >= 2:
                    value = value + turn * v[k, :, lanes]
                    edge = edge + turn * edge_v[k, :, lanes]
                v[k, :, lanes] = value
                edge_v[k, :, lanes] = edge
                value = z[k, :, lanes] - length * value
                edge = edge_z[k, :, lanes] - length * edge
            edge_z[k, :, lanes] = edge
            if last:
                shared = fold(residual[k, :, lanes] * value)
                for start in range(0, rows, 8):
                    carry = carry + shared[start : start + 8]
            around[k, spare : spare + rows, lanes] = value
            around[k, spare - 1 : spare, lanes] = edge[0:1]
            around[k, spare + rows : spare + rows + 1, lanes] = edge[1:2]
        return carry

    diagonal_copy = pltpu.make_async_copy(diagonal_ref, diagonal, late_semaphores.at[0])
    diagonal_copy.start()
    nothing = jnp.zeros((8, columns), jnp.float32)
    product = lax.fori_loop(0, blocks, finish_block, nothing)
    done = [(around.at[:, spare : spare + rows], z_ref), (edge_z, edge_z_ref)]
    if stage >= 1:
        done += [(v, v_ref), (edge_v, edge_v_ref)]
    done = start_all(done, late_semaphores.at[2:6])
    ahead = None
    if not last and chunks > 1:
        ahead = column_stream(basis_ref, basis, block, 0, width // block, basis_semaphores)
        ahead.begin()
    diagonal_copy.wait()

    def operate(index, carry):
        k = index // (rows // 8)
        tile = index - k * (rows // 8)
        own = piece(tile, 8)
        window = around[k, pl.ds(pl.multiple_of(tile * 8, 8), 24), :]
        value = window[8:16]
        above = pltpu.roll(window, 1, 0)[8:16]
        below = pltpu.roll(window, 23, 0)[8:16]
        middle = pl.ds(pl.multiple_of(tile * 8 + spare, 8), 8)
        before = around[jnp.where(k == 0, planes - 1, k - 1), middle, :]
        after = around[jnp.where(k == planes - 1, 0, k + 1), middle, :]
        total = diagonal[k, own, :] * value
        total = total + (low_x[own, :] * (value - above) - high_x[own, :] * (below - value))
        left = pltpu.roll(value, 1, 1)
        right = pltpu.roll(value, full - 1, 1)
        total = total + (low_y[...] * (value - left) - high_y[...] * (right - value))
        total = total + (2.0 * value - before - after)
        image[k, own, :] = total
        return carry + fold(value * total) if last else carry

    bend = lax.fori_loop(0, planes * (rows // 8), operate, nothing, unroll=2)
    if last:
        product = jnp.sum(product, axis=0, keepdims=True)
        bend = jnp.sum(bend, axis=0, keepdims=True)
        aux_ref[...] = jnp.concatenate([nothing[:2], product, bend, nothing[4:]], axis=0)
    image_copy = pltpu.make_async_copy(image, y_ref, late_semaphores.at[1])
    image_copy.start()
    if not last:
        mix_planes(lambda k, i, j: image[k, i, j], mix_ref, ahead_lines, rows)
        send_lines(ahead_lines, basis, sent, out_ref, block, 0, out_semaphores, ahead)
    image_copy.wait()
    wait_all(done)


def turn_lines(stage, last, got, part, operator, basis_z, basis_y, state, chunks):
    planes, rows, full = operator[0].shape
    _, _, columns = got.shape
    block = min(512, full // chunks)
    blocks = full // block
    field_shape = jax.ShapeDtypeStruct((planes, rows, full), jnp.float32)
    edge_shape = jax.ShapeDtypeStruct((planes, spare, full), jnp.float32)
    before = part if chunks > 1 else state
    specs = [scalar] + [anywhere] * 3 + [vector] * 4
    given = [basis_z, got, basis_y] + list(operator)
    if last:
        specs.append(anywhere)
        given.append(state["residual"])
    if stage >= 1:
        specs.append(vector)
        given.append(state["scalars"])
    for name in ("z", "v"):
        if name in before:
            specs += [anywhere] * 2
            given += [before[name], before["edge_" + name]]
    names = ["z", "edge_z", "y"]
    outs = [anywhere] * 3
    shapes = [field_shape, edge_shape, field_shape]
    if last:
        names.append("aux")
        outs.append(vector)
        shapes.append(jax.ShapeDtypeStruct((spare, columns), jnp.float32))
    if stage >= 1:
        names += ["v", "edge_v"]
        outs += [anywhere, anywhere]
        shapes += [field_shape, edge_shape]
    field = pltpu.VMEM((planes, rows, full), jnp.float32)
    edge = pltpu.VMEM((planes, spare, full), jnp.float32)
    scratch = [
        pltpu.VMEM(got.shape, jnp.float32),
        pltpu.VMEM(basis_y.shape, jnp.bfloat16),
        field,
        pltpu.VMEM((2 * planes * (rows + spare), full // chunks), jnp.bfloat16),
        pltpu.VMEM((planes, rows + 2 * spare, full), jnp.float32),
        edge,
        field,
    ]
    if last:
        scratch.append(field)
    if "z" in before:
        scratch.append(field)
    if stage >= 1:
        scratch += [field, edge]
    if not last:
        sent = (planes, full // chunks // columns, rows, columns)
        names.append("sent")
        outs.append(anywhere)
        shapes.append(jax.ShapeDtypeStruct(sent, jnp.float32))
        scratch += [pltpu.VMEM((2 * planes * rows, full), jnp.bfloat16), pltpu.VMEM(sent, jnp.float32)]
    scratch += [
        pltpu.SemaphoreType.DMA((planes,)),
        pltpu.SemaphoreType.DMA((blocks, 6)),
        pltpu.SemaphoreType.DMA((6,)),
    ]
    if not last:
        scratch += [pltpu.SemaphoreType.DMA((blocks // chunks, 1))] * 2
    results = pl.pallas_call(
        functools.partial(turn_kernel, stage, last, block, chunks),
        in_specs=specs,
        out_specs=outs,
        out_shape=shapes,
        scratch_shapes=scratch,
        compiler_params=params(),
    )(*given)
    return dict(zip(names, results))


def first_kernel(
    rows, velocity_ref, weight_ref, code_ref, above_ref, below_ref, side_ref, half_x_ref, half_y_ref,
    source_ref, predicted_ref, fields, moved, kept, semaphores,
):
    planes, count, span = weight_ref.shape
    wide = half_y_ref.shape[1]
    pad = 16
    copies = []
    for channel in range(5):
        if channel < 3:
            main = velocity_ref.at[channel]
        else:
            main = weight_ref if channel == 3 else code_ref
        target = fields.at[channel]
        copies.append((main, target.at[:, pad : pad + count, :span]))
        copies.append((above_ref.at[channel], target.at[:, pad - 8 : pad, :span]))
        copies.append((below_ref.at[channel], target.at[:, pad + count : pad + count + 8, :span]))
        copies.append((side_ref.at[channel], target.at[:, :, span:]))
    copies = [
        pltpu.make_async_copy(given, target, semaphores.at[index])
        for index, (given, target) in enumerate(copies)
    ]
    for copy in copies:
        copy.start()
    for copy in copies:
        copy.wait()
    tiles = count // 8 + 2
    half_y = half_y_ref[...]

    def lane_slope(value):
        return pltpu.roll(value, wide - 1, 1) - pltpu.roll(value, 1, 1)

    def advance(index, carry):
        k = index // tiles
        start = pl.multiple_of(8 + (index - k * tiles) * 8, 8)
        window = pl.ds(pl.multiple_of(start - 8, 8), 24)
        own = pl.ds(start, 8)
        before = jnp.where(k == 0, planes - 1, k - 1)
        after = jnp.where(k == planes - 1, 0, k + 1)
        half_x = half_x_ref[own, :]
        first = fields[0, k, window, :]
        second = fields[1, k, own, :]
        third_before = fields[2, before, own, :]
        third_after = fields[2, after, own, :]
        weight = fields[3, k, own, :]
        for c in range(3):
            value = first if c == 0 else fields[c, k, window, :]
            along = first * value
            center = value[8:16]
            total = half_x * (pltpu.roll(along, 23, 0)[8:16] - pltpu.roll(along, 1, 0)[8:16])
            total = total + half_y * lane_slope(second * center)
            total = total + 0.5 * (third_after * fields[c, after, own, :] - third_before * fields[c, before, own, :])
            share = weight * total
            moved[c, k, own, :] = share
            kept[c, k, own, :] = total - share
        return carry

    lax.fori_loop(0, planes * tiles, advance, 0, unroll=4)

    def settle(index, carry):
        k = index // tiles
        start = pl.multiple_of(8 + (index - k * tiles) * 8, 8)
        window = pl.ds(pl.multiple_of(start - 8, 8), 24)
        own = pl.ds(start, 8)
        code = fields[4, k, window, :]
        inside_x = half_x_ref[own, :] > 0.0
        inside_y = half_y > 0.0
        for c in range(3):
            share = moved[c, k, window, :]
            received = pltpu.roll(jnp.where(code == 1.0, share, 0.0), 1, 0)[8:16] + pltpu.roll(jnp.where(code == 2.0, share, 0.0), 23, 0)[8:16]
            center = share[8:16]
            middle = code[8:16]
            received = received + pltpu.roll(jnp.where(middle == 3.0, center, 0.0), 1, 1)
            received = received + pltpu.roll(jnp.where(middle == 4.0, center, 0.0), wide - 1, 1)
            result = fields[c, k, own, :] - time_step * (kept[c, k, own, :] + received)
            if c == 0:
                result = jnp.where(inside_x, result, 0.0)
            if c == 1:
                result = jnp.where(inside_y, result, 0.0)
            kept[c, k, own, :] = result
        return carry

    lax.fori_loop(0, planes * tiles, settle, 0, unroll=4)
    inner = count // 8
    group = rows // 8

    def collect(index, carry):
        k = index // inner
        tile = index - k * inner
        start = pl.multiple_of(pad + tile * 8, 8)
        window = pl.ds(pl.multiple_of(start - 8, 8), 24)
        own = pl.ds(start, 8)
        before = jnp.where(k == 0, planes - 1, k - 1)
        after = jnp.where(k == planes - 1, 0, k + 1)
        first = kept[0, k, window, :]
        second = kept[1, k, own, :]
        total = half_x_ref[own, :] * (pltpu.roll(first, 23, 0)[8:16] - pltpu.roll(first, 1, 0)[8:16])
        total = total + half_y * lane_slope(second)
        total = total + 0.5 * (kept[2, after, own, :] - kept[2, before, own, :])
        target = tile // group
        spot = pl.multiple_of((tile - target * group) * 8, 8)
        source_ref[target, k, pl.ds(spot, 8), :] = -total[:, :span]
        out = pl.ds(pl.multiple_of(tile * 8, 8), 8)
        predicted_ref[0, k, out, :] = first[8:16, :span]
        predicted_ref[1, k, out, :] = second[:, :span]
        predicted_ref[2, k, out, :] = kept[2, k, own, :span]
        return carry

    lax.fori_loop(0, planes * inner, collect, 0, unroll=8)


def first_step(velocity, weight, code, above, below, side, half_x, half_y, rows):
    planes, count, span = weight.shape
    tall, wide = half_x.shape[0], half_y.shape[1]
    return pl.pallas_call(
        functools.partial(first_kernel, rows),
        in_specs=[anywhere] * 6 + [vector] * 2,
        out_specs=[vector] * 2,
        out_shape=[
            jax.ShapeDtypeStruct((count // rows, planes, rows, span), jnp.float32),
            jax.ShapeDtypeStruct((3, planes, count, span), jnp.float32),
        ],
        scratch_shapes=[
            pltpu.VMEM((5, planes, tall, wide), jnp.float32),
            pltpu.VMEM((3, planes, tall, wide), jnp.float32),
            pltpu.VMEM((3, planes, tall, wide), jnp.float32),
            pltpu.SemaphoreType.DMA((20,)),
        ],
        compiler_params=params(),
    )(velocity, weight, code, above, below, side, half_x, half_y)


def neighbours(axis, last, leading):
    size = lax.axis_size(axis)
    up = [(i, i + 1) for i in range(size - 1)]
    down = [(i + 1, i) for i in range(size - 1)]
    return lax.ppermute(last, axis, up), lax.ppermute(leading, axis, down)


def extended_1(value, start, count, before, after):
    padded = jnp.pad(value, (before, after))
    return lax.dynamic_slice_in_dim(padded, start, count + before + after)


def lanes_sum(value, columns):
    return jnp.sum(value.reshape(-1, value.shape[-1] // columns, columns), axis=(0, 1))


def add_kernel(numbers_ref, sums_ref, pressure_ref, direction_ref, lifted_ref, out_ref):
    total = jnp.sum(jnp.sum(sums_ref[...], axis=0), axis=1, keepdims=True)
    turn = total[2:3] / numbers_ref[0:1, 0:1]
    length = total[2:3] / (total[3:4] - turn * turn * numbers_ref[1:2, 0:1])
    for k in range(pressure_ref.shape[0]):
        direction = lifted_ref[k] + turn * direction_ref[k]
        out_ref[0, k] = pressure_ref[k] + length * direction


def add_step(numbers, sums, pressure, direction, lifted, pieces):
    planes, rows, full = pressure.shape
    span = full // pieces
    field = pl.BlockSpec((planes, rows, span), lambda n: (0, 0, n))
    return pl.pallas_call(
        add_kernel,
        grid=(pieces,),
        in_specs=[vector] * 2 + [field] * 3,
        out_specs=pl.BlockSpec((1, planes, rows, span), lambda n: (n, 0, 0, 0)),
        out_shape=jax.ShapeDtypeStruct((pieces, planes, rows, span), jnp.float32),
        compiler_params=params(),
    )(numbers, sums, pressure, direction, lifted)


def correct_kernel(
    predicted_ref, own_ref, previous_ref, next_ref, above_ref, below_ref, left_ref, right_ref,
    half_x_ref, half_y_ref, corrected_ref, pressure_ref,
):
    n = pl.program_id(0)
    last = pl.num_programs(0) - 1
    _, planes, rows, _ = own_ref.shape
    for k in range(planes):
        value = own_ref[0, k]
        above = jnp.where(n == 0, above_ref[k], previous_ref[0, k, rows - 1 : rows, :])
        below = jnp.where(n == last, below_ref[k], next_ref[0, k, 0:1, :])
        rising = jnp.concatenate([value[1:], below], axis=0) - jnp.concatenate([above, value[:-1]], axis=0)
        ahead = jnp.concatenate([value[:, 1:], right_ref[0, k]], axis=1)
        behind = jnp.concatenate([left_ref[0, k], value[:, :-1]], axis=1)
        across = own_ref[0, (k + 1) % planes] - own_ref[0, (k - 1) % planes]
        pressure_ref[:, k, :] = value
        corrected_ref[0, :, k, :] = predicted_ref[0, k] - half_x_ref[...] * rising
        corrected_ref[1, :, k, :] = predicted_ref[1, k] - half_y_ref[...] * (ahead - behind)
        corrected_ref[2, :, k, :] = predicted_ref[2, k] - 0.5 * across


def correct_step(predicted, pressure, above, below, left, right, half_x, half_y):
    pieces, planes, rows, span = pressure.shape
    count = pieces * rows
    own = lambda shift: pl.BlockSpec(
        (1, planes, rows, span), lambda n: (jnp.clip(n + shift, 0, pieces - 1), 0, 0, 0)
    )
    column = pl.BlockSpec((1, planes, rows, 1), lambda n: (n, 0, 0, 0))
    return pl.pallas_call(
        correct_kernel,
        grid=(pieces,),
        in_specs=[
            pl.BlockSpec((3, planes, rows, span), lambda n: (0, 0, n, 0)),
            own(0),
            own(-1),
            own(1),
            vector,
            vector,
            column,
            column,
            pl.BlockSpec((rows, 1), lambda n: (n, 0)),
            vector,
        ],
        out_specs=[
            pl.BlockSpec((3, rows, planes, span), lambda n: (0, n, 0, 0)),
            pl.BlockSpec((rows, planes, span), lambda n: (n, 0, 0)),
        ],
        out_shape=[
            jax.ShapeDtypeStruct((3, count, planes, span), jnp.float32),
            jax.ShapeDtypeStruct((count, planes, span), jnp.float32),
        ],
        compiler_params=params(),
    )(predicted, pressure, pressure, pressure, above, below, left, right, half_x, half_y)


def per_device(
    velocity,
    cut_flags,
    redirect,
    share_weight,
    inverse_dx,
    inverse_dy,
    basis_x,
    basis_y,
    basis_z,
    eigen_x,
    eigen_y,
    eigen_z,
):
    x_parts = lax.axis_size("gx")
    y_parts = lax.axis_size("gy")
    devices = x_parts * y_parts
    x_index = lax.axis_index("gx")
    y_index = lax.axis_index("gy")
    own = x_index * y_parts + y_index
    x_count, planes, y_count = velocity.shape[1:]
    full_x = x_count * x_parts
    full_y = y_count * y_parts
    rows = full_x // devices
    columns = planes * full_y // devices
    chunks = 2 if columns % 256 == 0 else 1
    columns = columns // chunks
    column_blocks = devices // planes
    inverse_x = lax.dynamic_slice_in_dim(inverse_dx, x_index * x_count, x_count)
    inverse_y = lax.dynamic_slice_in_dim(inverse_dy, y_index * y_count, y_count)
    flags = cut_flags.astype(jnp.float32)
    code = (cut_flags * (redirect + 1)).astype(jnp.float32)
    weight = share_weight * flags
    reach = 3

    def edge_rows(part):
        cut = cut_flags[part]
        share = share_weight[part] * cut.astype(jnp.float32)
        target = (cut * (redirect[part] + 1)).astype(jnp.float32)
        return jnp.concatenate([velocity[:, part], share[None], target[None]])

    above, below = neighbours("gx", edge_rows(slice(x_count - reach, None)), edge_rows(slice(0, reach)))
    velocity = velocity.transpose(0, 2, 1, 3)
    weight = weight.transpose(1, 0, 2)
    code = code.transpose(1, 0, 2)
    above = above.transpose(0, 2, 1, 3)
    below = below.transpose(0, 2, 1, 3)

    def edge_columns(part):
        middle = jnp.concatenate([velocity[..., part], weight[None, ..., part], code[None, ..., part]])
        return jnp.concatenate([above[..., part], middle, below[..., part]], axis=2).swapaxes(2, 3)

    left, right = neighbours("gy", edge_columns(slice(y_count - reach, None)), edge_columns(slice(0, reach)))
    side = jnp.concatenate([right, jnp.zeros((5, planes, 128 - 2 * reach, x_count + 2 * reach), jnp.float32), left], axis=2)
    side = jnp.pad(side.swapaxes(2, 3), ((0, 0), (0, 0), (16 - reach, 16 - reach), (0, 0)))
    above = jnp.pad(above, ((0, 0), (0, 0), (8 - reach, 0), (0, 0)))
    below = jnp.pad(below, ((0, 0), (0, 0), (0, 8 - reach), (0, 0)))
    half_x = 0.5 * extended_1(inverse_dx, x_index * x_count, x_count, 16, 16)[:, None]
    half_y = 0.5 * extended_1(inverse_dy, y_index * y_count, y_count, reach, reach)
    half_y = jnp.concatenate([half_y[reach:], jnp.zeros((128 - 2 * reach,), jnp.float32), half_y[:reach]])[None]
    source, predicted = first_step(velocity, weight, code, above, below, side, half_x, half_y, rows)
    diagonal = (cell_shift + cut_shift * flags).reshape(y_parts, rows, planes, y_count).transpose(0, 2, 1, 3)
    diagonal = lax.all_to_all(diagonal, "gy", 0, 0, tiled=True)
    source, diagonal = lax.optimization_barrier((source, diagonal))
    source = lax.all_to_all(source, "gy", 0, 0, tiled=True)
    source, basis_xt = lax.optimization_barrier((source, basis_x.T))
    diagonal = diagonal.transpose(1, 2, 0, 3).reshape(planes, rows, full_y)
    whole_x = jnp.pad(inverse_dx, 1)
    face_x = lax.dynamic_slice_in_dim(whole_x[:-1] * whole_x[1:], own * rows, rows + 1)
    whole_y = jnp.pad(inverse_dy, 1)
    face_y = whole_y[:-1] * whole_y[1:]
    operator = (diagonal, face_x[:-1, None], face_x[1:, None], face_y[None, :-1], face_y[None, 1:])
    along = eigen_x[:, None]
    other = [
        (
            lax.dynamic_slice_in_dim(
                eigen_y, full_y // chunks * chunk + (own % column_blocks) * columns, columns
            )
            + lax.dynamic_slice_in_dim(eigen_z, own // column_blocks, 1)
        )[None]
        for chunk in range(chunks)
    ]

    def apply(stage, field, sent, aux, state):
        sents = [sent] + [
            more_lines(field, basis_z, basis_y, columns, chunks, chunk) for chunk in range(1, chunks)
        ]
        gots = []
        for chunk, sent in enumerate(sents):
            sent = sent.reshape(devices, rows, columns)
            got = lax.all_to_all(sent, both, 0, 0, tiled=True).reshape(full_x, columns)
            given = aux if chunk == 0 else jnp.zeros((spare, columns), jnp.float32)
            got = column_lines(got, given, basis_xt, basis_x, along, other[chunk], rows)
            gots.append(lax.all_to_all(got, both, 0, 0, tiled=True))
        if stage > 0:
            state["scalars"] = numbers_of(gots[0][:, rows:], state.get("scalars"))
        part = None
        if chunks > 1:
            part = part_lines(stage, gots[0], basis_z, basis_y, rows, chunks, state)
        return gots[-1], part

    def numbers_of(sums, numbers):
        product = jnp.sum(sums[:, 2])
        bend = jnp.sum(sums[:, 3])
        turn = jnp.zeros_like(product)
        if numbers is not None:
            turn = product / numbers[0, 0]
            bend = bend - turn * turn * numbers[1, 0]
        numbers = jnp.stack([product, bend, product / bend, turn])
        return jnp.broadcast_to(jnp.pad(numbers, (0, 4))[:, None], (8, 128))

    residual, sent = start_lines(source, basis_z, basis_y, columns, chunks)
    state = {}
    got, part = apply(0, residual, sent, jnp.zeros((spare, columns), jnp.float32), state)
    state |= turn_lines(0, False, got, part, operator, basis_z, basis_y, state, chunks)
    for stage in range(1, ITERS):
        partial = [lanes_sum(residual * state["z"], columns), lanes_sum(state["z"] * state["y"], columns)]
        aux = jnp.pad(jnp.stack(partial), ((2, spare - 4), (0, 0)))
        got, part = apply(stage, state["y"], state["sent"], aux, state)
        length, turn = state["scalars"][2, 0], state["scalars"][3, 0]
        if stage == 1:
            direction, image = state["z"], state["y"]
            pressure = length * direction
        else:
            direction = state["z"] + turn * direction
            image = state["y"] + turn * image
            pressure = pressure + length * direction
        residual = residual - length * image
        state["residual"] = residual
        last = stage + 1 == ITERS
        state |= turn_lines(stage, last, got, part, operator, basis_z, basis_y, state, chunks)
    sums = jnp.broadcast_to(state["aux"][None], (devices, spare, columns))
    sums = lax.all_to_all(sums, both, 0, 0, tiled=True)
    pressure = add_step(state["scalars"], sums, pressure, direction, state["z"], y_parts)
    pressure = lax.all_to_all(pressure, "gy", 0, 0, tiled=True)
    above, below = neighbours("gx", pressure[-1, :, -1:], pressure[0, :, :1])
    left, right = neighbours("gy", pressure[..., -1], pressure[..., 0])
    half_x = 0.5 * inverse_x[:, None]
    half_y = 0.5 * inverse_y[None]
    corrected, pressure = correct_step(
        predicted, pressure, above, below, left[..., None], right[..., None], half_x, half_y
    )
    return corrected, pressure


def solution(mesh):
    in_specs = (
        P(None, "gx", None, "gy"),
        P("gx", None, "gy"),
        P("gx", None, "gy"),
        P("gx", None, "gy"),
        P(),
        P(),
        P(),
        P(),
        P(),
        P(),
        P(),
        P(),
    )
    out_specs = (P(None, "gx", None, "gy"), P("gx", None, "gy"))
    return jax.shard_map(
        per_device, mesh=mesh, in_specs=in_specs, out_specs=out_specs, check_vma=False
    )
```

```python
import functools

import jax
import jax.numpy as jnp
from jax import lax
from jax.experimental import pallas as pl
from jax.experimental.pallas import tpu as pltpu
from jax.sharding import PartitionSpec as P

ITERS = 4


time_step = 0.25
cell_shift = 0.05
cut_shift = 0.45
both = ("gx", "gy")
spare = 8


def halves(value):
    high = value.astype(jnp.bfloat16)
    low = (value - high.astype(jnp.float32)).astype(jnp.bfloat16)
    return high, low


def params(mebibytes):
    return pltpu.CompilerParams(vmem_limit_bytes=mebibytes * 1024 * 1024)


def mix_planes(read, mix_ref, lines, rows):
    planes = mix_ref.shape[0]
    width = lines.shape[1]
    lane = 512 if width % 512 == 0 else width
    half = planes * rows

    def strip(index, carry):
        start = pl.multiple_of(index * 16, 16)
        for left in range(0, width, lane):
            fields = [read(k, pl.ds(start, 16), pl.ds(left, lane)) for k in range(planes)]
            for m in range(planes):
                total = fields[0] * mix_ref[0, m]
                for k in range(1, planes):
                    total = total + fields[k] * mix_ref[k, m]
                high, low = halves(total)
                lines[pl.ds(m * rows + start, 16), pl.ds(left, lane)] = high
                lines[pl.ds(half + m * rows + start, 16), pl.ds(left, lane)] = low
        return carry

    lax.fori_loop(0, rows // 16, strip, 0)


anywhere = pl.BlockSpec(memory_space=pl.ANY)
vector = pl.BlockSpec(memory_space=pltpu.VMEM)
scalar = pl.BlockSpec(memory_space=pltpu.SMEM)


class Stream:
    def __init__(self, pairs, count, semaphores):
        self.pairs = pairs
        self.count = count
        self.semaphores = semaphores

    def copies(self, n):
        pairs = self.pairs(n)
        return [
            pltpu.make_async_copy(given, target, self.semaphores.at[n, index])
            for index, (given, target) in enumerate(pairs)
        ]

    def start(self, n):
        for copy in self.copies(n):
            copy.start()

    def begin(self):
        for n in range(min(2, self.count)):
            self.start(n)

    def take(self, n):
        for copy in self.copies(n):
            copy.wait()

        @pl.when(n + 2 < self.count)
        def _():
            self.start(n + 2)

    def end(self):
        def step(n, carry):
            for copy in self.copies(n):
                copy.wait()
            return carry

        lax.fori_loop(0, self.count, step, 0)


def start_all(pairs, semaphores):
    copies = [
        pltpu.make_async_copy(given, target, semaphores.at[index])
        for index, (given, target) in enumerate(pairs)
    ]
    for copy in copies:
        copy.start()
    return copies


def wait_all(copies):
    for copy in copies:
        copy.wait()


def far(*values):
    return [pltpu.with_memory_space_constraint(value, pltpu.HBM) for value in values]


def piece(index, size):
    return pl.ds(pl.multiple_of(index * size, size), size)


def send_lines(lines, basis, sent, out_ref, block, chunk, semaphores, stream=None):
    planes, all_parts, rows, columns = sent.shape
    half = planes * rows
    parts = block // columns
    blocks = all_parts // parts
    out = Stream(
        lambda n: [(sent.at[:, pl.ds(n * parts, parts)], out_ref.at[:, pl.ds(n * parts, parts)])],
        blocks,
        semaphores,
    )

    def step(n, carry):
        if stream is not None:
            stream.take(n)
        result = jnp.dot(lines[...], basis[:, piece(chunk * blocks + n, block)], preferred_element_type=jnp.float32)
        result = result[:half] + result[half:]
        for m in range(planes):
            for part in range(parts):
                sent[m, n * parts + part] = result[
                    m * rows : (m + 1) * rows, part * columns : (part + 1) * columns
                ]
        out.start(n)
        return carry

    lax.fori_loop(0, blocks, step, 0)
    out.end()


def column_stream(basis_ref, basis, block, chunk, blocks, semaphores):
    def pairs(n):
        own = piece(chunk * blocks + n, block)
        return [(basis_ref.at[:, own], basis.at[:, own])]

    return Stream(pairs, blocks, semaphores)


def start_kernel(
    block, mix_ref, field_ref, basis_ref, kept_ref, out_ref,
    field, basis, lines, sent, semaphores, basis_semaphores, out_semaphores,
):
    pieces, planes, rows, span = field_ref.shape
    given = [(field_ref.at[n], field.at[:, :, n * span : (n + 1) * span]) for n in range(pieces)]
    given = start_all(given, semaphores)
    stream = column_stream(basis_ref, basis, block, 0, basis_semaphores.shape[0], basis_semaphores)
    stream.begin()
    wait_all(given)
    kept = pltpu.make_async_copy(field, kept_ref, semaphores.at[pieces])
    kept.start()
    mix_planes(lambda k, i, j: field[k, i, j], mix_ref, lines, rows)
    send_lines(lines, basis, sent, out_ref, block, 0, out_semaphores, stream)
    kept.wait()


def start_lines(field, basis_z, basis_y, columns, chunks):
    pieces, planes, rows, span = field.shape
    full = pieces * span
    block = min(256, full // chunks)
    blocks = full // chunks // block
    sent = (planes, full // chunks // columns, rows, columns)
    return pl.pallas_call(
        functools.partial(start_kernel, block),
        in_specs=[scalar, vector, anywhere],
        out_specs=[anywhere] * 2,
        out_shape=[
            pltpu.HBM((planes, rows, full), jnp.float32),
            pltpu.HBM(sent, jnp.float32),
        ],
        scratch_shapes=[
            pltpu.VMEM((planes, rows, full), jnp.float32),
            pltpu.VMEM(basis_y.shape, jnp.bfloat16),
            pltpu.VMEM((2 * planes * rows, full), jnp.bfloat16),
            pltpu.VMEM(sent, jnp.float32),
            pltpu.SemaphoreType.DMA((pieces + 1,)),
            pltpu.SemaphoreType.DMA((blocks, 1)),
            pltpu.SemaphoreType.DMA((blocks, 1)),
        ],
        compiler_params=params(24),
    )(basis_z, field, *far(basis_y))


def more_kernel(
    block, chunk, mix_ref, field_ref, basis_ref, out_ref, field, basis, lines, sent, semaphore, basis_semaphores, out_semaphores
):
    given = pltpu.make_async_copy(field_ref, field, semaphore)
    given.start()
    stream = column_stream(basis_ref, basis, block, chunk, basis_semaphores.shape[0], basis_semaphores)
    stream.begin()
    given.wait()
    mix_planes(lambda k, i, j: field[k, i, j], mix_ref, lines, field.shape[1])
    send_lines(lines, basis, sent, out_ref, block, chunk, out_semaphores, stream)


def more_lines(field, basis_z, basis_y, columns, chunks, chunk):
    planes, rows, full = field.shape
    block = min(256, full // chunks)
    blocks = full // chunks // block
    sent = (planes, full // chunks // columns, rows, columns)
    return pl.pallas_call(
        functools.partial(more_kernel, block, chunk),
        in_specs=[scalar, anywhere, anywhere],
        out_specs=anywhere,
        out_shape=pltpu.HBM(sent, jnp.float32),
        scratch_shapes=[
            pltpu.VMEM(field.shape, jnp.float32),
            pltpu.VMEM(basis_y.shape, jnp.bfloat16),
            pltpu.VMEM((2 * planes * rows, full), jnp.bfloat16),
            pltpu.VMEM(sent, jnp.float32),
            pltpu.SemaphoreType.DMA,
            pltpu.SemaphoreType.DMA((blocks, 1)),
            pltpu.SemaphoreType.DMA((blocks, 1)),
        ],
        compiler_params=params(24),
    )(basis_z, *far(field, basis_y))


def take_lines(got, lines, planes, rows):
    devices, _, columns = got.shape
    parts = devices // planes
    half = planes * (rows + spare)
    main = planes * rows
    edge_rows = lax.broadcasted_iota(jnp.int32, (spare, columns), 0) < 2
    for part in range(parts):
        lanes = slice(part * columns, (part + 1) * columns)
        edges = []
        for m in range(planes):
            high, low = halves(got[m * parts + part, :rows, :])
            lines[m * rows : (m + 1) * rows, lanes] = high
            lines[half + m * rows : half + (m + 1) * rows, lanes] = low
            edges.append(jnp.where(edge_rows, got[m * parts + part, rows:, :], 0.0))
        high, low = halves(jnp.concatenate(edges, axis=0))
        lines[main:half, lanes] = high
        lines[half + main :, lanes] = low


def mixed_back(result, mix_ref, k, rows):
    planes = mix_ref.shape[0]
    main = planes * rows
    value = result[:rows] * mix_ref[k, 0]
    edge = result[main : main + spare] * mix_ref[k, 0]
    for m in range(1, planes):
        value = value + result[m * rows : (m + 1) * rows] * mix_ref[k, m]
        edge = edge + result[main + m * spare : main + (m + 1) * spare] * mix_ref[k, m]
    return value, edge


def part_kernel(stage, rows, block, *refs):
    refs = list(refs)
    take = lambda: refs.pop(0)
    mix_ref, got_ref, basis_ref = take(), take(), take()
    if stage >= 1:
        scalars_ref, old_z, old_edge_z = take(), take(), take()
    if stage >= 2:
        old_v, old_edge_v = take(), take()
    out_refs = [take() for _ in range(4 if stage >= 1 else 2)]
    got, basis, lines = take(), take(), take()
    outs = [take() for _ in range(4 if stage >= 1 else 2)]
    given_semaphores, semaphores, out_semaphores = take(), take(), take()
    z, edge_z = outs[:2]
    planes = mix_ref.shape[0]
    parts = got.shape[0] // planes
    width = lines.shape[1]
    half = planes * (rows + spare)
    blocks = basis.shape[0] // block
    groups = [slice(m * parts, (m + 1) * parts) for m in range(planes)]
    given = start_all([(got_ref.at[group], got.at[group]) for group in groups], given_semaphores)
    fields = []
    if stage >= 1:
        v, edge_v = outs[2:]
        fields += [(old_z, z), (old_edge_z, edge_z)]
    if stage >= 2:
        fields += [(old_v, v), (old_edge_v, edge_v)]

    def needed(n):
        own = piece(n, block)
        pairs = [(basis_ref.at[own, :width], basis.at[own])]
        return pairs + [(old.at[:, :, own], target.at[:, :, own]) for old, target in fields]

    def made(n):
        own = piece(n, block)
        return [(out.at[:, :, own], out_ref.at[:, :, own]) for out, out_ref in zip(outs, out_refs)]

    stream = Stream(needed, blocks, semaphores)
    sink = Stream(made, blocks, out_semaphores)
    stream.begin()
    wait_all(given)
    take_lines(got, lines, planes, rows)

    def step(n, carry):
        stream.take(n)
        lanes = piece(n, block)
        result = lax.dot_general(
            lines[...], basis[lanes, :], (((1,), (1,)), ((), ())), preferred_element_type=jnp.float32
        )
        result = result[:half] + result[half:]
        if stage >= 1:
            length = scalars_ref[2:3, 0:1]
            turn = scalars_ref[3:4, 0:1]
        for k in range(planes):
            value, edge = mixed_back(result, mix_ref, k, rows)
            if stage >= 1:
                if stage >= 2:
                    value = value + turn * v[k, :, lanes]
                    edge = edge + turn * edge_v[k, :, lanes]
                v[k, :, lanes] = value
                edge_v[k, :, lanes] = edge
                value = z[k, :, lanes] - length * value
                edge = edge_z[k, :, lanes] - length * edge
            z[k, :, lanes] = value
            edge_z[k, :, lanes] = edge
        sink.start(n)
        return carry

    lax.fori_loop(0, blocks, step, 0)
    sink.end()


def part_lines(stage, got, basis_z, basis_y, rows, chunks, state):
    planes = basis_z.shape[0]
    full = basis_y.shape[0]
    block = min(256, full)
    half = planes * (rows + spare)
    field, edge = (planes, rows, full), (planes, spare, full)
    names = ["z", "edge_z"]
    given = [basis_z, got, *far(basis_y)]
    specs = [scalar, vector, anywhere]
    if stage >= 1:
        names += ["v", "edge_v"]
        given += [state["scalars"], *far(state["z"], state["edge_z"])]
        specs += [vector, anywhere, anywhere]
    if stage >= 2:
        given += far(state["v"], state["edge_v"])
        specs += [anywhere, anywhere]
    shapes = [field, edge] * (len(names) // 2)
    results = pl.pallas_call(
        functools.partial(part_kernel, stage, rows, block),
        in_specs=specs,
        out_specs=[anywhere] * len(names),
        out_shape=[pltpu.HBM(shape, jnp.float32) for shape in shapes],
        scratch_shapes=[
            pltpu.VMEM(got.shape, jnp.float32),
            pltpu.VMEM((full, full // chunks), jnp.bfloat16),
            pltpu.VMEM((2 * half, full // chunks), jnp.bfloat16),
        ]
        + [pltpu.VMEM(shape, jnp.float32) for shape in shapes]
        + [
            pltpu.SemaphoreType.DMA((planes,)),
            pltpu.SemaphoreType.DMA((full // block, 5)),
            pltpu.SemaphoreType.DMA((full // block, 4)),
        ],
        compiler_params=params(28),
    )(*given)
    return dict(zip(names, results))


def column_kernel(
    rows, block, field_ref, aux_ref, ahead_ref, back_ref, along_ref, other_ref, out_ref,
    field, ahead, back, lines, spectral, buffer, given_semaphores, semaphores, out_semaphores,
):
    full, columns = field_ref.shape
    blocks = full // block
    group = block // rows
    devices = full // rows
    given = Stream(
        lambda n: [(field_ref.at[piece(n, block)], field.at[piece(n, block)])], blocks, given_semaphores
    )
    aheads = Stream(
        lambda n: [(ahead_ref.at[piece(n, block)], ahead.at[piece(n, block)])], blocks, semaphores.at[0]
    )
    backs = Stream(
        lambda n: [(back_ref.at[piece(n, block)], back.at[piece(n, block)])], blocks, semaphores.at[1]
    )
    out = Stream(
        lambda n: [(buffer.at[pl.ds(n * group, group)], out_ref.at[pl.ds(n * group, group)])],
        blocks,
        out_semaphores,
    )
    for n in range(blocks):
        given.start(n)
    aheads.begin()
    given.end()

    def strip(index, carry):
        own = piece(index, 64)
        high, low = halves(field[own, :])
        lines[own, :columns] = high
        lines[own, columns:] = low
        return carry

    lax.fori_loop(0, full // 64, strip, 0, unroll=4)

    def forth(n, carry):
        aheads.take(n)

        @pl.when(n == blocks - 1)
        def _():
            backs.begin()

        own = piece(n, block)
        result = jnp.dot(ahead[own, :], lines[...], preferred_element_type=jnp.float32)
        result = result[:, :columns] + result[:, columns:]
        high, low = halves(result / (along_ref[own, :] + other_ref[...]))
        spectral[own, :columns] = high
        spectral[own, columns:] = low
        return carry

    lax.fori_loop(0, blocks, forth, 0)

    def reverse(n, carry):
        backs.take(n)
        result = jnp.dot(back[piece(n, block), :], spectral[...], preferred_element_type=jnp.float32)
        result = result[:, :columns] + result[:, columns:]
        for part in range(group):
            buffer[n * group + part, :rows, :] = result[part * rows : (part + 1) * rows]
        return carry

    lax.fori_loop(0, blocks, reverse, 0)
    rest = aux_ref[2:, :]

    def close(n, carry):
        for part in range(group):
            own = n * group + part
            above = buffer[jnp.maximum(own - 1, 0), rows - 1 : rows, :]
            above = jnp.where(own > 0, above, 0.0)
            below = buffer[jnp.minimum(own + 1, devices - 1), 0:1, :]
            below = jnp.where(own + 1 < devices, below, 0.0)
            buffer[own, rows:, :] = jnp.concatenate([above, below, rest], axis=0)
        out.start(n)
        return carry

    lax.fori_loop(0, blocks, close, 0)
    out.end()


def column_lines(field, aux, basis_xt, basis_x, along, other, rows):
    full, columns = field.shape
    block = min(512, full)
    devices = full // rows
    return pl.pallas_call(
        functools.partial(column_kernel, rows, block),
        in_specs=[vector, vector, anywhere, anywhere, vector, vector],
        out_specs=anywhere,
        out_shape=pltpu.HBM((devices, rows + spare, columns), jnp.float32),
        scratch_shapes=[
            pltpu.VMEM((full, columns), jnp.float32),
            pltpu.VMEM((full, full), jnp.bfloat16),
            pltpu.VMEM((full, full), jnp.bfloat16),
            pltpu.VMEM((full, 2 * columns), jnp.bfloat16),
            pltpu.VMEM((full, 2 * columns), jnp.bfloat16),
            pltpu.VMEM((devices, rows + spare, columns), jnp.float32),
            pltpu.SemaphoreType.DMA((full // block, 1)),
            pltpu.SemaphoreType.DMA((2, full // block, 1)),
            pltpu.SemaphoreType.DMA((full // block, 1)),
        ],
        compiler_params=params(28),
    )(field, aux, *far(basis_xt, basis_x), along, other)


def turn_kernel(stage, last, block, chunks, *refs):
    refs = list(refs)
    take = lambda: refs.pop(0)
    mix_ref, got_ref, basis_ref = take(), take(), take()
    has_z = stage >= 1 or chunks > 1
    has_v = stage >= 2 or (stage >= 1 and chunks > 1)
    diagonal_ref, low_x, high_x, low_y, high_y = take(), take(), take(), take(), take()
    residual_ref = take() if last else None
    scalars_ref = take() if stage >= 1 else None
    if has_z:
        old_z, old_edge_z = take(), take()
    if has_v:
        old_v, old_edge_v = take(), take()
    z_ref, edge_z_ref, y_ref = take(), take(), take()
    aux_ref = take() if last else None
    if stage >= 1:
        v_ref, edge_v_ref = take(), take()
    if not last:
        out_ref = take()
    got, basis, diagonal, lines, around, edge_z, image = [take() for _ in range(7)]
    residual = take() if last else None
    z = take() if has_z else None
    if stage >= 1:
        v, edge_v = take(), take()
    if not last:
        ahead_lines, sent = take(), take()
    given_semaphores, semaphores, late_semaphores = take(), take(), take()
    if not last:
        basis_semaphores, out_semaphores = take(), take()
    planes, rows, full = diagonal.shape
    devices, _, columns = got.shape
    parts = devices // planes
    half = planes * (rows + spare)
    main = planes * rows
    blocks = full // block
    groups = [slice(m * parts, (m + 1) * parts) for m in range(planes)]
    given = start_all([(got_ref.at[group], got.at[group]) for group in groups], given_semaphores)
    width = full // chunks
    turned = slice(full - width, full)
    fields = [(residual_ref, residual)] if last else []
    if has_z:
        fields += [(old_z, z), (old_edge_z, edge_z)]
    if has_v:
        fields += [(old_v, v), (old_edge_v, edge_v)]

    def needed(n):
        own = piece(n, block)
        pairs = [(basis_ref.at[own, turned], basis.at[own, turned])]
        return pairs + [(old.at[:, :, own], target.at[:, :, own]) for old, target in fields]

    stream = Stream(needed, blocks, semaphores)
    stream.begin()
    wait_all(given)
    take_lines(got, lines, planes, rows)
    def fold(value):
        total = value[:, :columns]
        for left in range(columns, value.shape[1], columns):
            total = total + value[:, left : left + columns]
        return total

    def finish_block(n, carry):
        stream.take(n)
        lanes = piece(n, block)
        result = lax.dot_general(
            lines[...], basis[lanes, turned], (((1,), (1,)), ((), ())), preferred_element_type=jnp.float32
        )
        result = result[:half] + result[half:]
        if stage >= 1:
            length = scalars_ref[2:3, 0:1]
            turn = scalars_ref[3:4, 0:1]
        for k in range(planes):
            value, edge = mixed_back(result, mix_ref, k, rows)
            if chunks > 1:
                scale = 1.0 if stage == 0 else -length
                if stage >= 1:
                    v[k, :, lanes] = v[k, :, lanes] + value
                    edge_v[k, :, lanes] = edge_v[k, :, lanes] + edge
                value = z[k, :, lanes] + scale * value
                edge = edge_z[k, :, lanes] + scale * edge
            elif stage >= 1:
                if stage >= 2:
                    value = value + turn * v[k, :, lanes]
                    edge = edge + turn * edge_v[k, :, lanes]
                v[k, :, lanes] = value
                edge_v[k, :, lanes] = edge
                value = z[k, :, lanes] - length * value
                edge = edge_z[k, :, lanes] - length * edge
            edge_z[k, :, lanes] = edge
            if last:
                shared = fold(residual[k, :, lanes] * value)
                for start in range(0, rows, 8):
                    carry = carry + shared[start : start + 8]
            around[k, spare : spare + rows, lanes] = value
            around[k, spare - 1 : spare, lanes] = edge[0:1]
            around[k, spare + rows : spare + rows + 1, lanes] = edge[1:2]
        return carry

    diagonal_copy = pltpu.make_async_copy(diagonal_ref, diagonal, late_semaphores.at[0])
    diagonal_copy.start()
    nothing = jnp.zeros((8, columns), jnp.float32)
    product = lax.fori_loop(0, blocks, finish_block, nothing)
    done = [(around.at[:, spare : spare + rows], z_ref), (edge_z, edge_z_ref)]
    if stage >= 1:
        done += [(v, v_ref), (edge_v, edge_v_ref)]
    done = start_all(done, late_semaphores.at[2:6])
    ahead = None
    if not last and chunks > 1:
        ahead = column_stream(basis_ref, basis, block, 0, width // block, basis_semaphores)
        ahead.begin()
    diagonal_copy.wait()

    def operate(index, carry):
        k = index // (rows // 8)
        tile = index - k * (rows // 8)
        own = piece(tile, 8)
        window = around[k, pl.ds(pl.multiple_of(tile * 8, 8), 24), :]
        value = window[8:16]
        above = pltpu.roll(window, 1, 0)[8:16]
        below = pltpu.roll(window, 23, 0)[8:16]
        middle = pl.ds(pl.multiple_of(tile * 8 + spare, 8), 8)
        before = around[jnp.where(k == 0, planes - 1, k - 1), middle, :]
        after = around[jnp.where(k == planes - 1, 0, k + 1), middle, :]
        total = diagonal[k, own, :] * value
        total = total + (low_x[own, :] * (value - above) - high_x[own, :] * (below - value))
        left = pltpu.roll(value, 1, 1)
        right = pltpu.roll(value, full - 1, 1)
        total = total + (low_y[...] * (value - left) - high_y[...] * (right - value))
        total = total + (2.0 * value - before - after)
        image[k, own, :] = total
        return carry + fold(value * total) if last else carry

    bend = lax.fori_loop(0, planes * (rows // 8), operate, nothing, unroll=2)
    if last:
        product = jnp.sum(product, axis=0, keepdims=True)
        bend = jnp.sum(bend, axis=0, keepdims=True)
        aux_ref[...] = jnp.concatenate([nothing[:2], product, bend, nothing[4:]], axis=0)
    image_copy = pltpu.make_async_copy(image, y_ref, late_semaphores.at[1])
    image_copy.start()
    if not last:
        mix_planes(lambda k, i, j: image[k, i, j], mix_ref, ahead_lines, rows)
        send_lines(ahead_lines, basis, sent, out_ref, block, 0, out_semaphores, ahead)
    image_copy.wait()
    wait_all(done)


def turn_lines(stage, last, got, part, operator, basis_z, basis_y, state, chunks):
    planes, rows, full = operator[0].shape
    _, _, columns = got.shape
    block = min(512, full // chunks)
    blocks = full // block
    field_shape = pltpu.HBM((planes, rows, full), jnp.float32)
    edge_shape = pltpu.HBM((planes, spare, full), jnp.float32)
    before = part if chunks > 1 else state
    specs = [scalar, vector] + [anywhere] * 2 + [vector] * 4
    given = [basis_z, got, *far(basis_y, operator[0])] + list(operator[1:])
    if last:
        specs.append(anywhere)
        given += far(state["residual"])
    if stage >= 1:
        specs.append(vector)
        given.append(state["scalars"])
    for name in ("z", "v"):
        if name in before:
            specs += [anywhere] * 2
            given += far(before[name], before["edge_" + name])
    names = ["z", "edge_z", "y"]
    outs = [anywhere] * 3
    shapes = [field_shape, edge_shape, field_shape]
    if last:
        names.append("aux")
        outs.append(vector)
        shapes.append(jax.ShapeDtypeStruct((spare, columns), jnp.float32))
    if stage >= 1:
        names += ["v", "edge_v"]
        outs += [anywhere, anywhere]
        shapes += [field_shape, edge_shape]
    field = pltpu.VMEM((planes, rows, full), jnp.float32)
    edge = pltpu.VMEM((planes, spare, full), jnp.float32)
    scratch = [
        pltpu.VMEM(got.shape, jnp.float32),
        pltpu.VMEM(basis_y.shape, jnp.bfloat16),
        field,
        pltpu.VMEM((2 * planes * (rows + spare), full // chunks), jnp.bfloat16),
        pltpu.VMEM((planes, rows + 2 * spare, full), jnp.float32),
        edge,
        field,
    ]
    if last:
        scratch.append(field)
    if "z" in before:
        scratch.append(field)
    if stage >= 1:
        scratch += [field, edge]
    if not last:
        sent = (planes, full // chunks // columns, rows, columns)
        names.append("sent")
        outs.append(anywhere)
        shapes.append(pltpu.HBM(sent, jnp.float32))
        scratch += [pltpu.VMEM((2 * planes * rows, full), jnp.bfloat16), pltpu.VMEM(sent, jnp.float32)]
    scratch += [
        pltpu.SemaphoreType.DMA((planes,)),
        pltpu.SemaphoreType.DMA((blocks, 6)),
        pltpu.SemaphoreType.DMA((6,)),
    ]
    if not last:
        scratch += [pltpu.SemaphoreType.DMA((blocks // chunks, 1))] * 2
    results = pl.pallas_call(
        functools.partial(turn_kernel, stage, last, block, chunks),
        in_specs=specs,
        out_specs=outs,
        out_shape=shapes,
        scratch_shapes=scratch,
        compiler_params=params(40),
    )(*given)
    return dict(zip(names, results))


def first_kernel(
    rows, velocity_ref, weight_ref, code_ref, above_ref, below_ref, side_ref, half_x_ref, half_y_ref,
    source_ref, predicted_ref, fields, moved, kept, semaphores, late_semaphores,
):
    planes, count, span = weight_ref.shape
    wide = half_y_ref.shape[1]
    pad = 16
    middle = count // 16 * 8
    early, late = [], []
    for channel in range(5):
        if channel < 3:
            main = velocity_ref.at[channel]
        else:
            main = weight_ref if channel == 3 else code_ref
        target = fields.at[channel]
        early.append((main.at[:, :middle], target.at[:, pad : pad + middle, :span]))
        early.append((above_ref.at[channel], target.at[:, pad - 8 : pad, :span]))
        early.append((below_ref.at[channel], target.at[:, pad + count : pad + count + 8, :span]))
        early.append((side_ref.at[channel], target.at[:, :, span:]))
        late.append((main.at[:, middle:], target.at[:, pad + middle : pad + count, :span]))
    early = start_all(early, semaphores)
    late = start_all(late, late_semaphores)
    wait_all(early)
    tiles = count // 8 + 2
    half_y = half_y_ref[...]

    def lane_slope(value):
        return pltpu.roll(value, wide - 1, 1) - pltpu.roll(value, 1, 1)

    def advance(index, carry):
        tile = index // planes
        k = index - tile * planes
        start = pl.multiple_of(8 + tile * 8, 8)
        window = pl.ds(pl.multiple_of(start - 8, 8), 24)
        own = pl.ds(start, 8)
        before = jnp.where(k == 0, planes - 1, k - 1)
        after = jnp.where(k == planes - 1, 0, k + 1)
        half_x = half_x_ref[own, :]
        first = fields[0, k, window, :]
        second = fields[1, k, own, :]
        third_before = fields[2, before, own, :]
        third_after = fields[2, after, own, :]
        weight = fields[3, k, own, :]
        for c in range(3):
            value = first if c == 0 else fields[c, k, window, :]
            along = first * value
            center = value[8:16]
            total = half_x * (pltpu.roll(along, 23, 0)[8:16] - pltpu.roll(along, 1, 0)[8:16])
            total = total + half_y * lane_slope(second * center)
            total = total + 0.5 * (third_after * fields[c, after, own, :] - third_before * fields[c, before, own, :])
            share = weight * total
            moved[c, k, own, :] = share
            kept[c, k, own, :] = total - share
        return carry

    safe = planes * (middle // 8)
    lax.fori_loop(0, safe, advance, 0, unroll=4)
    wait_all(late)
    lax.fori_loop(safe, planes * tiles, advance, 0, unroll=4)

    def settle(index, carry):
        k = index // tiles
        start = pl.multiple_of(8 + (index - k * tiles) * 8, 8)
        window = pl.ds(pl.multiple_of(start - 8, 8), 24)
        own = pl.ds(start, 8)
        code = fields[4, k, window, :]
        inside_x = half_x_ref[own, :] > 0.0
        inside_y = half_y > 0.0
        for c in range(3):
            share = moved[c, k, window, :]
            received = pltpu.roll(jnp.where(code == 1.0, share, 0.0), 1, 0)[8:16] + pltpu.roll(jnp.where(code == 2.0, share, 0.0), 23, 0)[8:16]
            center = share[8:16]
            middle = code[8:16]
            received = received + pltpu.roll(jnp.where(middle == 3.0, center, 0.0), 1, 1)
            received = received + pltpu.roll(jnp.where(middle == 4.0, center, 0.0), wide - 1, 1)
            result = fields[c, k, own, :] - time_step * (kept[c, k, own, :] + received)
            if c == 0:
                result = jnp.where(inside_x, result, 0.0)
            if c == 1:
                result = jnp.where(inside_y, result, 0.0)
            kept[c, k, own, :] = result
        return carry

    lax.fori_loop(0, planes * tiles, settle, 0, unroll=4)
    done = start_all(
        [(kept.at[c, :, pad : pad + count, :span], predicted_ref.at[c]) for c in range(3)], late_semaphores
    )
    inner = count // 8
    group = rows // 8

    def collect(index, carry):
        k = index // inner
        tile = index - k * inner
        start = pl.multiple_of(pad + tile * 8, 8)
        window = pl.ds(pl.multiple_of(start - 8, 8), 24)
        own = pl.ds(start, 8)
        before = jnp.where(k == 0, planes - 1, k - 1)
        after = jnp.where(k == planes - 1, 0, k + 1)
        first = kept[0, k, window, :]
        second = kept[1, k, own, :]
        total = half_x_ref[own, :] * (pltpu.roll(first, 23, 0)[8:16] - pltpu.roll(first, 1, 0)[8:16])
        total = total + half_y * lane_slope(second)
        total = total + 0.5 * (kept[2, after, own, :] - kept[2, before, own, :])
        target = tile // group
        spot = pl.multiple_of((tile - target * group) * 8, 8)
        source_ref[target, k, pl.ds(spot, 8), :] = -total[:, :span]
        return carry

    lax.fori_loop(0, planes * inner, collect, 0, unroll=8)
    wait_all(done)


def first_step(velocity, weight, code, above, below, side, half_x, half_y, rows):
    planes, count, span = weight.shape
    tall, wide = half_x.shape[0], half_y.shape[1]
    return pl.pallas_call(
        functools.partial(first_kernel, rows),
        in_specs=[anywhere] * 6 + [vector] * 2,
        out_specs=[vector, anywhere],
        out_shape=[
            jax.ShapeDtypeStruct((count // rows, planes, rows, span), jnp.float32),
            jax.ShapeDtypeStruct((3, planes, count, span), jnp.float32),
        ],
        scratch_shapes=[
            pltpu.VMEM((5, planes, tall, wide), jnp.float32),
            pltpu.VMEM((3, planes, tall, wide), jnp.float32),
            pltpu.VMEM((3, planes, tall, wide), jnp.float32),
            pltpu.SemaphoreType.DMA((20,)),
            pltpu.SemaphoreType.DMA((5,)),
        ],
        compiler_params=params(48),
    )(*far(velocity, weight, code, above, below, side), half_x, half_y)


def neighbours(axis, last, leading):
    size = lax.axis_size(axis)
    up = [(i, i + 1) for i in range(size - 1)]
    down = [(i + 1, i) for i in range(size - 1)]
    return lax.ppermute(last, axis, up), lax.ppermute(leading, axis, down)


def extended_1(value, start, count, before, after):
    padded = jnp.pad(value, (before, after))
    return lax.dynamic_slice_in_dim(padded, start, count + before + after)


def lanes_sum(value, columns):
    return jnp.sum(value.reshape(-1, value.shape[-1] // columns, columns), axis=(0, 1))


def add_kernel(numbers_ref, sums_ref, pressure_ref, direction_ref, lifted_ref, out_ref):
    total = jnp.sum(jnp.sum(sums_ref[...], axis=0), axis=1, keepdims=True)
    turn = total[2:3] / numbers_ref[0:1, 0:1]
    length = total[2:3] / (total[3:4] - turn * turn * numbers_ref[1:2, 0:1])
    for k in range(pressure_ref.shape[0]):
        direction = lifted_ref[k] + turn * direction_ref[k]
        out_ref[0, k] = pressure_ref[k] + length * direction


def add_step(numbers, sums, pressure, direction, lifted, pieces):
    planes, rows, full = pressure.shape
    span = full // pieces
    field = pl.BlockSpec((planes, rows, span), lambda n: (0, 0, n))
    return pl.pallas_call(
        add_kernel,
        grid=(pieces,),
        in_specs=[vector] * 2 + [field] * 3,
        out_specs=pl.BlockSpec((1, planes, rows, span), lambda n: (n, 0, 0, 0)),
        out_shape=pltpu.HBM((pieces, planes, rows, span), jnp.float32),
        compiler_params=params(20),
    )(numbers, sums, pressure, direction, lifted)


def correct_kernel(
    predicted_ref, own_ref, previous_ref, next_ref, above_ref, below_ref, left_ref, right_ref,
    half_x_ref, half_y_ref, corrected_ref, pressure_ref,
):
    n = pl.program_id(0)
    last = pl.num_programs(0) - 1
    _, planes, rows, _ = own_ref.shape
    for k in range(planes):
        value = own_ref[0, k]
        above = jnp.where(n == 0, above_ref[k], previous_ref[0, k, rows - 1 : rows, :])
        below = jnp.where(n == last, below_ref[k], next_ref[0, k, 0:1, :])
        rising = jnp.concatenate([value[1:], below], axis=0) - jnp.concatenate([above, value[:-1]], axis=0)
        ahead = jnp.concatenate([value[:, 1:], right_ref[0, k]], axis=1)
        behind = jnp.concatenate([left_ref[0, k], value[:, :-1]], axis=1)
        across = own_ref[0, (k + 1) % planes] - own_ref[0, (k - 1) % planes]
        pressure_ref[:, k, :] = value
        corrected_ref[0, :, k, :] = predicted_ref[0, k] - half_x_ref[...] * rising
        corrected_ref[1, :, k, :] = predicted_ref[1, k] - half_y_ref[...] * (ahead - behind)
        corrected_ref[2, :, k, :] = predicted_ref[2, k] - 0.5 * across


def correct_step(predicted, pressure, above, below, left, right, half_x, half_y):
    pieces, planes, rows, span = pressure.shape
    count = pieces * rows
    own = lambda shift: pl.BlockSpec(
        (1, planes, rows, span), lambda n: (jnp.clip(n + shift, 0, pieces - 1), 0, 0, 0)
    )
    column = pl.BlockSpec((1, planes, rows, 1), lambda n: (n, 0, 0, 0))
    return pl.pallas_call(
        correct_kernel,
        grid=(pieces,),
        in_specs=[
            pl.BlockSpec((3, planes, rows, span), lambda n: (0, 0, n, 0)),
            own(0),
            own(-1),
            own(1),
            vector,
            vector,
            column,
            column,
            pl.BlockSpec((rows, 1), lambda n: (n, 0)),
            vector,
        ],
        out_specs=[
            pl.BlockSpec((3, rows, planes, span), lambda n: (0, n, 0, 0)),
            pl.BlockSpec((rows, planes, span), lambda n: (n, 0, 0)),
        ],
        out_shape=[
            jax.ShapeDtypeStruct((3, count, planes, span), jnp.float32),
            jax.ShapeDtypeStruct((count, planes, span), jnp.float32),
        ],
        compiler_params=params(28),
    )(predicted, pressure, pressure, pressure, above, below, left, right, half_x, half_y)


def per_device(
    velocity,
    cut_flags,
    redirect,
    share_weight,
    inverse_dx,
    inverse_dy,
    basis_x,
    basis_y,
    basis_z,
    eigen_x,
    eigen_y,
    eigen_z,
):
    x_parts = lax.axis_size("gx")
    y_parts = lax.axis_size("gy")
    devices = x_parts * y_parts
    x_index = lax.axis_index("gx")
    y_index = lax.axis_index("gy")
    own = x_index * y_parts + y_index
    x_count, planes, y_count = velocity.shape[1:]
    full_x = x_count * x_parts
    full_y = y_count * y_parts
    rows = full_x // devices
    columns = planes * full_y // devices
    chunks = 2 if columns % 256 == 0 else 1
    columns = columns // chunks
    column_blocks = devices // planes
    inverse_x = lax.dynamic_slice_in_dim(inverse_dx, x_index * x_count, x_count)
    inverse_y = lax.dynamic_slice_in_dim(inverse_dy, y_index * y_count, y_count)
    flags = cut_flags.astype(jnp.float32)
    code = (cut_flags * (redirect + 1)).astype(jnp.float32)
    weight = share_weight * flags
    reach = 3

    def edge_rows(part):
        cut = cut_flags[part]
        share = share_weight[part] * cut.astype(jnp.float32)
        target = (cut * (redirect[part] + 1)).astype(jnp.float32)
        return jnp.concatenate([velocity[:, part], share[None], target[None]])

    above, below = neighbours("gx", edge_rows(slice(x_count - reach, None)), edge_rows(slice(0, reach)))
    velocity = velocity.transpose(0, 2, 1, 3)
    weight = weight.transpose(1, 0, 2)
    code = code.transpose(1, 0, 2)
    above = above.transpose(0, 2, 1, 3)
    below = below.transpose(0, 2, 1, 3)

    def edge_columns(part):
        middle = jnp.concatenate([velocity[..., part], weight[None, ..., part], code[None, ..., part]])
        return jnp.concatenate([above[..., part], middle, below[..., part]], axis=2).swapaxes(2, 3)

    left, right = neighbours("gy", edge_columns(slice(y_count - reach, None)), edge_columns(slice(0, reach)))
    left, right = [
        jnp.pad(part, ((0, 0), (0, 0), (0, 0), (16 - reach, 16 - reach))) for part in (left, right)
    ]
    side = jnp.concatenate([right, jnp.zeros((5, planes, 128 - 2 * reach, x_count + 32), jnp.float32), left], axis=2)
    side = side.swapaxes(2, 3)
    above = jnp.pad(above, ((0, 0), (0, 0), (8 - reach, 0), (0, 0)))
    below = jnp.pad(below, ((0, 0), (0, 0), (0, 8 - reach), (0, 0)))
    half_x = 0.5 * extended_1(inverse_dx, x_index * x_count, x_count, 16, 16)[:, None]
    half_y = 0.5 * extended_1(inverse_dy, y_index * y_count, y_count, reach, reach)
    half_y = jnp.concatenate([half_y[reach:], jnp.zeros((128 - 2 * reach,), jnp.float32), half_y[:reach]])[None]
    source, predicted = first_step(velocity, weight, code, above, below, side, half_x, half_y, rows)
    diagonal = (cell_shift + cut_shift * flags).reshape(y_parts, rows, planes, y_count).transpose(0, 2, 1, 3)
    diagonal = lax.all_to_all(diagonal, "gy", 0, 0, tiled=True)
    source, diagonal = lax.optimization_barrier((source, diagonal))
    source = lax.all_to_all(source, "gy", 0, 0, tiled=True)
    source, basis_xt = lax.optimization_barrier((source, basis_x.T))
    diagonal = diagonal.transpose(1, 2, 0, 3).reshape(planes, rows, full_y)
    whole_x = jnp.pad(inverse_dx, 1)
    face_x = lax.dynamic_slice_in_dim(whole_x[:-1] * whole_x[1:], own * rows, rows + 1)
    whole_y = jnp.pad(inverse_dy, 1)
    face_y = whole_y[:-1] * whole_y[1:]
    operator = (diagonal, face_x[:-1, None], face_x[1:, None], face_y[None, :-1], face_y[None, 1:])
    along = eigen_x[:, None]
    other = [
        (
            lax.dynamic_slice_in_dim(
                eigen_y, full_y // chunks * chunk + (own % column_blocks) * columns, columns
            )
            + lax.dynamic_slice_in_dim(eigen_z, own // column_blocks, 1)
        )[None]
        for chunk in range(chunks)
    ]

    def apply(stage, field, sent, aux, state):
        sents = [sent] + [
            more_lines(field, basis_z, basis_y, columns, chunks, chunk) for chunk in range(1, chunks)
        ]
        gots = []
        for chunk, sent in enumerate(sents):
            sent = sent.reshape(devices, rows, columns)
            got = lax.all_to_all(sent, both, 0, 0, tiled=True).reshape(full_x, columns)
            given = aux if chunk == 0 else jnp.zeros((spare, columns), jnp.float32)
            got = column_lines(got, given, basis_xt, basis_x, along, other[chunk], rows)
            gots.append(lax.all_to_all(got, both, 0, 0, tiled=True))
        if stage > 0:
            state["scalars"] = numbers_of(gots[0][:, rows:], state.get("scalars"))
        part = None
        if chunks > 1:
            part = part_lines(stage, gots[0], basis_z, basis_y, rows, chunks, state)
        return gots[-1], part

    def numbers_of(sums, numbers):
        product = jnp.sum(sums[:, 2])
        bend = jnp.sum(sums[:, 3])
        turn = jnp.zeros_like(product)
        if numbers is not None:
            turn = product / numbers[0, 0]
            bend = bend - turn * turn * numbers[1, 0]
        numbers = jnp.stack([product, bend, product / bend, turn])
        return jnp.broadcast_to(jnp.pad(numbers, (0, 4))[:, None], (8, 128))

    residual, sent = start_lines(source, basis_z, basis_y, columns, chunks)
    state = {}
    got, part = apply(0, residual, sent, jnp.zeros((spare, columns), jnp.float32), state)
    state |= turn_lines(0, False, got, part, operator, basis_z, basis_y, state, chunks)
    for stage in range(1, ITERS):
        partial = [lanes_sum(residual * state["z"], columns), lanes_sum(state["z"] * state["y"], columns)]
        aux = jnp.pad(jnp.stack(partial), ((2, spare - 4), (0, 0)))
        got, part = apply(stage, state["y"], state["sent"], aux, state)
        length, turn = state["scalars"][2, 0], state["scalars"][3, 0]
        if stage == 1:
            direction, image = state["z"], state["y"]
            pressure = length * direction
        else:
            direction = state["z"] + turn * direction
            image = state["y"] + turn * image
            pressure = pressure + length * direction
        residual = residual - length * image
        state["residual"] = residual
        last = stage + 1 == ITERS
        state |= turn_lines(stage, last, got, part, operator, basis_z, basis_y, state, chunks)
    sums = jnp.broadcast_to(state["aux"][None], (devices, spare, columns))
    sums = lax.all_to_all(sums, both, 0, 0, tiled=True)
    pressure = add_step(state["scalars"], sums, pressure, direction, state["z"], y_parts)
    pressure = lax.all_to_all(pressure, "gy", 0, 0, tiled=True)
    above, below = neighbours("gx", pressure[-1, :, -1:], pressure[0, :, :1])
    left, right = neighbours("gy", pressure[..., -1], pressure[..., 0])
    half_x = 0.5 * inverse_x[:, None]
    half_y = 0.5 * inverse_y[None]
    corrected, pressure = correct_step(
        predicted, pressure, above, below, left[..., None], right[..., None], half_x, half_y
    )
    return corrected, pressure


def solution(mesh):
    in_specs = (
        P(None, "gx", None, "gy"),
        P("gx", None, "gy"),
        P("gx", None, "gy"),
        P("gx", None, "gy"),
        P(),
        P(),
        P(),
        P(),
        P(),
        P(),
        P(),
        P(),
    )
    out_specs = (P(None, "gx", None, "gy"), P("gx", None, "gy"))
    return jax.shard_map(
        per_device, mesh=mesh, in_specs=in_specs, out_specs=out_specs, check_vma=False
    )
```

```python
import functools

import jax
import jax.numpy as jnp
from jax import lax
from jax.experimental import pallas as pl
from jax.experimental.pallas import tpu as pltpu
from jax.sharding import PartitionSpec as P

ITERS = 4


time_step = 0.25
cell_shift = 0.05
cut_shift = 0.45
both = ("gx", "gy")
spare = 8


def halves(value):
    high = value.astype(jnp.bfloat16)
    low = (value - high.astype(jnp.float32)).astype(jnp.bfloat16)
    return high, low


def params(mebibytes):
    return pltpu.CompilerParams(vmem_limit_bytes=mebibytes * 1024 * 1024)


def mix_planes(read, mix_ref, lines, rows):
    planes = mix_ref.shape[0]
    width = lines.shape[1]
    lane = 512 if width % 512 == 0 else width
    half = planes * rows

    def strip(index, carry):
        start = pl.multiple_of(index * 16, 16)
        for left in range(0, width, lane):
            fields = [read(k, pl.ds(start, 16), pl.ds(left, lane)) for k in range(planes)]
            for m in range(planes):
                total = fields[0] * mix_ref[0, m]
                for k in range(1, planes):
                    total = total + fields[k] * mix_ref[k, m]
                high, low = halves(total)
                lines[pl.ds(m * rows + start, 16), pl.ds(left, lane)] = high
                lines[pl.ds(half + m * rows + start, 16), pl.ds(left, lane)] = low
        return carry

    lax.fori_loop(0, rows // 16, strip, 0)


anywhere = pl.BlockSpec(memory_space=pl.ANY)
vector = pl.BlockSpec(memory_space=pltpu.VMEM)
scalar = pl.BlockSpec(memory_space=pltpu.SMEM)


class Stream:
    def __init__(self, pairs, count, semaphores):
        self.pairs = pairs
        self.count = count
        self.semaphores = semaphores

    def copies(self, n):
        pairs = self.pairs(n)
        return [
            pltpu.make_async_copy(given, target, self.semaphores.at[n, index])
            for index, (given, target) in enumerate(pairs)
        ]

    def start(self, n):
        for copy in self.copies(n):
            copy.start()

    def begin(self):
        for n in range(min(2, self.count)):
            self.start(n)

    def take(self, n):
        for copy in self.copies(n):
            copy.wait()

        @pl.when(n + 2 < self.count)
        def _():
            self.start(n + 2)

    def end(self):
        def step(n, carry):
            for copy in self.copies(n):
                copy.wait()
            return carry

        lax.fori_loop(0, self.count, step, 0)


def start_all(pairs, semaphores):
    copies = [
        pltpu.make_async_copy(given, target, semaphores.at[index])
        for index, (given, target) in enumerate(pairs)
    ]
    for copy in copies:
        copy.start()
    return copies


def wait_all(copies):
    for copy in copies:
        copy.wait()


def far(*values):
    return [pltpu.with_memory_space_constraint(value, pltpu.HBM) for value in values]


def piece(index, size):
    return pl.ds(pl.multiple_of(index * size, size), size)


def send_lines(lines, basis, sent, out_ref, block, chunk, semaphores, stream=None):
    planes, all_parts, rows, columns = sent.shape
    half = planes * rows
    parts = block // columns
    blocks = all_parts // parts
    out = Stream(
        lambda n: [(sent.at[:, pl.ds(n * parts, parts)], out_ref.at[:, pl.ds(n * parts, parts)])],
        blocks,
        semaphores,
    )

    def step(n, carry):
        if stream is not None:
            stream.take(n)
        result = jnp.dot(lines[...], basis[:, piece(chunk * blocks + n, block)], preferred_element_type=jnp.float32)
        result = result[:half] + result[half:]
        for m in range(planes):
            for part in range(parts):
                sent[m, n * parts + part] = result[
                    m * rows : (m + 1) * rows, part * columns : (part + 1) * columns
                ]
        out.start(n)
        return carry

    lax.fori_loop(0, blocks, step, 0)
    out.end()


def column_stream(basis_ref, basis, block, chunk, blocks, semaphores):
    def pairs(n):
        own = piece(chunk * blocks + n, block)
        return [(basis_ref.at[:, own], basis.at[:, own])]

    return Stream(pairs, blocks, semaphores)


def start_kernel(
    block, mix_ref, field_ref, basis_ref, kept_ref, out_ref,
    field, basis, lines, sent, semaphores, basis_semaphores, out_semaphores,
):
    pieces, planes, rows, span = field_ref.shape
    given = [(field_ref.at[n], field.at[:, :, n * span : (n + 1) * span]) for n in range(pieces)]
    given = start_all(given, semaphores)
    stream = column_stream(basis_ref, basis, block, 0, basis_semaphores.shape[0], basis_semaphores)
    stream.begin()
    wait_all(given)
    kept = pltpu.make_async_copy(field, kept_ref, semaphores.at[pieces])
    kept.start()
    mix_planes(lambda k, i, j: field[k, i, j], mix_ref, lines, rows)
    send_lines(lines, basis, sent, out_ref, block, 0, out_semaphores, stream)
    kept.wait()


def start_lines(field, basis_z, basis_y, columns, chunks):
    pieces, planes, rows, span = field.shape
    full = pieces * span
    block = min(256, full // chunks)
    blocks = full // chunks // block
    sent = (planes, full // chunks // columns, rows, columns)
    return pl.pallas_call(
        functools.partial(start_kernel, block),
        in_specs=[scalar, vector, anywhere],
        out_specs=[anywhere] * 2,
        out_shape=[
            pltpu.HBM((planes, rows, full), jnp.float32),
            pltpu.HBM(sent, jnp.float32),
        ],
        scratch_shapes=[
            pltpu.VMEM((planes, rows, full), jnp.float32),
            pltpu.VMEM(basis_y.shape, jnp.bfloat16),
            pltpu.VMEM((2 * planes * rows, full), jnp.bfloat16),
            pltpu.VMEM(sent, jnp.float32),
            pltpu.SemaphoreType.DMA((pieces + 1,)),
            pltpu.SemaphoreType.DMA((blocks, 1)),
            pltpu.SemaphoreType.DMA((blocks, 1)),
        ],
        compiler_params=params(24),
    )(basis_z, field, *far(basis_y))


def more_kernel(
    block, chunk, mix_ref, field_ref, basis_ref, out_ref, field, basis, lines, sent, semaphore, basis_semaphores, out_semaphores
):
    given = pltpu.make_async_copy(field_ref, field, semaphore)
    given.start()
    stream = column_stream(basis_ref, basis, block, chunk, basis_semaphores.shape[0], basis_semaphores)
    stream.begin()
    given.wait()
    mix_planes(lambda k, i, j: field[k, i, j], mix_ref, lines, field.shape[1])
    send_lines(lines, basis, sent, out_ref, block, chunk, out_semaphores, stream)


def more_lines(field, basis_z, basis_y, columns, chunks, chunk):
    planes, rows, full = field.shape
    block = min(256, full // chunks)
    blocks = full // chunks // block
    sent = (planes, full // chunks // columns, rows, columns)
    return pl.pallas_call(
        functools.partial(more_kernel, block, chunk),
        in_specs=[scalar, anywhere, anywhere],
        out_specs=anywhere,
        out_shape=pltpu.HBM(sent, jnp.float32),
        scratch_shapes=[
            pltpu.VMEM(field.shape, jnp.float32),
            pltpu.VMEM(basis_y.shape, jnp.bfloat16),
            pltpu.VMEM((2 * planes * rows, full), jnp.bfloat16),
            pltpu.VMEM(sent, jnp.float32),
            pltpu.SemaphoreType.DMA,
            pltpu.SemaphoreType.DMA((blocks, 1)),
            pltpu.SemaphoreType.DMA((blocks, 1)),
        ],
        compiler_params=params(24),
    )(basis_z, *far(field, basis_y))


def take_lines(got, lines, planes, rows):
    devices, _, _, columns = got.shape
    parts = devices // planes
    half = planes * (rows + spare)
    main = planes * rows
    edge_rows = lax.broadcasted_iota(jnp.int32, (spare, columns), 0) < 2
    for part in range(parts):
        lanes = slice(part * columns, (part + 1) * columns)
        edges = []
        for m in range(planes):
            high, low = halves(got[m * parts + part, : rows // 4].reshape(rows, columns))
            lines[m * rows : (m + 1) * rows, lanes] = high
            lines[half + m * rows : half + (m + 1) * rows, lanes] = low
            edge = got[m * parts + part, rows // 4]
            edges.append(jnp.where(edge_rows, jnp.concatenate([edge, edge], axis=0), 0.0))
        high, low = halves(jnp.concatenate(edges, axis=0))
        lines[main:half, lanes] = high
        lines[half + main :, lanes] = low


def mixed_back(result, mix_ref, k, rows):
    planes = mix_ref.shape[0]
    main = planes * rows
    value = result[:rows] * mix_ref[k, 0]
    edge = result[main : main + spare] * mix_ref[k, 0]
    for m in range(1, planes):
        value = value + result[m * rows : (m + 1) * rows] * mix_ref[k, m]
        edge = edge + result[main + m * spare : main + (m + 1) * spare] * mix_ref[k, m]
    return value, edge


def part_kernel(stage, rows, block, *refs):
    refs = list(refs)
    take = lambda: refs.pop(0)
    mix_ref, got_ref, basis_ref = take(), take(), take()
    if stage >= 1:
        scalars_ref, old_z, old_edge_z = take(), take(), take()
    if stage >= 2:
        old_v, old_edge_v = take(), take()
    out_refs = [take() for _ in range(4 if stage >= 1 else 2)]
    got, basis, lines = take(), take(), take()
    outs = [take() for _ in range(4 if stage >= 1 else 2)]
    given_semaphores, semaphores, out_semaphores = take(), take(), take()
    z, edge_z = outs[:2]
    planes = mix_ref.shape[0]
    parts = got.shape[0] // planes
    width = lines.shape[1]
    half = planes * (rows + spare)
    blocks = basis.shape[0] // block
    groups = [slice(m * parts, (m + 1) * parts) for m in range(planes)]
    given = start_all([(got_ref.at[group], got.at[group]) for group in groups], given_semaphores)
    fields = []
    if stage >= 1:
        v, edge_v = outs[2:]
        fields += [(old_z, z), (old_edge_z, edge_z)]
    if stage >= 2:
        fields += [(old_v, v), (old_edge_v, edge_v)]

    def needed(n):
        own = piece(n, block)
        pairs = [(basis_ref.at[own, :width], basis.at[own])]
        return pairs + [(old.at[:, :, own], target.at[:, :, own]) for old, target in fields]

    def made(n):
        own = piece(n, block)
        return [(out.at[:, :, own], out_ref.at[:, :, own]) for out, out_ref in zip(outs, out_refs)]

    stream = Stream(needed, blocks, semaphores)
    sink = Stream(made, blocks, out_semaphores)
    stream.begin()
    wait_all(given)
    take_lines(got, lines, planes, rows)

    def step(n, carry):
        stream.take(n)
        lanes = piece(n, block)
        result = lax.dot_general(
            lines[...], basis[lanes, :], (((1,), (1,)), ((), ())), preferred_element_type=jnp.float32
        )
        result = result[:half] + result[half:]
        if stage >= 1:
            length = scalars_ref[2:3, 0:1]
            turn = scalars_ref[3:4, 0:1]
        for k in range(planes):
            value, edge = mixed_back(result, mix_ref, k, rows)
            if stage >= 1:
                if stage >= 2:
                    value = value + turn * v[k, :, lanes]
                    edge = edge + turn * edge_v[k, :, lanes]
                v[k, :, lanes] = value
                edge_v[k, :, lanes] = edge
                value = z[k, :, lanes] - length * value
                edge = edge_z[k, :, lanes] - length * edge
            z[k, :, lanes] = value
            edge_z[k, :, lanes] = edge
        sink.start(n)
        return carry

    lax.fori_loop(0, blocks, step, 0)
    sink.end()


def part_lines(stage, got, basis_z, basis_y, rows, chunks, state):
    planes = basis_z.shape[0]
    full = basis_y.shape[0]
    block = min(256, full)
    half = planes * (rows + spare)
    field, edge = (planes, rows, full), (planes, spare, full)
    names = ["z", "edge_z"]
    given = [basis_z, got, *far(basis_y)]
    specs = [scalar, vector, anywhere]
    if stage >= 1:
        names += ["v", "edge_v"]
        given += [state["scalars"], *far(state["z"], state["edge_z"])]
        specs += [vector, anywhere, anywhere]
    if stage >= 2:
        given += far(state["v"], state["edge_v"])
        specs += [anywhere, anywhere]
    shapes = [field, edge] * (len(names) // 2)
    results = pl.pallas_call(
        functools.partial(part_kernel, stage, rows, block),
        in_specs=specs,
        out_specs=[anywhere] * len(names),
        out_shape=[pltpu.HBM(shape, jnp.float32) for shape in shapes],
        scratch_shapes=[
            pltpu.VMEM(got.shape, jnp.float32),
            pltpu.VMEM((full, full // chunks), jnp.bfloat16),
            pltpu.VMEM((2 * half, full // chunks), jnp.bfloat16),
        ]
        + [pltpu.VMEM(shape, jnp.float32) for shape in shapes]
        + [
            pltpu.SemaphoreType.DMA((planes,)),
            pltpu.SemaphoreType.DMA((full // block, 5)),
            pltpu.SemaphoreType.DMA((full // block, 4)),
        ],
        compiler_params=params(28),
    )(*given)
    return dict(zip(names, results))


def column_kernel(
    rows, block, field_ref, aux_ref, ahead_ref, back_ref, along_ref, other_ref, out_ref,
    field, ahead, back, lines, spectral, buffer, given_semaphores, semaphores, out_semaphores,
):
    full, columns = field_ref.shape
    blocks = full // block
    group = block // rows
    devices = full // rows
    given = Stream(
        lambda n: [(field_ref.at[piece(n, block)], field.at[piece(n, block)])], blocks, given_semaphores
    )
    aheads = Stream(
        lambda n: [(ahead_ref.at[piece(n, block)], ahead.at[piece(n, block)])], blocks, semaphores.at[0]
    )
    backs = Stream(
        lambda n: [(back_ref.at[piece(n, block)], back.at[piece(n, block)])], blocks, semaphores.at[1]
    )
    out = Stream(
        lambda n: [(buffer.at[pl.ds(n * group, group)], out_ref.at[pl.ds(n * group, group)])],
        blocks,
        out_semaphores,
    )
    for n in range(blocks):
        given.start(n)
    aheads.begin()
    given.end()

    def strip(index, carry):
        own = piece(index, 64)
        high, low = halves(field[own, :])
        lines[own, :columns] = high
        lines[own, columns:] = low
        return carry

    lax.fori_loop(0, full // 64, strip, 0, unroll=4)

    def forth(n, carry):
        aheads.take(n)

        @pl.when(n == blocks - 1)
        def _():
            backs.begin()

        own = piece(n, block)
        result = jnp.dot(ahead[own, :], lines[...], preferred_element_type=jnp.float32)
        result = result[:, :columns] + result[:, columns:]
        high, low = halves(result / (along_ref[own, :] + other_ref[...]))
        spectral[own, :columns] = high
        spectral[own, columns:] = low
        return carry

    lax.fori_loop(0, blocks, forth, 0)

    def reverse(n, carry):
        backs.take(n)
        result = jnp.dot(back[piece(n, block), :], spectral[...], preferred_element_type=jnp.float32)
        result = result[:, :columns] + result[:, columns:]
        for part in range(group):
            own = result[part * rows : (part + 1) * rows]
            buffer[n * group + part, : rows // 4] = own.reshape(rows // 4, 4, columns)
        return carry

    lax.fori_loop(0, blocks, reverse, 0)
    rest = aux_ref[2:4, :]

    def close(n, carry):
        for part in range(group):
            own = n * group + part
            above = buffer[jnp.maximum(own - 1, 0), rows // 4 - 1, 3:4, :]
            above = jnp.where(own > 0, above, 0.0)
            below = buffer[jnp.minimum(own + 1, devices - 1), 0, 0:1, :]
            below = jnp.where(own + 1 < devices, below, 0.0)
            buffer[own, rows // 4] = jnp.concatenate([above, below, rest], axis=0)
        out.start(n)
        return carry

    lax.fori_loop(0, blocks, close, 0)
    out.end()


def column_lines(field, aux, basis_xt, basis_x, along, other, rows):
    full, columns = field.shape
    block = min(512, full)
    devices = full // rows
    return pl.pallas_call(
        functools.partial(column_kernel, rows, block),
        in_specs=[vector, vector, anywhere, anywhere, vector, vector],
        out_specs=anywhere,
        out_shape=pltpu.HBM((devices, rows // 4 + 1, 4, columns), jnp.float32),
        scratch_shapes=[
            pltpu.VMEM((full, columns), jnp.float32),
            pltpu.VMEM((full, full), jnp.bfloat16),
            pltpu.VMEM((full, full), jnp.bfloat16),
            pltpu.VMEM((full, 2 * columns), jnp.bfloat16),
            pltpu.VMEM((full, 2 * columns), jnp.bfloat16),
            pltpu.VMEM((devices, rows // 4 + 1, 4, columns), jnp.float32),
            pltpu.SemaphoreType.DMA((full // block, 1)),
            pltpu.SemaphoreType.DMA((2, full // block, 1)),
            pltpu.SemaphoreType.DMA((full // block, 1)),
        ],
        compiler_params=params(28),
    )(field, aux, *far(basis_xt, basis_x), along, other)


def turn_kernel(stage, last, block, chunks, *refs):
    refs = list(refs)
    take = lambda: refs.pop(0)
    mix_ref, got_ref, basis_ref = take(), take(), take()
    has_z = stage >= 1 or chunks > 1
    has_v = stage >= 2 or (stage >= 1 and chunks > 1)
    diagonal_ref, low_x, high_x, low_y, high_y = take(), take(), take(), take(), take()
    residual_ref = take() if last else None
    scalars_ref = take() if stage >= 1 else None
    if has_z:
        old_z, old_edge_z = take(), take()
    if has_v:
        old_v, old_edge_v = take(), take()
    z_ref, edge_z_ref, y_ref = take(), take(), take()
    aux_ref = take() if last else None
    if stage >= 1:
        v_ref, edge_v_ref = take(), take()
    if not last:
        out_ref = take()
    got, basis, diagonal, lines, around, edge_z, image = [take() for _ in range(7)]
    residual = take() if last else None
    z = take() if has_z else None
    if stage >= 1:
        v, edge_v = take(), take()
    if not last:
        ahead_lines, sent = take(), take()
    given_semaphores, semaphores, late_semaphores = take(), take(), take()
    if not last:
        basis_semaphores, out_semaphores = take(), take()
    planes, rows, full = diagonal.shape
    devices, _, _, columns = got.shape
    parts = devices // planes
    half = planes * (rows + spare)
    main = planes * rows
    blocks = full // block
    groups = [slice(m * parts, (m + 1) * parts) for m in range(planes)]
    given = start_all([(got_ref.at[group], got.at[group]) for group in groups], given_semaphores)
    width = full // chunks
    turned = slice(full - width, full)
    fields = [(residual_ref, residual)] if last else []
    if has_z:
        fields += [(old_z, z), (old_edge_z, edge_z)]
    if has_v:
        fields += [(old_v, v), (old_edge_v, edge_v)]

    def needed(n):
        own = piece(n, block)
        pairs = [(basis_ref.at[own, turned], basis.at[own, turned])]
        return pairs + [(old.at[:, :, own], target.at[:, :, own]) for old, target in fields]

    stream = Stream(needed, blocks, semaphores)
    stream.begin()
    wait_all(given)
    take_lines(got, lines, planes, rows)
    def fold(value):
        total = value[:, :columns]
        for left in range(columns, value.shape[1], columns):
            total = total + value[:, left : left + columns]
        return total

    def finish_block(n, carry):
        stream.take(n)
        lanes = piece(n, block)
        result = lax.dot_general(
            lines[...], basis[lanes, turned], (((1,), (1,)), ((), ())), preferred_element_type=jnp.float32
        )
        result = result[:half] + result[half:]
        if stage >= 1:
            length = scalars_ref[2:3, 0:1]
            turn = scalars_ref[3:4, 0:1]
        for k in range(planes):
            value, edge = mixed_back(result, mix_ref, k, rows)
            if chunks > 1:
                scale = 1.0 if stage == 0 else -length
                if stage >= 1:
                    v[k, :, lanes] = v[k, :, lanes] + value
                    edge_v[k, :, lanes] = edge_v[k, :, lanes] + edge
                value = z[k, :, lanes] + scale * value
                edge = edge_z[k, :, lanes] + scale * edge
            elif stage >= 1:
                if stage >= 2:
                    value = value + turn * v[k, :, lanes]
                    edge = edge + turn * edge_v[k, :, lanes]
                v[k, :, lanes] = value
                edge_v[k, :, lanes] = edge
                value = z[k, :, lanes] - length * value
                edge = edge_z[k, :, lanes] - length * edge
            edge_z[k, :, lanes] = edge
            if last:
                shared = fold(residual[k, :, lanes] * value)
                for start in range(0, rows, 8):
                    carry = carry + shared[start : start + 8]
            around[k, spare : spare + rows, lanes] = value
            around[k, spare - 1 : spare, lanes] = edge[0:1]
            around[k, spare + rows : spare + rows + 1, lanes] = edge[1:2]
        return carry

    diagonal_copy = pltpu.make_async_copy(diagonal_ref, diagonal, late_semaphores.at[0])
    diagonal_copy.start()
    nothing = jnp.zeros((8, columns), jnp.float32)
    product = lax.fori_loop(0, blocks, finish_block, nothing)
    done = [(around.at[:, spare : spare + rows], z_ref), (edge_z, edge_z_ref)]
    if stage >= 1:
        done += [(v, v_ref), (edge_v, edge_v_ref)]
    done = start_all(done, late_semaphores.at[2:6])
    ahead = None
    if not last and chunks > 1:
        ahead = column_stream(basis_ref, basis, block, 0, width // block, basis_semaphores)
        ahead.begin()
    diagonal_copy.wait()

    def operate(index, carry):
        k = index // (rows // 8)
        tile = index - k * (rows // 8)
        own = piece(tile, 8)
        window = around[k, pl.ds(pl.multiple_of(tile * 8, 8), 24), :]
        value = window[8:16]
        above = pltpu.roll(window, 1, 0)[8:16]
        below = pltpu.roll(window, 23, 0)[8:16]
        middle = pl.ds(pl.multiple_of(tile * 8 + spare, 8), 8)
        before = around[jnp.where(k == 0, planes - 1, k - 1), middle, :]
        after = around[jnp.where(k == planes - 1, 0, k + 1), middle, :]
        total = diagonal[k, own, :] * value
        total = total + (low_x[own, :] * (value - above) - high_x[own, :] * (below - value))
        left = pltpu.roll(value, 1, 1)
        right = pltpu.roll(value, full - 1, 1)
        total = total + (low_y[...] * (value - left) - high_y[...] * (right - value))
        total = total + (2.0 * value - before - after)
        image[k, own, :] = total
        return carry + fold(value * total) if last else carry

    bend = lax.fori_loop(0, planes * (rows // 8), operate, nothing, unroll=2)
    if last:
        product = jnp.sum(product, axis=0, keepdims=True)
        bend = jnp.sum(bend, axis=0, keepdims=True)
        aux_ref[...] = jnp.concatenate([nothing[:2], product, bend, nothing[4:]], axis=0)
    image_copy = pltpu.make_async_copy(image, y_ref, late_semaphores.at[1])
    image_copy.start()
    if not last:
        mix_planes(lambda k, i, j: image[k, i, j], mix_ref, ahead_lines, rows)
        send_lines(ahead_lines, basis, sent, out_ref, block, 0, out_semaphores, ahead)
    image_copy.wait()
    wait_all(done)


def turn_lines(stage, last, got, part, operator, basis_z, basis_y, state, chunks):
    planes, rows, full = operator[0].shape
    columns = got.shape[-1]
    block = min(512, full // chunks)
    blocks = full // block
    field_shape = pltpu.HBM((planes, rows, full), jnp.float32)
    edge_shape = pltpu.HBM((planes, spare, full), jnp.float32)
    before = part if chunks > 1 else state
    specs = [scalar, vector] + [anywhere] * 2 + [vector] * 4
    given = [basis_z, got, *far(basis_y, operator[0])] + list(operator[1:])
    if last:
        specs.append(anywhere)
        given += far(state["residual"])
    if stage >= 1:
        specs.append(vector)
        given.append(state["scalars"])
    for name in ("z", "v"):
        if name in before:
            specs += [anywhere] * 2
            given += far(before[name], before["edge_" + name])
    names = ["z", "edge_z", "y"]
    outs = [anywhere] * 3
    shapes = [field_shape, edge_shape, field_shape]
    if last:
        names.append("aux")
        outs.append(vector)
        shapes.append(jax.ShapeDtypeStruct((spare, columns), jnp.float32))
    if stage >= 1:
        names += ["v", "edge_v"]
        outs += [anywhere, anywhere]
        shapes += [field_shape, edge_shape]
    field = pltpu.VMEM((planes, rows, full), jnp.float32)
    edge = pltpu.VMEM((planes, spare, full), jnp.float32)
    scratch = [
        pltpu.VMEM(got.shape, jnp.float32),
        pltpu.VMEM(basis_y.shape, jnp.bfloat16),
        field,
        pltpu.VMEM((2 * planes * (rows + spare), full // chunks), jnp.bfloat16),
        pltpu.VMEM((planes, rows + 2 * spare, full), jnp.float32),
        edge,
        field,
    ]
    if last:
        scratch.append(field)
    if "z" in before:
        scratch.append(field)
    if stage >= 1:
        scratch += [field, edge]
    if not last:
        sent = (planes, full // chunks // columns, rows, columns)
        names.append("sent")
        outs.append(anywhere)
        shapes.append(pltpu.HBM(sent, jnp.float32))
        scratch += [pltpu.VMEM((2 * planes * rows, full), jnp.bfloat16), pltpu.VMEM(sent, jnp.float32)]
    scratch += [
        pltpu.SemaphoreType.DMA((planes,)),
        pltpu.SemaphoreType.DMA((blocks, 6)),
        pltpu.SemaphoreType.DMA((6,)),
    ]
    if not last:
        scratch += [pltpu.SemaphoreType.DMA((blocks // chunks, 1))] * 2
    results = pl.pallas_call(
        functools.partial(turn_kernel, stage, last, block, chunks),
        in_specs=specs,
        out_specs=outs,
        out_shape=shapes,
        scratch_shapes=scratch,
        compiler_params=params(40),
    )(*given)
    return dict(zip(names, results))


def first_kernel(
    rows, velocity_ref, weight_ref, code_ref, above_ref, below_ref, side_ref, half_x_ref, half_y_ref,
    source_ref, predicted_ref, fields, moved, kept, semaphores, late_semaphores,
):
    planes, count, span = weight_ref.shape
    wide = half_y_ref.shape[1]
    pad = 16
    middle = count // 16 * 8
    early, late = [], []
    for channel in range(5):
        if channel < 3:
            main = velocity_ref.at[channel]
        else:
            main = weight_ref if channel == 3 else code_ref
        target = fields.at[channel]
        early.append((main.at[:, :middle], target.at[:, pad : pad + middle, :span]))
        early.append((above_ref.at[channel], target.at[:, pad - 8 : pad, :span]))
        early.append((below_ref.at[channel], target.at[:, pad + count : pad + count + 8, :span]))
        early.append((side_ref.at[channel], target.at[:, :, span:]))
        late.append((main.at[:, middle:], target.at[:, pad + middle : pad + count, :span]))
    early = start_all(early, semaphores)
    late = start_all(late, late_semaphores)
    wait_all(early)
    tiles = count // 8 + 2
    half_y = half_y_ref[...]

    def lane_slope(value):
        return pltpu.roll(value, wide - 1, 1) - pltpu.roll(value, 1, 1)

    def advance(index, carry):
        tile = index // planes
        k = index - tile * planes
        start = pl.multiple_of(8 + tile * 8, 8)
        window = pl.ds(pl.multiple_of(start - 8, 8), 24)
        own = pl.ds(start, 8)
        before = jnp.where(k == 0, planes - 1, k - 1)
        after = jnp.where(k == planes - 1, 0, k + 1)
        half_x = half_x_ref[own, :]
        first = fields[0, k, window, :]
        second = fields[1, k, own, :]
        third_before = fields[2, before, own, :]
        third_after = fields[2, after, own, :]
        weight = fields[3, k, own, :]
        for c in range(3):
            value = first if c == 0 else fields[c, k, window, :]
            along = first * value
            center = value[8:16]
            total = half_x * (pltpu.roll(along, 23, 0)[8:16] - pltpu.roll(along, 1, 0)[8:16])
            total = total + half_y * lane_slope(second * center)
            total = total + 0.5 * (third_after * fields[c, after, own, :] - third_before * fields[c, before, own, :])
            share = weight * total
            moved[c, k, own, :] = share
            kept[c, k, own, :] = total - share
        return carry

    safe = planes * (middle // 8)
    lax.fori_loop(0, safe, advance, 0, unroll=4)
    wait_all(late)
    lax.fori_loop(safe, planes * tiles, advance, 0, unroll=4)

    def settle(index, carry):
        k = index // tiles
        start = pl.multiple_of(8 + (index - k * tiles) * 8, 8)
        window = pl.ds(pl.multiple_of(start - 8, 8), 24)
        own = pl.ds(start, 8)
        code = fields[4, k, window, :]
        inside_x = half_x_ref[own, :] > 0.0
        inside_y = half_y > 0.0
        for c in range(3):
            share = moved[c, k, window, :]
            received = pltpu.roll(jnp.where(code == 1.0, share, 0.0), 1, 0)[8:16] + pltpu.roll(jnp.where(code == 2.0, share, 0.0), 23, 0)[8:16]
            center = share[8:16]
            middle = code[8:16]
            received = received + pltpu.roll(jnp.where(middle == 3.0, center, 0.0), 1, 1)
            received = received + pltpu.roll(jnp.where(middle == 4.0, center, 0.0), wide - 1, 1)
            result = fields[c, k, own, :] - time_step * (kept[c, k, own, :] + received)
            if c == 0:
                result = jnp.where(inside_x, result, 0.0)
            if c == 1:
                result = jnp.where(inside_y, result, 0.0)
            kept[c, k, own, :] = result
        return carry

    lax.fori_loop(0, planes * tiles, settle, 0, unroll=4)
    done = start_all(
        [(kept.at[c, :, pad : pad + count, :span], predicted_ref.at[c]) for c in range(3)], late_semaphores
    )
    inner = count // 8
    group = rows // 8

    def collect(index, carry):
        k = index // inner
        tile = index - k * inner
        start = pl.multiple_of(pad + tile * 8, 8)
        window = pl.ds(pl.multiple_of(start - 8, 8), 24)
        own = pl.ds(start, 8)
        before = jnp.where(k == 0, planes - 1, k - 1)
        after = jnp.where(k == planes - 1, 0, k + 1)
        first = kept[0, k, window, :]
        second = kept[1, k, own, :]
        total = half_x_ref[own, :] * (pltpu.roll(first, 23, 0)[8:16] - pltpu.roll(first, 1, 0)[8:16])
        total = total + half_y * lane_slope(second)
        total = total + 0.5 * (kept[2, after, own, :] - kept[2, before, own, :])
        target = tile // group
        spot = pl.multiple_of((tile - target * group) * 8, 8)
        source_ref[target, k, pl.ds(spot, 8), :] = -total[:, :span]
        return carry

    lax.fori_loop(0, planes * inner, collect, 0, unroll=8)
    wait_all(done)


def first_step(velocity, weight, code, above, below, side, half_x, half_y, rows):
    planes, count, span = weight.shape
    tall, wide = half_x.shape[0], half_y.shape[1]
    return pl.pallas_call(
        functools.partial(first_kernel, rows),
        in_specs=[anywhere] * 6 + [vector] * 2,
        out_specs=[vector, anywhere],
        out_shape=[
            jax.ShapeDtypeStruct((count // rows, planes, rows, span), jnp.float32),
            jax.ShapeDtypeStruct((3, planes, count, span), jnp.float32),
        ],
        scratch_shapes=[
            pltpu.VMEM((5, planes, tall, wide), jnp.float32),
            pltpu.VMEM((3, planes, tall, wide), jnp.float32),
            pltpu.VMEM((3, planes, tall, wide), jnp.float32),
            pltpu.SemaphoreType.DMA((20,)),
            pltpu.SemaphoreType.DMA((5,)),
        ],
        compiler_params=params(48),
    )(*far(velocity, weight, code, above, below, side), half_x, half_y)


def neighbours(axis, last, leading):
    size = lax.axis_size(axis)
    up = [(i, i + 1) for i in range(size - 1)]
    down = [(i + 1, i) for i in range(size - 1)]
    return lax.ppermute(last, axis, up), lax.ppermute(leading, axis, down)


def extended_1(value, start, count, before, after):
    padded = jnp.pad(value, (before, after))
    return lax.dynamic_slice_in_dim(padded, start, count + before + after)


def lanes_sum(value, columns):
    return jnp.sum(value.reshape(-1, value.shape[-1] // columns, columns), axis=(0, 1))


def add_kernel(numbers_ref, sums_ref, pressure_ref, direction_ref, lifted_ref, out_ref):
    total = jnp.sum(jnp.sum(sums_ref[...], axis=0), axis=1, keepdims=True)
    turn = total[2:3] / numbers_ref[0:1, 0:1]
    length = total[2:3] / (total[3:4] - turn * turn * numbers_ref[1:2, 0:1])
    for k in range(pressure_ref.shape[0]):
        direction = lifted_ref[k] + turn * direction_ref[k]
        out_ref[0, k] = pressure_ref[k] + length * direction


def add_step(numbers, sums, pressure, direction, lifted, pieces):
    planes, rows, full = pressure.shape
    span = full // pieces
    field = pl.BlockSpec((planes, rows, span), lambda n: (0, 0, n))
    return pl.pallas_call(
        add_kernel,
        grid=(pieces,),
        in_specs=[vector] * 2 + [field] * 3,
        out_specs=pl.BlockSpec((1, planes, rows, span), lambda n: (n, 0, 0, 0)),
        out_shape=pltpu.HBM((pieces, planes, rows, span), jnp.float32),
        compiler_params=params(20),
    )(numbers, sums, pressure, direction, lifted)


def correct_kernel(
    predicted_ref, own_ref, previous_ref, next_ref, above_ref, below_ref, left_ref, right_ref,
    half_x_ref, half_y_ref, corrected_ref, pressure_ref,
):
    n = pl.program_id(0)
    last = pl.num_programs(0) - 1
    _, planes, rows, _ = own_ref.shape
    for k in range(planes):
        value = own_ref[0, k]
        above = jnp.where(n == 0, above_ref[k], previous_ref[0, k, rows - 1 : rows, :])
        below = jnp.where(n == last, below_ref[k], next_ref[0, k, 0:1, :])
        rising = jnp.concatenate([value[1:], below], axis=0) - jnp.concatenate([above, value[:-1]], axis=0)
        ahead = jnp.concatenate([value[:, 1:], right_ref[0, k]], axis=1)
        behind = jnp.concatenate([left_ref[0, k], value[:, :-1]], axis=1)
        across = own_ref[0, (k + 1) % planes] - own_ref[0, (k - 1) % planes]
        pressure_ref[:, k, :] = value
        corrected_ref[0, :, k, :] = predicted_ref[0, k] - half_x_ref[...] * rising
        corrected_ref[1, :, k, :] = predicted_ref[1, k] - half_y_ref[...] * (ahead - behind)
        corrected_ref[2, :, k, :] = predicted_ref[2, k] - 0.5 * across


def correct_step(predicted, pressure, above, below, left, right, half_x, half_y):
    pieces, planes, rows, span = pressure.shape
    count = pieces * rows
    own = lambda shift: pl.BlockSpec(
        (1, planes, rows, span), lambda n: (jnp.clip(n + shift, 0, pieces - 1), 0, 0, 0)
    )
    column = pl.BlockSpec((1, planes, rows, 1), lambda n: (n, 0, 0, 0))
    return pl.pallas_call(
        correct_kernel,
        grid=(pieces,),
        in_specs=[
            pl.BlockSpec((3, planes, rows, span), lambda n: (0, 0, n, 0)),
            own(0),
            own(-1),
            own(1),
            vector,
            vector,
            column,
            column,
            pl.BlockSpec((rows, 1), lambda n: (n, 0)),
            vector,
        ],
        out_specs=[
            pl.BlockSpec((3, rows, planes, span), lambda n: (0, n, 0, 0)),
            pl.BlockSpec((rows, planes, span), lambda n: (n, 0, 0)),
        ],
        out_shape=[
            jax.ShapeDtypeStruct((3, count, planes, span), jnp.float32),
            jax.ShapeDtypeStruct((count, planes, span), jnp.float32),
        ],
        compiler_params=params(28),
    )(predicted, pressure, pressure, pressure, above, below, left, right, half_x, half_y)


def per_device(
    velocity,
    cut_flags,
    redirect,
    share_weight,
    inverse_dx,
    inverse_dy,
    basis_x,
    basis_y,
    basis_z,
    eigen_x,
    eigen_y,
    eigen_z,
):
    x_parts = lax.axis_size("gx")
    y_parts = lax.axis_size("gy")
    devices = x_parts * y_parts
    x_index = lax.axis_index("gx")
    y_index = lax.axis_index("gy")
    own = x_index * y_parts + y_index
    x_count, planes, y_count = velocity.shape[1:]
    full_x = x_count * x_parts
    full_y = y_count * y_parts
    rows = full_x // devices
    columns = planes * full_y // devices
    chunks = 2 if columns % 256 == 0 else 1
    columns = columns // chunks
    column_blocks = devices // planes
    inverse_x = lax.dynamic_slice_in_dim(inverse_dx, x_index * x_count, x_count)
    inverse_y = lax.dynamic_slice_in_dim(inverse_dy, y_index * y_count, y_count)
    flags = cut_flags.astype(jnp.float32)
    code = (cut_flags * (redirect + 1)).astype(jnp.float32)
    weight = share_weight * flags
    reach = 3

    def edge_rows(part):
        cut = cut_flags[part]
        share = share_weight[part] * cut.astype(jnp.float32)
        target = (cut * (redirect[part] + 1)).astype(jnp.float32)
        return jnp.concatenate([velocity[:, part], share[None], target[None]])

    above, below = neighbours("gx", edge_rows(slice(x_count - reach, None)), edge_rows(slice(0, reach)))
    velocity = velocity.transpose(0, 2, 1, 3)
    weight = weight.transpose(1, 0, 2)
    code = code.transpose(1, 0, 2)
    above = above.transpose(0, 2, 1, 3)
    below = below.transpose(0, 2, 1, 3)

    def edge_columns(part):
        middle = jnp.concatenate([velocity[..., part], weight[None, ..., part], code[None, ..., part]])
        return jnp.concatenate([above[..., part], middle, below[..., part]], axis=2).swapaxes(2, 3)

    left, right = neighbours("gy", edge_columns(slice(y_count - reach, None)), edge_columns(slice(0, reach)))
    left, right = [
        jnp.pad(part, ((0, 0), (0, 0), (0, 0), (16 - reach, 16 - reach))) for part in (left, right)
    ]
    side = jnp.concatenate([right, jnp.zeros((5, planes, 128 - 2 * reach, x_count + 32), jnp.float32), left], axis=2)
    side = side.swapaxes(2, 3)
    above = jnp.pad(above, ((0, 0), (0, 0), (8 - reach, 0), (0, 0)))
    below = jnp.pad(below, ((0, 0), (0, 0), (0, 8 - reach), (0, 0)))
    half_x = 0.5 * extended_1(inverse_dx, x_index * x_count, x_count, 16, 16)[:, None]
    half_y = 0.5 * extended_1(inverse_dy, y_index * y_count, y_count, reach, reach)
    half_y = jnp.concatenate([half_y[reach:], jnp.zeros((128 - 2 * reach,), jnp.float32), half_y[:reach]])[None]
    source, predicted = first_step(velocity, weight, code, above, below, side, half_x, half_y, rows)
    diagonal = (cell_shift + cut_shift * flags).reshape(y_parts, rows, planes, y_count).transpose(0, 2, 1, 3)
    diagonal = lax.all_to_all(diagonal, "gy", 0, 0, tiled=True)
    source, diagonal = lax.optimization_barrier((source, diagonal))
    source = lax.all_to_all(source, "gy", 0, 0, tiled=True)
    source, basis_xt = lax.optimization_barrier((source, basis_x.T))
    diagonal = diagonal.transpose(1, 2, 0, 3).reshape(planes, rows, full_y)
    whole_x = jnp.pad(inverse_dx, 1)
    face_x = lax.dynamic_slice_in_dim(whole_x[:-1] * whole_x[1:], own * rows, rows + 1)
    whole_y = jnp.pad(inverse_dy, 1)
    face_y = whole_y[:-1] * whole_y[1:]
    operator = (diagonal, face_x[:-1, None], face_x[1:, None], face_y[None, :-1], face_y[None, 1:])
    along = eigen_x[:, None]
    other = [
        (
            lax.dynamic_slice_in_dim(
                eigen_y, full_y // chunks * chunk + (own % column_blocks) * columns, columns
            )
            + lax.dynamic_slice_in_dim(eigen_z, own // column_blocks, 1)
        )[None]
        for chunk in range(chunks)
    ]

    def apply(stage, field, sent, aux, state):
        sents = [sent] + [
            more_lines(field, basis_z, basis_y, columns, chunks, chunk) for chunk in range(1, chunks)
        ]
        gots = []
        for chunk, sent in enumerate(sents):
            sent = sent.reshape(devices, rows, columns)
            got = lax.all_to_all(sent, both, 0, 0, tiled=True).reshape(full_x, columns)
            given = aux if chunk == 0 else jnp.zeros((spare, columns), jnp.float32)
            got = column_lines(got, given, basis_xt, basis_x, along, other[chunk], rows)
            gots.append(lax.all_to_all(got, both, 0, 0, tiled=True))
        if stage > 0:
            state["scalars"] = numbers_of(gots[0][:, rows // 4], state.get("scalars"))
        part = None
        if chunks > 1:
            part = part_lines(stage, gots[0], basis_z, basis_y, rows, chunks, state)
        return gots[-1], part

    def numbers_of(sums, numbers):
        product = jnp.sum(sums[:, 2])
        bend = jnp.sum(sums[:, 3])
        turn = jnp.zeros_like(product)
        if numbers is not None:
            turn = product / numbers[0, 0]
            bend = bend - turn * turn * numbers[1, 0]
        numbers = jnp.stack([product, bend, product / bend, turn])
        return jnp.broadcast_to(jnp.pad(numbers, (0, 4))[:, None], (8, 128))

    residual, sent = start_lines(source, basis_z, basis_y, columns, chunks)
    state = {}
    got, part = apply(0, residual, sent, jnp.zeros((spare, columns), jnp.float32), state)
    state |= turn_lines(0, False, got, part, operator, basis_z, basis_y, state, chunks)
    for stage in range(1, ITERS):
        partial = [lanes_sum(residual * state["z"], columns), lanes_sum(state["z"] * state["y"], columns)]
        aux = jnp.pad(jnp.stack(partial), ((2, spare - 4), (0, 0)))
        got, part = apply(stage, state["y"], state["sent"], aux, state)
        length, turn = state["scalars"][2, 0], state["scalars"][3, 0]
        if stage == 1:
            direction, image = state["z"], state["y"]
            pressure = length * direction
        else:
            direction = state["z"] + turn * direction
            image = state["y"] + turn * image
            pressure = pressure + length * direction
        residual = residual - length * image
        state["residual"] = residual
        last = stage + 1 == ITERS
        state |= turn_lines(stage, last, got, part, operator, basis_z, basis_y, state, chunks)
    sums = jnp.broadcast_to(state["aux"][None], (devices, spare, columns))
    sums = lax.all_to_all(sums, both, 0, 0, tiled=True)
    pressure = add_step(state["scalars"], sums, pressure, direction, state["z"], y_parts)
    pressure = lax.all_to_all(pressure, "gy", 0, 0, tiled=True)
    above, below = neighbours("gx", pressure[-1, :, -1:], pressure[0, :, :1])
    left, right = neighbours("gy", pressure[..., -1], pressure[..., 0])
    half_x = 0.5 * inverse_x[:, None]
    half_y = 0.5 * inverse_y[None]
    corrected, pressure = correct_step(
        predicted, pressure, above, below, left[..., None], right[..., None], half_x, half_y
    )
    return corrected, pressure


def solution(mesh):
    in_specs = (
        P(None, "gx", None, "gy"),
        P("gx", None, "gy"),
        P("gx", None, "gy"),
        P("gx", None, "gy"),
        P(),
        P(),
        P(),
        P(),
        P(),
        P(),
        P(),
        P(),
    )
    out_specs = (P(None, "gx", None, "gy"), P("gx", None, "gy"))
    return jax.shard_map(
        per_device, mesh=mesh, in_specs=in_specs, out_specs=out_specs, check_vma=False
    )
```

```python
import functools

import jax
import jax.numpy as jnp
from jax import lax
from jax.experimental import pallas as pl
from jax.experimental.pallas import tpu as pltpu
from jax.sharding import PartitionSpec as P

ITERS = 4


time_step = 0.25
cell_shift = 0.05
cut_shift = 0.45
both = ("gx", "gy")
spare = 8


def halves(value):
    high = value.astype(jnp.bfloat16)
    low = (value - high.astype(jnp.float32)).astype(jnp.bfloat16)
    return high, low


def params(mebibytes):
    return pltpu.CompilerParams(vmem_limit_bytes=mebibytes * 1024 * 1024)


def mix_planes(read, mix_ref, lines, rows):
    planes = mix_ref.shape[0]
    width = lines.shape[1]
    lane = 512 if width % 512 == 0 else width
    half = planes * rows

    def strip(index, carry):
        start = pl.multiple_of(index * 16, 16)
        for left in range(0, width, lane):
            fields = [read(k, pl.ds(start, 16), pl.ds(left, lane)) for k in range(planes)]
            for m in range(planes):
                total = fields[0] * mix_ref[0, m]
                for k in range(1, planes):
                    total = total + fields[k] * mix_ref[k, m]
                high, low = halves(total)
                lines[pl.ds(m * rows + start, 16), pl.ds(left, lane)] = high
                lines[pl.ds(half + m * rows + start, 16), pl.ds(left, lane)] = low
        return carry

    lax.fori_loop(0, rows // 16, strip, 0)


anywhere = pl.BlockSpec(memory_space=pl.ANY)
vector = pl.BlockSpec(memory_space=pltpu.VMEM)
scalar = pl.BlockSpec(memory_space=pltpu.SMEM)


class Stream:
    def __init__(self, pairs, count, semaphores):
        self.pairs = pairs
        self.count = count
        self.semaphores = semaphores

    def copies(self, n):
        pairs = self.pairs(n)
        return [
            pltpu.make_async_copy(given, target, self.semaphores.at[n, index])
            for index, (given, target) in enumerate(pairs)
        ]

    def start(self, n):
        for copy in self.copies(n):
            copy.start()

    def begin(self):
        for n in range(min(2, self.count)):
            self.start(n)

    def take(self, n):
        for copy in self.copies(n):
            copy.wait()

        @pl.when(n + 2 < self.count)
        def _():
            self.start(n + 2)

    def end(self):
        def step(n, carry):
            for copy in self.copies(n):
                copy.wait()
            return carry

        lax.fori_loop(0, self.count, step, 0)


def start_all(pairs, semaphores):
    copies = [
        pltpu.make_async_copy(given, target, semaphores.at[index])
        for index, (given, target) in enumerate(pairs)
    ]
    for copy in copies:
        copy.start()
    return copies


def wait_all(copies):
    for copy in copies:
        copy.wait()


def far(*values):
    return [pltpu.with_memory_space_constraint(value, pltpu.HBM) for value in values]


def piece(index, size):
    return pl.ds(pl.multiple_of(index * size, size), size)


def send_lines(lines, basis, sent, out_ref, block, chunk, semaphores, stream=None):
    planes, all_parts, rows, columns = sent.shape
    half = planes * rows
    parts = block // columns
    blocks = all_parts // parts
    out = Stream(
        lambda n: [(sent.at[:, pl.ds(n * parts, parts)], out_ref.at[:, pl.ds(n * parts, parts)])],
        blocks,
        semaphores,
    )

    def step(n, carry):
        if stream is not None:
            stream.take(n)
        result = jnp.dot(lines[...], basis[:, piece(chunk * blocks + n, block)], preferred_element_type=jnp.float32)
        result = result[:half] + result[half:]
        for m in range(planes):
            for part in range(parts):
                sent[m, n * parts + part] = result[
                    m * rows : (m + 1) * rows, part * columns : (part + 1) * columns
                ]
        out.start(n)
        return carry

    lax.fori_loop(0, blocks, step, 0)
    out.end()


def column_stream(basis_ref, basis, block, chunk, blocks, semaphores):
    def pairs(n):
        own = piece(chunk * blocks + n, block)
        return [(basis_ref.at[:, own], basis.at[:, own])]

    return Stream(pairs, blocks, semaphores)


def start_kernel(
    block, mix_ref, field_ref, basis_ref, kept_ref, out_ref,
    field, basis, lines, sent, semaphores, basis_semaphores, out_semaphores,
):
    pieces, planes, rows, span = field_ref.shape
    given = [(field_ref.at[n], field.at[:, :, n * span : (n + 1) * span]) for n in range(pieces)]
    given = start_all(given, semaphores)
    stream = column_stream(basis_ref, basis, block, 0, basis_semaphores.shape[0], basis_semaphores)
    stream.begin()
    wait_all(given)
    kept = pltpu.make_async_copy(field, kept_ref, semaphores.at[pieces])
    kept.start()
    mix_planes(lambda k, i, j: field[k, i, j], mix_ref, lines, rows)
    send_lines(lines, basis, sent, out_ref, block, 0, out_semaphores, stream)
    kept.wait()


def start_lines(field, basis_z, basis_y, columns, chunks):
    pieces, planes, rows, span = field.shape
    full = pieces * span
    block = min(256, full // chunks)
    blocks = full // chunks // block
    sent = (planes, full // chunks // columns, rows, columns)
    return pl.pallas_call(
        functools.partial(start_kernel, block),
        in_specs=[scalar, vector, anywhere],
        out_specs=[anywhere] * 2,
        out_shape=[
            pltpu.HBM((planes, rows, full), jnp.float32),
            pltpu.HBM(sent, jnp.float32),
        ],
        scratch_shapes=[
            pltpu.VMEM((planes, rows, full), jnp.float32),
            pltpu.VMEM(basis_y.shape, jnp.bfloat16),
            pltpu.VMEM((2 * planes * rows, full), jnp.bfloat16),
            pltpu.VMEM(sent, jnp.float32),
            pltpu.SemaphoreType.DMA((pieces + 1,)),
            pltpu.SemaphoreType.DMA((blocks, 1)),
            pltpu.SemaphoreType.DMA((blocks, 1)),
        ],
        compiler_params=params(24),
    )(basis_z, field, *far(basis_y))


def more_kernel(
    block, chunk, mix_ref, field_ref, basis_ref, out_ref, field, basis, lines, sent, semaphore, basis_semaphores, out_semaphores
):
    given = pltpu.make_async_copy(field_ref, field, semaphore)
    given.start()
    stream = column_stream(basis_ref, basis, block, chunk, basis_semaphores.shape[0], basis_semaphores)
    stream.begin()
    given.wait()
    mix_planes(lambda k, i, j: field[k, i, j], mix_ref, lines, field.shape[1])
    send_lines(lines, basis, sent, out_ref, block, chunk, out_semaphores, stream)


def more_lines(field, basis_z, basis_y, columns, chunks, chunk):
    planes, rows, full = field.shape
    block = min(256, full // chunks)
    blocks = full // chunks // block
    sent = (planes, full // chunks // columns, rows, columns)
    return pl.pallas_call(
        functools.partial(more_kernel, block, chunk),
        in_specs=[scalar, anywhere, anywhere],
        out_specs=anywhere,
        out_shape=pltpu.HBM(sent, jnp.float32),
        scratch_shapes=[
            pltpu.VMEM(field.shape, jnp.float32),
            pltpu.VMEM(basis_y.shape, jnp.bfloat16),
            pltpu.VMEM((2 * planes * rows, full), jnp.bfloat16),
            pltpu.VMEM(sent, jnp.float32),
            pltpu.SemaphoreType.DMA,
            pltpu.SemaphoreType.DMA((blocks, 1)),
            pltpu.SemaphoreType.DMA((blocks, 1)),
        ],
        compiler_params=params(24),
    )(basis_z, *far(field, basis_y))


def take_lines(got, lines, planes, rows):
    devices, _, _, columns = got.shape
    parts = devices // planes
    half = planes * (rows + spare)
    main = planes * rows
    edge_rows = lax.broadcasted_iota(jnp.int32, (spare, columns), 0) < 2
    for part in range(parts):
        lanes = slice(part * columns, (part + 1) * columns)
        edges = []
        for m in range(planes):
            high, low = halves(got[m * parts + part, : rows // 4].reshape(rows, columns))
            lines[m * rows : (m + 1) * rows, lanes] = high
            lines[half + m * rows : half + (m + 1) * rows, lanes] = low
            edge = got[m * parts + part, rows // 4]
            edges.append(jnp.where(edge_rows, jnp.concatenate([edge, edge], axis=0), 0.0))
        high, low = halves(jnp.concatenate(edges, axis=0))
        lines[main:half, lanes] = high
        lines[half + main :, lanes] = low


def mixed_back(result, mix_ref, k, rows):
    planes = mix_ref.shape[0]
    main = planes * rows
    value = result[:rows] * mix_ref[k, 0]
    edge = result[main : main + spare] * mix_ref[k, 0]
    for m in range(1, planes):
        value = value + result[m * rows : (m + 1) * rows] * mix_ref[k, m]
        edge = edge + result[main + m * spare : main + (m + 1) * spare] * mix_ref[k, m]
    return value, edge


def part_kernel(stage, rows, block, *refs):
    refs = list(refs)
    take = lambda: refs.pop(0)
    mix_ref, got_ref, basis_ref = take(), take(), take()
    if stage >= 1:
        scalars_ref, old_z, old_edge_z = take(), take(), take()
    if stage >= 2:
        old_v, old_edge_v = take(), take()
    out_refs = [take() for _ in range(4 if stage >= 1 else 2)]
    got, basis, lines = take(), take(), take()
    outs = [take() for _ in range(4 if stage >= 1 else 2)]
    given_semaphores, semaphores, out_semaphores = take(), take(), take()
    z, edge_z = outs[:2]
    planes = mix_ref.shape[0]
    parts = got.shape[0] // planes
    width = lines.shape[1]
    half = planes * (rows + spare)
    blocks = basis.shape[0] // block
    groups = [slice(m * parts, (m + 1) * parts) for m in range(planes)]
    given = start_all([(got_ref.at[group], got.at[group]) for group in groups], given_semaphores)
    fields = []
    if stage >= 1:
        v, edge_v = outs[2:]
        fields += [(old_z, z), (old_edge_z, edge_z)]
    if stage >= 2:
        fields += [(old_v, v), (old_edge_v, edge_v)]

    def needed(n):
        own = piece(n, block)
        pairs = [(basis_ref.at[own, :width], basis.at[own])]
        return pairs + [(old.at[:, :, own], target.at[:, :, own]) for old, target in fields]

    def made(n):
        own = piece(n, block)
        return [(out.at[:, :, own], out_ref.at[:, :, own]) for out, out_ref in zip(outs, out_refs)]

    stream = Stream(needed, blocks, semaphores)
    sink = Stream(made, blocks, out_semaphores)
    stream.begin()
    wait_all(given)
    take_lines(got, lines, planes, rows)

    def step(n, carry):
        stream.take(n)
        lanes = piece(n, block)
        result = lax.dot_general(
            lines[...], basis[lanes, :], (((1,), (1,)), ((), ())), preferred_element_type=jnp.float32
        )
        result = result[:half] + result[half:]
        if stage >= 1:
            length = scalars_ref[2:3, 0:1]
            turn = scalars_ref[3:4, 0:1]
        for k in range(planes):
            value, edge = mixed_back(result, mix_ref, k, rows)
            if stage >= 1:
                if stage >= 2:
                    value = value + turn * v[k, :, lanes]
                    edge = edge + turn * edge_v[k, :, lanes]
                v[k, :, lanes] = value
                edge_v[k, :, lanes] = edge
                value = z[k, :, lanes] - length * value
                edge = edge_z[k, :, lanes] - length * edge
            z[k, :, lanes] = value
            edge_z[k, :, lanes] = edge
        sink.start(n)
        return carry

    lax.fori_loop(0, blocks, step, 0)
    sink.end()


def part_lines(stage, got, basis_z, basis_y, rows, chunks, state):
    planes = basis_z.shape[0]
    full = basis_y.shape[0]
    block = min(256, full)
    half = planes * (rows + spare)
    field, edge = (planes, rows, full), (planes, spare, full)
    names = ["z", "edge_z"]
    given = [basis_z, got, *far(basis_y)]
    specs = [scalar, vector, anywhere]
    if stage >= 1:
        names += ["v", "edge_v"]
        given += [state["scalars"], *far(state["z"], state["edge_z"])]
        specs += [vector, anywhere, anywhere]
    if stage >= 2:
        given += far(state["v"], state["edge_v"])
        specs += [anywhere, anywhere]
    shapes = [field, edge] * (len(names) // 2)
    results = pl.pallas_call(
        functools.partial(part_kernel, stage, rows, block),
        in_specs=specs,
        out_specs=[anywhere] * len(names),
        out_shape=[pltpu.HBM(shape, jnp.float32) for shape in shapes],
        scratch_shapes=[
            pltpu.VMEM(got.shape, jnp.float32),
            pltpu.VMEM((full, full // chunks), jnp.bfloat16),
            pltpu.VMEM((2 * half, full // chunks), jnp.bfloat16),
        ]
        + [pltpu.VMEM(shape, jnp.float32) for shape in shapes]
        + [
            pltpu.SemaphoreType.DMA((planes,)),
            pltpu.SemaphoreType.DMA((full // block, 5)),
            pltpu.SemaphoreType.DMA((full // block, 4)),
        ],
        compiler_params=params(28),
    )(*given)
    return dict(zip(names, results))


def column_kernel(
    rows, block, field_ref, aux_ref, ahead_ref, back_ref, along_ref, other_ref, out_ref,
    field, ahead, back, lines, spectral, buffer, given_semaphores, semaphores, out_semaphores,
):
    full, columns = field_ref.shape
    blocks = full // block
    group = block // rows
    devices = full // rows
    given = Stream(
        lambda n: [(field_ref.at[piece(n, block)], field.at[piece(n, block)])], blocks, given_semaphores
    )
    aheads = Stream(
        lambda n: [(ahead_ref.at[piece(n, block)], ahead.at[piece(n, block)])], blocks, semaphores.at[0]
    )
    backs = Stream(
        lambda n: [(back_ref.at[piece(n, block)], back.at[piece(n, block)])], blocks, semaphores.at[1]
    )
    out = Stream(
        lambda n: [(buffer.at[pl.ds(n * group, group)], out_ref.at[pl.ds(n * group, group)])],
        blocks,
        out_semaphores,
    )
    for n in range(blocks):
        given.start(n)
    aheads.begin()
    given.end()

    def strip(index, carry):
        own = piece(index, 64)
        high, low = halves(field[own, :])
        lines[own, :columns] = high
        lines[own, columns:] = low
        return carry

    lax.fori_loop(0, full // 64, strip, 0, unroll=4)

    def forth(n, carry):
        aheads.take(n)

        @pl.when(n == blocks - 1)
        def _():
            backs.begin()

        own = piece(n, block)
        result = jnp.dot(ahead[own, :], lines[...], preferred_element_type=jnp.float32)
        result = result[:, :columns] + result[:, columns:]
        high, low = halves(result / (along_ref[own, :] + other_ref[...]))
        spectral[own, :columns] = high
        spectral[own, columns:] = low
        return carry

    lax.fori_loop(0, blocks, forth, 0)

    def reverse(n, carry):
        backs.take(n)
        result = jnp.dot(back[piece(n, block), :], spectral[...], preferred_element_type=jnp.float32)
        result = result[:, :columns] + result[:, columns:]
        for part in range(group):
            own = result[part * rows : (part + 1) * rows]
            buffer[n * group + part, : rows // 4] = own.reshape(rows // 4, 4, columns)
        return carry

    lax.fori_loop(0, blocks, reverse, 0)
    rest = aux_ref[2:4, :]

    def close(n, carry):
        for part in range(group):
            own = n * group + part
            above = buffer[jnp.maximum(own - 1, 0), rows // 4 - 1, 3:4, :]
            above = jnp.where(own > 0, above, 0.0)
            below = buffer[jnp.minimum(own + 1, devices - 1), 0, 0:1, :]
            below = jnp.where(own + 1 < devices, below, 0.0)
            buffer[own, rows // 4] = jnp.concatenate([above, below, rest], axis=0)
        out.start(n)
        return carry

    lax.fori_loop(0, blocks, close, 0)
    out.end()


def column_lines(field, aux, basis_xt, basis_x, along, other, rows):
    full, columns = field.shape
    block = min(512, full)
    devices = full // rows
    return pl.pallas_call(
        functools.partial(column_kernel, rows, block),
        in_specs=[vector, vector, anywhere, anywhere, vector, vector],
        out_specs=anywhere,
        out_shape=pltpu.HBM((devices, rows // 4 + 1, 4, columns), jnp.float32),
        scratch_shapes=[
            pltpu.VMEM((full, columns), jnp.float32),
            pltpu.VMEM((full, full), jnp.bfloat16),
            pltpu.VMEM((full, full), jnp.bfloat16),
            pltpu.VMEM((full, 2 * columns), jnp.bfloat16),
            pltpu.VMEM((full, 2 * columns), jnp.bfloat16),
            pltpu.VMEM((devices, rows // 4 + 1, 4, columns), jnp.float32),
            pltpu.SemaphoreType.DMA((full // block, 1)),
            pltpu.SemaphoreType.DMA((2, full // block, 1)),
            pltpu.SemaphoreType.DMA((full // block, 1)),
        ],
        compiler_params=params(28),
    )(field, aux, *far(basis_xt, basis_x), along, other)


def turn_kernel(stage, last, block, chunks, *refs):
    refs = list(refs)
    take = lambda: refs.pop(0)
    mix_ref, got_ref, basis_ref = take(), take(), take()
    has_z = stage >= 1 or chunks > 1
    has_v = stage >= 2 or (stage >= 1 and chunks > 1)
    diagonal_ref, low_x, high_x, low_y, high_y = take(), take(), take(), take(), take()
    residual_ref = take() if last else None
    scalars_ref = take() if stage >= 1 else None
    if has_z:
        old_z, old_edge_z = take(), take()
    if has_v:
        old_v, old_edge_v = take(), take()
    z_ref, edge_z_ref, y_ref = take(), take(), take()
    aux_ref = take() if last else None
    if stage >= 1:
        v_ref, edge_v_ref = take(), take()
    if not last:
        out_ref = take()
    got, basis, diagonal, lines, around, edge_z, image = [take() for _ in range(7)]
    residual = take() if last else None
    z = take() if has_z else None
    if stage >= 1:
        v, edge_v = take(), take()
    if not last:
        ahead_lines, sent = take(), take()
    given_semaphores, semaphores, late_semaphores = take(), take(), take()
    if not last:
        basis_semaphores, out_semaphores = take(), take()
    planes, rows, full = diagonal.shape
    devices, _, _, columns = got.shape
    parts = devices // planes
    half = planes * (rows + spare)
    main = planes * rows
    blocks = full // block
    groups = [slice(m * parts, (m + 1) * parts) for m in range(planes)]
    given = start_all([(got_ref.at[group], got.at[group]) for group in groups], given_semaphores)
    width = full // chunks
    turned = slice(full - width, full)
    fields = [(residual_ref, residual)] if last else []
    if has_z:
        fields += [(old_z, z), (old_edge_z, edge_z)]
    if has_v:
        fields += [(old_v, v), (old_edge_v, edge_v)]

    def needed(n):
        own = piece(n, block)
        pairs = [(basis_ref.at[own, turned], basis.at[own, turned])]
        return pairs + [(old.at[:, :, own], target.at[:, :, own]) for old, target in fields]

    stream = Stream(needed, blocks, semaphores)
    stream.begin()
    wait_all(given)
    take_lines(got, lines, planes, rows)
    def fold(value):
        total = value[:, :columns]
        for left in range(columns, value.shape[1], columns):
            total = total + value[:, left : left + columns]
        return total

    def finish_block(n, carry):
        stream.take(n)
        lanes = piece(n, block)
        result = lax.dot_general(
            lines[...], basis[lanes, turned], (((1,), (1,)), ((), ())), preferred_element_type=jnp.float32
        )
        result = result[:half] + result[half:]
        if stage >= 1:
            length = scalars_ref[2:3, 0:1]
            turn = scalars_ref[3:4, 0:1]
        for k in range(planes):
            value, edge = mixed_back(result, mix_ref, k, rows)
            if chunks > 1:
                scale = 1.0 if stage == 0 else -length
                if stage >= 1:
                    v[k, :, lanes] = v[k, :, lanes] + value
                    edge_v[k, :, lanes] = edge_v[k, :, lanes] + edge
                value = z[k, :, lanes] + scale * value
                edge = edge_z[k, :, lanes] + scale * edge
            elif stage >= 1:
                if stage >= 2:
                    value = value + turn * v[k, :, lanes]
                    edge = edge + turn * edge_v[k, :, lanes]
                v[k, :, lanes] = value
                edge_v[k, :, lanes] = edge
                value = z[k, :, lanes] - length * value
                edge = edge_z[k, :, lanes] - length * edge
            edge_z[k, :, lanes] = edge
            if last:
                shared = fold(residual[k, :, lanes] * value)
                for start in range(0, rows, 8):
                    carry = carry + shared[start : start + 8]
            around[k, spare : spare + rows, lanes] = value
            around[k, spare - 1 : spare, lanes] = edge[0:1]
            around[k, spare + rows : spare + rows + 1, lanes] = edge[1:2]
        return carry

    diagonal_copy = pltpu.make_async_copy(diagonal_ref, diagonal, late_semaphores.at[0])
    diagonal_copy.start()
    nothing = jnp.zeros((8, columns), jnp.float32)
    product = lax.fori_loop(0, blocks, finish_block, nothing)
    done = [(around.at[:, spare : spare + rows], z_ref), (edge_z, edge_z_ref)]
    if stage >= 1:
        done += [(v, v_ref), (edge_v, edge_v_ref)]
    done = start_all(done, late_semaphores.at[2:6])
    ahead = None
    if not last and chunks > 1:
        ahead = column_stream(basis_ref, basis, block, 0, width // block, basis_semaphores)
        ahead.begin()
    diagonal_copy.wait()

    def operate(index, carry):
        k = index // (rows // 8)
        tile = index - k * (rows // 8)
        own = piece(tile, 8)
        window = around[k, pl.ds(pl.multiple_of(tile * 8, 8), 24), :]
        value = window[8:16]
        above = pltpu.roll(window, 1, 0)[8:16]
        below = pltpu.roll(window, 23, 0)[8:16]
        middle = pl.ds(pl.multiple_of(tile * 8 + spare, 8), 8)
        before = around[jnp.where(k == 0, planes - 1, k - 1), middle, :]
        after = around[jnp.where(k == planes - 1, 0, k + 1), middle, :]
        total = diagonal[k, own, :] * value
        total = total + (low_x[own, :] * (value - above) - high_x[own, :] * (below - value))
        left = pltpu.roll(value, 1, 1)
        right = pltpu.roll(value, full - 1, 1)
        total = total + (low_y[...] * (value - left) - high_y[...] * (right - value))
        total = total + (2.0 * value - before - after)
        image[k, own, :] = total
        return carry + fold(value * total) if last else carry

    bend = lax.fori_loop(0, planes * (rows // 8), operate, nothing, unroll=2)
    if last:
        product = jnp.sum(product, axis=0, keepdims=True)
        bend = jnp.sum(bend, axis=0, keepdims=True)
        aux_ref[...] = jnp.concatenate([nothing[:2], product, bend, nothing[4:]], axis=0)
    image_copy = pltpu.make_async_copy(image, y_ref, late_semaphores.at[1])
    image_copy.start()
    if not last:
        mix_planes(lambda k, i, j: image[k, i, j], mix_ref, ahead_lines, rows)
        send_lines(ahead_lines, basis, sent, out_ref, block, 0, out_semaphores, ahead)
    image_copy.wait()
    wait_all(done)


def turn_lines(stage, last, got, part, operator, basis_z, basis_y, state, chunks):
    planes, rows, full = operator[0].shape
    columns = got.shape[-1]
    block = min(512, full // chunks)
    blocks = full // block
    field_shape = pltpu.HBM((planes, rows, full), jnp.float32)
    edge_shape = pltpu.HBM((planes, spare, full), jnp.float32)
    before = part if chunks > 1 else state
    specs = [scalar, vector] + [anywhere] * 2 + [vector] * 4
    given = [basis_z, got, *far(basis_y, operator[0])] + list(operator[1:])
    if last:
        specs.append(anywhere)
        given += far(state["residual"])
    if stage >= 1:
        specs.append(vector)
        given.append(state["scalars"])
    for name in ("z", "v"):
        if name in before:
            specs += [anywhere] * 2
            given += far(before[name], before["edge_" + name])
    names = ["z", "edge_z", "y"]
    outs = [anywhere] * 3
    shapes = [field_shape, edge_shape, field_shape]
    if last:
        names.append("aux")
        outs.append(vector)
        shapes.append(jax.ShapeDtypeStruct((spare, columns), jnp.float32))
    if stage >= 1:
        names += ["v", "edge_v"]
        outs += [anywhere, anywhere]
        shapes += [field_shape, edge_shape]
    field = pltpu.VMEM((planes, rows, full), jnp.float32)
    edge = pltpu.VMEM((planes, spare, full), jnp.float32)
    scratch = [
        pltpu.VMEM(got.shape, jnp.float32),
        pltpu.VMEM(basis_y.shape, jnp.bfloat16),
        field,
        pltpu.VMEM((2 * planes * (rows + spare), full // chunks), jnp.bfloat16),
        pltpu.VMEM((planes, rows + 2 * spare, full), jnp.float32),
        edge,
        field,
    ]
    if last:
        scratch.append(field)
    if "z" in before:
        scratch.append(field)
    if stage >= 1:
        scratch += [field, edge]
    if not last:
        sent = (planes, full // chunks // columns, rows, columns)
        names.append("sent")
        outs.append(anywhere)
        shapes.append(pltpu.HBM(sent, jnp.float32))
        scratch += [pltpu.VMEM((2 * planes * rows, full), jnp.bfloat16), pltpu.VMEM(sent, jnp.float32)]
    scratch += [
        pltpu.SemaphoreType.DMA((planes,)),
        pltpu.SemaphoreType.DMA((blocks, 6)),
        pltpu.SemaphoreType.DMA((6,)),
    ]
    if not last:
        scratch += [pltpu.SemaphoreType.DMA((blocks // chunks, 1))] * 2
    results = pl.pallas_call(
        functools.partial(turn_kernel, stage, last, block, chunks),
        in_specs=specs,
        out_specs=outs,
        out_shape=shapes,
        scratch_shapes=scratch,
        compiler_params=params(40),
    )(*given)
    return dict(zip(names, results))


def first_kernel(
    rows, velocity_ref, weight_ref, code_ref, above_ref, below_ref, side_ref, half_x_ref, half_y_ref,
    source_ref, predicted_ref, fields, moved, kept, semaphores, late_semaphores,
):
    planes, count, span = weight_ref.shape
    wide = half_y_ref.shape[1]
    pad = 16
    middle = count // 16 * 8
    early, late = [], []
    for channel in range(5):
        if channel < 3:
            main = velocity_ref.at[channel]
        else:
            main = weight_ref if channel == 3 else code_ref
        target = fields.at[channel]
        early.append((main.at[:, :middle], target.at[:, pad : pad + middle, :span]))
        early.append((above_ref.at[channel], target.at[:, pad - 8 : pad, :span]))
        early.append((below_ref.at[channel], target.at[:, pad + count : pad + count + 8, :span]))
        early.append((side_ref.at[channel], target.at[:, :, span:]))
        late.append((main.at[:, middle:], target.at[:, pad + middle : pad + count, :span]))
    early = start_all(early, semaphores)
    late = start_all(late, late_semaphores)
    wait_all(early)
    tiles = count // 8 + 2
    half_y = half_y_ref[...]

    def lane_slope(value):
        return pltpu.roll(value, wide - 1, 1) - pltpu.roll(value, 1, 1)

    def advance(index, carry):
        tile = index // planes
        k = index - tile * planes
        start = pl.multiple_of(8 + tile * 8, 8)
        window = pl.ds(pl.multiple_of(start - 8, 8), 24)
        own = pl.ds(start, 8)
        before = jnp.where(k == 0, planes - 1, k - 1)
        after = jnp.where(k == planes - 1, 0, k + 1)
        half_x = half_x_ref[own, :]
        first = fields[0, k, window, :]
        second = fields[1, k, own, :]
        third_before = fields[2, before, own, :]
        third_after = fields[2, after, own, :]
        weight = fields[3, k, own, :]
        for c in range(3):
            value = first if c == 0 else fields[c, k, window, :]
            along = first * value
            center = value[8:16]
            total = half_x * (pltpu.roll(along, 23, 0)[8:16] - pltpu.roll(along, 1, 0)[8:16])
            total = total + half_y * lane_slope(second * center)
            total = total + 0.5 * (third_after * fields[c, after, own, :] - third_before * fields[c, before, own, :])
            share = weight * total
            moved[c, k, own, :] = share
            kept[c, k, own, :] = total - share
        return carry

    safe = planes * (middle // 8)
    lax.fori_loop(0, safe, advance, 0, unroll=8)
    wait_all(late)
    lax.fori_loop(safe, planes * tiles, advance, 0, unroll=8)

    def settle(index, carry):
        k = index // tiles
        start = pl.multiple_of(8 + (index - k * tiles) * 8, 8)
        window = pl.ds(pl.multiple_of(start - 8, 8), 24)
        own = pl.ds(start, 8)
        code = fields[4, k, window, :]
        inside_x = half_x_ref[own, :] > 0.0
        inside_y = half_y > 0.0
        for c in range(3):
            share = moved[c, k, window, :]
            received = pltpu.roll(jnp.where(code == 1.0, share, 0.0), 1, 0)[8:16] + pltpu.roll(jnp.where(code == 2.0, share, 0.0), 23, 0)[8:16]
            center = share[8:16]
            middle = code[8:16]
            received = received + pltpu.roll(jnp.where(middle == 3.0, center, 0.0), 1, 1)
            received = received + pltpu.roll(jnp.where(middle == 4.0, center, 0.0), wide - 1, 1)
            result = fields[c, k, own, :] - time_step * (kept[c, k, own, :] + received)
            if c == 0:
                result = jnp.where(inside_x, result, 0.0)
            if c == 1:
                result = jnp.where(inside_y, result, 0.0)
            kept[c, k, own, :] = result
        return carry

    lax.fori_loop(0, planes * tiles, settle, 0, unroll=8)
    done = start_all(
        [(kept.at[c, :, pad : pad + count, :span], predicted_ref.at[c]) for c in range(3)], late_semaphores
    )
    inner = count // 8
    group = rows // 8

    def collect(index, carry):
        k = index // inner
        tile = index - k * inner
        start = pl.multiple_of(pad + tile * 8, 8)
        window = pl.ds(pl.multiple_of(start - 8, 8), 24)
        own = pl.ds(start, 8)
        before = jnp.where(k == 0, planes - 1, k - 1)
        after = jnp.where(k == planes - 1, 0, k + 1)
        first = kept[0, k, window, :]
        second = kept[1, k, own, :]
        total = half_x_ref[own, :] * (pltpu.roll(first, 23, 0)[8:16] - pltpu.roll(first, 1, 0)[8:16])
        total = total + half_y * lane_slope(second)
        total = total + 0.5 * (kept[2, after, own, :] - kept[2, before, own, :])
        target = tile // group
        spot = pl.multiple_of((tile - target * group) * 8, 8)
        source_ref[target, k, pl.ds(spot, 8), :] = -total[:, :span]
        return carry

    lax.fori_loop(0, planes * inner, collect, 0, unroll=8)
    wait_all(done)


def first_step(velocity, weight, code, above, below, side, half_x, half_y, rows):
    planes, count, span = weight.shape
    tall, wide = half_x.shape[0], half_y.shape[1]
    return pl.pallas_call(
        functools.partial(first_kernel, rows),
        in_specs=[anywhere] * 6 + [vector] * 2,
        out_specs=[vector, anywhere],
        out_shape=[
            jax.ShapeDtypeStruct((count // rows, planes, rows, span), jnp.float32),
            jax.ShapeDtypeStruct((3, planes, count, span), jnp.float32),
        ],
        scratch_shapes=[
            pltpu.VMEM((5, planes, tall, wide), jnp.float32),
            pltpu.VMEM((3, planes, tall, wide), jnp.float32),
            pltpu.VMEM((3, planes, tall, wide), jnp.float32),
            pltpu.SemaphoreType.DMA((20,)),
            pltpu.SemaphoreType.DMA((5,)),
        ],
        compiler_params=params(48),
    )(*far(velocity, weight, code, above, below, side), half_x, half_y)


def neighbours(axis, last, leading):
    size = lax.axis_size(axis)
    up = [(i, i + 1) for i in range(size - 1)]
    down = [(i + 1, i) for i in range(size - 1)]
    return lax.ppermute(last, axis, up), lax.ppermute(leading, axis, down)


def extended_1(value, start, count, before, after):
    padded = jnp.pad(value, (before, after))
    return lax.dynamic_slice_in_dim(padded, start, count + before + after)


def lanes_sum(value, columns):
    return jnp.sum(value.reshape(-1, value.shape[-1] // columns, columns), axis=(0, 1))


def add_kernel(numbers_ref, sums_ref, pressure_ref, direction_ref, lifted_ref, out_ref):
    total = jnp.sum(jnp.sum(sums_ref[...], axis=0), axis=1, keepdims=True)
    turn = total[2:3] / numbers_ref[0:1, 0:1]
    length = total[2:3] / (total[3:4] - turn * turn * numbers_ref[1:2, 0:1])
    for k in range(pressure_ref.shape[0]):
        direction = lifted_ref[k] + turn * direction_ref[k]
        out_ref[0, k] = pressure_ref[k] + length * direction


def add_step(numbers, sums, pressure, direction, lifted, pieces):
    planes, rows, full = pressure.shape
    span = full // pieces
    field = pl.BlockSpec((planes, rows, span), lambda n: (0, 0, n))
    return pl.pallas_call(
        add_kernel,
        grid=(pieces,),
        in_specs=[vector] * 2 + [field] * 3,
        out_specs=pl.BlockSpec((1, planes, rows, span), lambda n: (n, 0, 0, 0)),
        out_shape=pltpu.HBM((pieces, planes, rows, span), jnp.float32),
        compiler_params=params(20),
    )(numbers, sums, *far(pressure, direction, lifted))


def correct_kernel(
    predicted_ref, own_ref, previous_ref, next_ref, above_ref, below_ref, left_ref, right_ref,
    half_x_ref, half_y_ref, corrected_ref, pressure_ref,
):
    n = pl.program_id(0)
    last = pl.num_programs(0) - 1
    _, planes, rows, _ = own_ref.shape
    for k in range(planes):
        value = own_ref[0, k]
        above = jnp.where(n == 0, above_ref[k], previous_ref[0, k, rows - 1 : rows, :])
        below = jnp.where(n == last, below_ref[k], next_ref[0, k, 0:1, :])
        rising = jnp.concatenate([value[1:], below], axis=0) - jnp.concatenate([above, value[:-1]], axis=0)
        ahead = jnp.concatenate([value[:, 1:], right_ref[0, k]], axis=1)
        behind = jnp.concatenate([left_ref[0, k], value[:, :-1]], axis=1)
        across = own_ref[0, (k + 1) % planes] - own_ref[0, (k - 1) % planes]
        pressure_ref[:, k, :] = value
        corrected_ref[0, :, k, :] = predicted_ref[0, k] - half_x_ref[...] * rising
        corrected_ref[1, :, k, :] = predicted_ref[1, k] - half_y_ref[...] * (ahead - behind)
        corrected_ref[2, :, k, :] = predicted_ref[2, k] - 0.5 * across


def correct_step(predicted, pressure, above, below, left, right, half_x, half_y):
    pieces, planes, rows, span = pressure.shape
    count = pieces * rows
    own = lambda shift: pl.BlockSpec(
        (1, planes, rows, span), lambda n: (jnp.clip(n + shift, 0, pieces - 1), 0, 0, 0)
    )
    column = pl.BlockSpec((1, planes, rows, 1), lambda n: (n, 0, 0, 0))
    return pl.pallas_call(
        correct_kernel,
        grid=(pieces,),
        in_specs=[
            pl.BlockSpec((3, planes, rows, span), lambda n: (0, 0, n, 0)),
            own(0),
            own(-1),
            own(1),
            vector,
            vector,
            column,
            column,
            pl.BlockSpec((rows, 1), lambda n: (n, 0)),
            vector,
        ],
        out_specs=[
            pl.BlockSpec((3, rows, planes, span), lambda n: (0, n, 0, 0)),
            pl.BlockSpec((rows, planes, span), lambda n: (n, 0, 0)),
        ],
        out_shape=[
            jax.ShapeDtypeStruct((3, count, planes, span), jnp.float32),
            jax.ShapeDtypeStruct((count, planes, span), jnp.float32),
        ],
        compiler_params=params(28),
    )(predicted, pressure, pressure, pressure, above, below, left, right, half_x, half_y)


def per_device(
    velocity,
    cut_flags,
    redirect,
    share_weight,
    inverse_dx,
    inverse_dy,
    basis_x,
    basis_y,
    basis_z,
    eigen_x,
    eigen_y,
    eigen_z,
):
    x_parts = lax.axis_size("gx")
    y_parts = lax.axis_size("gy")
    devices = x_parts * y_parts
    x_index = lax.axis_index("gx")
    y_index = lax.axis_index("gy")
    own = x_index * y_parts + y_index
    x_count, planes, y_count = velocity.shape[1:]
    full_x = x_count * x_parts
    full_y = y_count * y_parts
    rows = full_x // devices
    columns = planes * full_y // devices
    chunks = 2 if columns % 256 == 0 else 1
    columns = columns // chunks
    column_blocks = devices // planes
    inverse_x = lax.dynamic_slice_in_dim(inverse_dx, x_index * x_count, x_count)
    inverse_y = lax.dynamic_slice_in_dim(inverse_dy, y_index * y_count, y_count)
    flags = cut_flags.astype(jnp.float32)
    code = (cut_flags * (redirect + 1)).astype(jnp.float32)
    weight = share_weight * flags
    reach = 3

    def edge_rows(part):
        cut = cut_flags[part]
        share = share_weight[part] * cut.astype(jnp.float32)
        target = (cut * (redirect[part] + 1)).astype(jnp.float32)
        return jnp.concatenate([velocity[:, part], share[None], target[None]])

    above, below = neighbours("gx", edge_rows(slice(x_count - reach, None)), edge_rows(slice(0, reach)))
    velocity = velocity.transpose(0, 2, 1, 3)
    weight = weight.transpose(1, 0, 2)
    code = code.transpose(1, 0, 2)
    above = above.transpose(0, 2, 1, 3)
    below = below.transpose(0, 2, 1, 3)

    def edge_columns(part):
        middle = jnp.concatenate([velocity[..., part], weight[None, ..., part], code[None, ..., part]])
        return jnp.concatenate([above[..., part], middle, below[..., part]], axis=2).swapaxes(2, 3)

    left, right = neighbours("gy", edge_columns(slice(y_count - reach, None)), edge_columns(slice(0, reach)))
    left, right = [
        jnp.pad(part, ((0, 0), (0, 0), (0, 0), (16 - reach, 16 - reach))) for part in (left, right)
    ]
    side = jnp.concatenate([right, jnp.zeros((5, planes, 128 - 2 * reach, x_count + 32), jnp.float32), left], axis=2)
    side = side.swapaxes(2, 3)
    above = jnp.pad(above, ((0, 0), (0, 0), (8 - reach, 0), (0, 0)))
    below = jnp.pad(below, ((0, 0), (0, 0), (0, 8 - reach), (0, 0)))
    half_x = 0.5 * extended_1(inverse_dx, x_index * x_count, x_count, 16, 16)[:, None]
    half_y = 0.5 * extended_1(inverse_dy, y_index * y_count, y_count, reach, reach)
    half_y = jnp.concatenate([half_y[reach:], jnp.zeros((128 - 2 * reach,), jnp.float32), half_y[:reach]])[None]
    source, predicted = first_step(velocity, weight, code, above, below, side, half_x, half_y, rows)
    diagonal = (cell_shift + cut_shift * flags).reshape(y_parts, rows, planes, y_count).transpose(0, 2, 1, 3)
    diagonal = lax.all_to_all(diagonal, "gy", 0, 0, tiled=True)
    source, diagonal = lax.optimization_barrier((source, diagonal))
    source = lax.all_to_all(source, "gy", 0, 0, tiled=True)
    source, basis_xt = lax.optimization_barrier((source, basis_x.T))
    diagonal = diagonal.transpose(1, 2, 0, 3).reshape(planes, rows, full_y)
    whole_x = jnp.pad(inverse_dx, 1)
    face_x = lax.dynamic_slice_in_dim(whole_x[:-1] * whole_x[1:], own * rows, rows + 1)
    whole_y = jnp.pad(inverse_dy, 1)
    face_y = whole_y[:-1] * whole_y[1:]
    operator = (diagonal, face_x[:-1, None], face_x[1:, None], face_y[None, :-1], face_y[None, 1:])
    along = eigen_x[:, None]
    other = [
        (
            lax.dynamic_slice_in_dim(
                eigen_y, full_y // chunks * chunk + (own % column_blocks) * columns, columns
            )
            + lax.dynamic_slice_in_dim(eigen_z, own // column_blocks, 1)
        )[None]
        for chunk in range(chunks)
    ]

    def apply(stage, field, sent, aux, state):
        sents = [sent] + [
            more_lines(field, basis_z, basis_y, columns, chunks, chunk) for chunk in range(1, chunks)
        ]
        gots = []
        for chunk, sent in enumerate(sents):
            sent = sent.reshape(devices, rows, columns)
            got = lax.all_to_all(sent, both, 0, 0, tiled=True).reshape(full_x, columns)
            given = aux if chunk == 0 else jnp.zeros((spare, columns), jnp.float32)
            got = column_lines(got, given, basis_xt, basis_x, along, other[chunk], rows)
            gots.append(lax.all_to_all(got, both, 0, 0, tiled=True))
        if stage > 0:
            state["scalars"] = numbers_of(gots[0][:, rows // 4], state.get("scalars"))
        part = None
        if chunks > 1:
            part = part_lines(stage, gots[0], basis_z, basis_y, rows, chunks, state)
        return gots[-1], part

    def numbers_of(sums, numbers):
        product = jnp.sum(sums[:, 2])
        bend = jnp.sum(sums[:, 3])
        turn = jnp.zeros_like(product)
        if numbers is not None:
            turn = product / numbers[0, 0]
            bend = bend - turn * turn * numbers[1, 0]
        numbers = jnp.stack([product, bend, product / bend, turn])
        return jnp.broadcast_to(jnp.pad(numbers, (0, 4))[:, None], (8, 128))

    residual, sent = start_lines(source, basis_z, basis_y, columns, chunks)
    state = {}
    got, part = apply(0, residual, sent, jnp.zeros((spare, columns), jnp.float32), state)
    state |= turn_lines(0, False, got, part, operator, basis_z, basis_y, state, chunks)
    for stage in range(1, ITERS):
        partial = [lanes_sum(residual * state["z"], columns), lanes_sum(state["z"] * state["y"], columns)]
        aux = jnp.pad(jnp.stack(partial), ((2, spare - 4), (0, 0)))
        got, part = apply(stage, state["y"], state["sent"], aux, state)
        length, turn = state["scalars"][2, 0], state["scalars"][3, 0]
        if stage == 1:
            direction, image = state["z"], state["y"]
            pressure = length * direction
        else:
            direction = state["z"] + turn * direction
            image = state["y"] + turn * image
            pressure = pressure + length * direction
        residual = residual - length * image
        state["residual"] = residual
        last = stage + 1 == ITERS
        state |= turn_lines(stage, last, got, part, operator, basis_z, basis_y, state, chunks)
    sums = jnp.broadcast_to(state["aux"][None], (devices, spare, columns))
    sums = lax.all_to_all(sums, both, 0, 0, tiled=True)
    pressure = add_step(state["scalars"], sums, pressure, direction, state["z"], y_parts)
    pressure = lax.all_to_all(pressure, "gy", 0, 0, tiled=True)
    above, below = neighbours("gx", pressure[-1, :, -1:], pressure[0, :, :1])
    left, right = neighbours("gy", pressure[..., -1], pressure[..., 0])
    half_x = 0.5 * inverse_x[:, None]
    half_y = 0.5 * inverse_y[None]
    corrected, pressure = correct_step(
        predicted, pressure, above, below, left[..., None], right[..., None], half_x, half_y
    )
    return corrected, pressure


def solution(mesh):
    in_specs = (
        P(None, "gx", None, "gy"),
        P("gx", None, "gy"),
        P("gx", None, "gy"),
        P("gx", None, "gy"),
        P(),
        P(),
        P(),
        P(),
        P(),
        P(),
        P(),
        P(),
    )
    out_specs = (P(None, "gx", None, "gy"), P("gx", None, "gy"))
    return jax.shard_map(
        per_device, mesh=mesh, in_specs=in_specs, out_specs=out_specs, check_vma=False
    )
```
